128 devices in a mesh: side: 2 (over core), grp: 4 (over y), dev: 16 (over x, z).
Axes of the slice: x: 4, y: 4, z: 4, core: 2. Of those that a mesh axis runs over, the one named last changes fastest.
Arguments:
- embeds: bfloat16 [2, 256, 256, 256], P('side', ('grp', 'dev')), may hold values from -16 to 16
- partners: int32 [256, 32], replicated, may hold values from 0 to 255, as said below
- counts: int32 [256], replicated, may hold values from 1 to 32, as said below
Outputs:
- mapped: bfloat16 [64, 2, 2, 256, 256], P(('grp', 'dev'), 'side')
- scale_b: float32 [256, 256], P(('grp', 'dev'))
The draws below stay inside these ranges and needn't reach their ends.
Inputs may be any that keep to these rules, and one draw needn't show every extreme that they name: `partners`: entry t of row a is a B block id; only the first counts[a] entries of a row are candidates. The entries of one row lie on distinct devices of catalog B (distinct entry // 4). All entries of the rows of one device's A blocks that lie on the same device of catalog B name the same block. `counts`: some A block has 32 candidates.
All inputs are finite; a program needn't handle non-finite values.
Results may differ from the reference program's by a relative error of at most 0.015.
Values may be sent and summed in bfloat16 or wider, within the bound.
A program may use at most 128 MiB of HBM per device.

```python
import math
import jax
import jax.numpy as jnp
from jax import lax

DIM = 256
BS = 256
BLK_DEV = 4
ITERS = 3
NCHIP = 64
NBLK = 256
SLOTS = 32
HALF = 2


def draw_embeds(key, part):
    subkeys = jax.random.split(jax.random.fold_in(key, 101), 3)
    normals = jnp.clip(jax.random.normal(subkeys[0], (2, NBLK, BS, DIM), jnp.float32), -6.0, 6.0)
    row_scale = jnp.exp(jax.random.uniform(subkeys[1], (2, NBLK, BS, 1), jnp.float32, math.log(0.6), math.log(1.6)))
    col_scale = jnp.exp(jax.random.uniform(subkeys[2], (2, 1, 1, DIM), jnp.float32, math.log(0.6), math.log(1.6)))
    values = normals * row_scale * col_scale
    return jnp.clip(values, -16.0, 16.0).astype(jnp.bfloat16)


def draw_partners(key, part):
    subkeys = jax.random.split(jax.random.fold_in(key, 202), 2)
    scores = jax.random.randint(subkeys[0], (NBLK, NCHIP), 0, 1 << 20) * NCHIP + jnp.arange(NCHIP, dtype=jnp.int32)[None, :]
    owners = jnp.argsort(scores, axis=1)[:, :SLOTS].astype(jnp.int32)
    block_picks = jax.random.randint(subkeys[1], (NCHIP, NCHIP), 0, BLK_DEV).astype(jnp.int32)
    chip_of = jnp.arange(NBLK, dtype=jnp.int32) // BLK_DEV
    chosen_blocks = jnp.take_along_axis(block_picks[chip_of], owners, axis=1)
    return (owners * BLK_DEV + chosen_blocks).astype(jnp.int32)


def draw_counts(key, part):
    lengths_drawn = jax.random.randint(jax.random.fold_in(key, 303), (NBLK,), 1, SLOTS + 1)
    return lengths_drawn.at[0].set(SLOTS).astype(jnp.int32)


def setup_inputs(seed: int = 0) -> dict:
    arg_keys = jax.random.split(jax.random.key(seed), 4)
    return {
        "embeds": draw_embeds(jax.random.fold_in(arg_keys[3], 71), 0),
        "partners": draw_partners(jax.random.fold_in(arg_keys[3], 71), 0),
        "counts": draw_counts(jax.random.fold_in(arg_keys[3], 71), 0),
    }


ENTROPY_TEMP = 0.05
group_slots = 8

def inverse_norms(values):
    widened = values.astype(jnp.float32)
    return lax.rsqrt(lax.optimization_barrier(jnp.mean(widened * widened, axis=-1)) + 1e-06) / math.sqrt(values.shape[-1])

def kernel_tile(rows_x, rows_norm, columns, column_norm, active_pairs):
    scores = jnp.dot(rows_x, columns.T, preferred_element_type=jnp.float32)
    cosine_similarity = scores * rows_norm[:, None] * column_norm[None, :]
    return jnp.where(active_pairs[None, :], jnp.exp((cosine_similarity - 1.0) / ENTROPY_TEMP), 0.0)

def reference(embeds, partners, counts):
    exact_mode = lax.Precision.HIGHEST
    a_data = embeds[0]
    b_data = embeds[1]
    a_norm = inverse_norms(a_data)
    b_norm = inverse_norms(b_data)

    def group_tiles(a_index, group_at):
        first_slot = (group_at * group_slots).astype(jnp.int32)
        block_ids = lax.dynamic_slice_in_dim(partners[a_index], first_slot, group_slots)
        places = jnp.arange(group_slots, dtype=jnp.int32) + first_slot
        active_pairs = jnp.repeat(places < counts[a_index], BS)
        columns = jnp.take(b_data, block_ids, axis=0).reshape(group_slots * BS, DIM)
        column_norm = jnp.take(b_norm, block_ids, axis=0).reshape(group_slots * BS)
        gibbs_kernel = kernel_tile(a_data[a_index], a_norm[a_index], columns, column_norm, active_pairs)
        return (block_ids, gibbs_kernel, columns)

    def group_total(a_index):
        return ((counts[a_index] + group_slots - 1) // group_slots).astype(jnp.int32)

    def row_sums(scales_b):

        def per_block(a_index, rows):

            def advance(group_at, carried):
                block_ids, gibbs_kernel, columns = group_tiles(a_index, group_at)
                weights = jnp.take(scales_b, block_ids, axis=0).reshape(group_slots * BS)
                return carried + jnp.dot(gibbs_kernel, weights, precision=exact_mode)
            summed_mass = lax.fori_loop(0, group_total(a_index), advance, jnp.zeros((BS,), jnp.float32))
            return rows.at[a_index].set(summed_mass)
        return lax.fori_loop(0, NBLK, per_block, jnp.zeros((NBLK, BS), jnp.float32))

    def column_sums(scales_a):

        def per_block(a_index, totals):

            def advance(group_at, carried):
                block_ids, gibbs_kernel, columns = group_tiles(a_index, group_at)
                part_sum = jnp.dot(scales_a[a_index], gibbs_kernel, precision=exact_mode).reshape(group_slots, BS)
                return carried.at[block_ids].add(part_sum)
            return lax.fori_loop(0, group_total(a_index), advance, totals)
        return lax.fori_loop(0, NBLK, per_block, jnp.zeros((NBLK, BS), jnp.float32))

    def mapping(scales_b):

        def per_block(a_index, carried_all):
            numer_all, rows_all = carried_all

            def advance(group_at, carried):
                block_ids, gibbs_kernel, columns = group_tiles(a_index, group_at)
                weights = jnp.take(scales_b, block_ids, axis=0).reshape(group_slots * BS)
                plan = (gibbs_kernel * weights[None, :]).astype(jnp.bfloat16)
                numer = carried[0] + jnp.dot(plan, columns, preferred_element_type=jnp.float32)
                rows = carried[1] + jnp.dot(gibbs_kernel, weights, precision=exact_mode)
                return (numer, rows)
            start = (jnp.zeros((BS, DIM), jnp.float32), jnp.zeros((BS,), jnp.float32))
            numer, rows = lax.fori_loop(0, group_total(a_index), advance, start)
            return (numer_all.at[a_index].set(numer), rows_all.at[a_index].set(rows))
        start = (jnp.zeros((NBLK, BS, DIM), jnp.float32), jnp.zeros((NBLK, BS), jnp.float32))
        return lax.fori_loop(0, NBLK, per_block, start)
    scales_b = jnp.ones((NBLK, BS), jnp.float32)
    for iteration in range(ITERS):
        scales_a = 1.0 / row_sums(scales_b)
        scales_b = 1.0 / (1.0 + column_sums(scales_a))
    numerators, final_rows = mapping(scales_b)
    mapped = (numerators / final_rows[:, :, None]).astype(jnp.bfloat16)
    return (mapped.reshape(NCHIP, 2, HALF, BS, DIM), scales_b)
```

```python
import functools
import math

import jax
import jax.numpy as jnp
from jax import lax
from jax.experimental import pallas as pl
from jax.experimental.pallas import tpu as pltpu
from jax.sharding import PartitionSpec as P

ITERS = 3
GAIN = 20.0 * math.log2(math.e)
MESH = pl.DeviceIdType.MESH
NT = (((1,), (1,)), ((), ()))
f32 = jnp.float32
bf16 = jnp.bfloat16
PIECES = ((0, 96), (96, 80), (176, 80))


def place():
    d = lax.axis_index("dev")
    return lax.axis_index("side"), (d // 4, lax.axis_index("grp"), d % 4)


def flip_a(p):
    return p + 1 - 2 * (p % 2)


def flip_b(p):
    return 3 - p


def member(at, flip, bits, core):
    x, y, z = [flip(p) if (bits >> k) & 1 else p for k, p in enumerate(at)]
    return (core, y, x * 4 + z)


def dot(a, b):
    return jnp.dot(a, b, preferred_element_type=f32)


def dot_nt(a, b):
    return lax.dot_general(a, b, NT, preferred_element_type=f32)


def split_dot(onehot, values):
    high = values.astype(bf16)
    low = (values - high.astype(f32)).astype(bf16)
    return dot(onehot, high) + dot(onehot, low)


def kernel(
    T,
    idx,
    shift,
    x_ref,
    oa,
    oat,
    ob,
    obt,
    obd,
    mapped_ref,
    scale_ref,
    abuf,
    bbuf,
    tiles,
    row_norm,
    col_norm,
    sums,
    spread,
    dense,
    row_send,
    col_send,
    row_recv,
    col_recv,
    numer,
    ship,
    landed,
    own_sem,
    sib_sem,
    gather_sem,
    relay_sem,
    out_sem,
    row_sem,
    col_sem,
    half_sem,
):
    core, at = place()
    other = 1 - core
    sibling = member(at, flip_a, 0, other)
    flips = (flip_a, flip_b)
    bufs = (abuf, bbuf)

    barrier = pltpu.get_barrier_semaphore()
    greeted = [sibling]
    for m in range(1, 8):
        greeted += [member(at, flip_a, m, core), member(at, flip_b, m, core), member(at, flip_b, m, other)]
    for peer in greeted:
        pl.semaphore_signal(barrier, inc=1, device_id=peer, device_id_type=MESH)
    pl.semaphore_wait(barrier, len(greeted))

    def remote(src, dst, send, recv, peer):
        return pltpu.make_async_remote_copy(
            src_ref=src, dst_ref=dst, send_sem=send, recv_sem=recv, device_id=peer, device_id_type=MESH
        )

    @pl.when(core == 0)
    def _():
        give = remote(x_ref.at[pl.ds(2, 2)], abuf.at[pl.ds(0, 2)], sib_sem.at[0], sib_sem.at[1], sibling)
        give.start()
        mine = pltpu.make_async_copy(x_ref.at[pl.ds(0, 2)], abuf.at[pl.ds(0, 2)], own_sem.at[0])
        mine.start()
        mine.wait()
        give.wait_send()
        here = bbuf.at[pl.ds(0, 4)]
        pltpu.make_async_copy(here, here, sib_sem.at[1]).wait()

    @pl.when(core == 1)
    def _():
        give = remote(x_ref, bbuf.at[pl.ds(0, 4)], sib_sem.at[0], sib_sem.at[1], sibling)
        give.start()
        mine = pltpu.make_async_copy(x_ref, bbuf.at[pl.ds(0, 4)], own_sem.at[0])
        mine.start()
        mine.wait()
        give.wait_send()
        here = abuf.at[pl.ds(0, 2)]
        pltpu.make_async_copy(here, here, sib_sem.at[1]).wait()

    def unit(cat, slot, piece):
        start, size = PIECES[piece]
        if cat == 0:
            return abuf.at[pl.ds(slot * 2, 2), pl.ds(start, size)]
        return bbuf.at[pl.ds(slot * 4 + core * 2, 2), pl.ds(start, size)]

    def send_unit(cat, dim, piece, slot):
        there = slot ^ (1 << dim)
        copy = remote(
            unit(cat, slot, piece),
            unit(cat, there, piece),
            out_sem.at[0],
            gather_sem.at[cat, piece, there],
            member(at, flips[cat], 1 << dim, core),
        )
        copy.start()
        return copy

    sent = []
    relays = []

    def arrived(cat, piece, slot):
        here = unit(cat, slot, piece)
        pltpu.make_async_copy(here, here, gather_sem.at[cat, piece, slot]).wait()
        if cat == 1:
            copy = remote(here, here, out_sem.at[1], relay_sem.at[0], sibling)
            copy.start()
            relays.append(copy)

    for step in range(3):
        for dim in range(3):
            for cat in range(2):
                sent.append(send_unit(cat, dim, (dim - step) % 3, 0))

    def a_norms(slot):
        def body(i, c):
            x = abuf[slot * 2 + i].astype(f32)
            total = jnp.sum(x * x, axis=1, keepdims=True)
            row_norm[slot * 2 + i] = lax.rsqrt(total * (1.0 / 256.0) + 1e-06) * (GAIN / 16.0)
            return c

        lax.fori_loop(0, 2, body, 0)

    ones = jnp.ones((8, 256), bf16)

    def b_norms(slot):
        def body(i, c):
            y = bbuf[slot * 4 + i].astype(f32)
            y2 = y * y
            high = y2.astype(bf16)
            low = (y2 - high.astype(f32)).astype(bf16)
            total = dot_nt(ones, high) + dot_nt(ones, low)
            col_norm[slot * 4 + i] = lax.rsqrt(total * (1.0 / 256.0) + 1e-06) * (1.0 / 16.0)
            return c

        lax.fori_loop(0, 4, body, 0)

    a_norms(0)
    b_norms(0)
    for r in range(3):
        for cat in range(2):
            arrived(cat, r, 1 << r)
            sent.append(send_unit(cat, (r + 1) % 3, r, 1 << r))
    for r in range(3):
        for cat in range(2):
            sent.append(send_unit(cat, (r + 2) % 3, r, 1 << r))
    for r in range(3):
        for cat in range(2):
            near = 1 << ((r + 1) % 3)
            arrived(cat, r, near)
            sent.append(send_unit(cat, (r + 2) % 3, r, near))
    for r in range(3):
        for cat in range(2):
            far = (1 << ((r + 1) % 3)) | (1 << r)
            arrived(cat, r, far)
            sent.append(send_unit(cat, (r + 2) % 3, r, far))
    for r in range(3):
        last = 1 << ((r + 2) % 3)
        for rest in (0, 1 << r, 1 << ((r + 1) % 3), (1 << r) | (1 << ((r + 1) % 3))):
            for cat in range(2):
                arrived(cat, r, last | rest)
    for slot in range(1, 8):
        a_norms(slot)
    from_sibling = bbuf.at[pl.ds(4, 14)]
    pltpu.make_async_copy(from_sibling, from_sibling, relay_sem.at[0]).wait()
    for copy in sent:
        copy.wait_send()
    for copy in relays:
        copy.wait_send()
    for slot in range(1, 8):
        b_norms(slot)

    row_id = lax.broadcasted_iota(jnp.int32, (8, 256), 0)

    def build(i, c):
        total = jnp.zeros((8, 256), f32)
        for u in range(8):
            t = i * 8 + u
            a, b = idx[t], idx[T + t]
            scores = dot_nt(abuf[a], bbuf[b])
            tile = jnp.exp2(scores * row_norm[a] * col_norm[b][0:1] - shift[t]).astype(bf16)
            tiles[t] = tile
            total = jnp.where(row_id == u, dot_nt(ones, tile), total)
        sums[pl.ds(pl.multiple_of(i * 8, 8), 8), :] = total
        return c

    lax.fori_loop(0, T // 8, build, 0)

    def sweep(transposed):
        def body(i, c):
            rows = pl.ds(pl.multiple_of(i * 8, 8), 8)
            left = spread[rows, :].astype(bf16)
            total = jnp.zeros((8, 256), f32)
            for u in range(8):
                tile = tiles[i * 8 + u]
                part = dot_nt(left, tile) if transposed else dot(left, tile)
                total = jnp.where(row_id == u, part, total)
            sums[rows, :] = total
            return c

        lax.fori_loop(0, T // 8, body, 0)

    def row_exchange(phase):
        row_send[phase] = split_dot(oa[...], sums[...]).astype(bf16)
        copies = []
        for m in range(1, 8):
            copy = remote(
                row_send.at[phase], row_recv.at[phase, m], row_sem.at[0, phase], row_sem.at[1, phase],
                member(at, flip_a, m, core),
            )
            copy.start()
            copies.append(copy)
        return copies

    def row_result(phase, copies):
        got = row_recv.at[phase, pl.ds(1, 7)]
        pltpu.make_async_copy(got, got, row_sem.at[1, phase]).wait()
        total = row_send[phase].astype(f32)
        for m in range(1, 8):
            total += row_recv[phase, m].astype(f32)
        for copy in copies:
            copy.wait_send()
        return total

    def col_exchange(phase):
        col_send[phase] = split_dot(ob[...], sums[...]).astype(bf16)
        copies = []
        for far in range(2):
            for m in range(8):
                if far + m:
                    copy = remote(
                        col_send.at[phase], col_recv.at[phase, far * 8 + m], col_sem.at[0, phase],
                        col_sem.at[1, phase], member(at, flip_b, m, other if far else core),
                    )
                    copy.start()
                    copies.append(copy)
        got = col_recv.at[phase, pl.ds(1, 15)]
        pltpu.make_async_copy(got, got, col_sem.at[1, phase]).wait()
        total = col_send[phase].astype(f32)
        for m in range(1, 16):
            total += col_recv[phase, m].astype(f32)
        for copy in copies:
            copy.wait_send()
        return total

    for phase in range(ITERS):
        if phase:
            sweep(True)
        scale_a = 1.0 / row_result(phase, row_exchange(phase))
        spread[...] = dot(oat[...], scale_a.astype(bf16))
        sweep(False)
        scale_b = 1.0 / (1.0 + col_exchange(phase))
        spread[...] = dot(obt[...], scale_b.astype(bf16))
    x, y, z = at
    own_b = x // 2 + 2 * (y // 2) + 4 * (z // 2)
    sums[pl.ds(0, 32), :] = scale_b
    near_rows = sums[pl.ds(pl.multiple_of((own_b // 2) * 8, 8), 8), :]
    scale_ref[...] = jnp.where(own_b % 2 == 0, near_rows[0:4], near_rows[4:8])
    dense[...] = dot(obd[...], scale_b.astype(bf16))

    def partial(slot):
        def body(i, c):
            total = None
            base = (slot * 2 + i) * 8
            rows = dense[pl.ds(pl.multiple_of(base, 8), 8), :]
            for d in range(8):
                scaled = (tiles[idx[2 * T + base + d]] * rows[d : d + 1]).astype(bf16)
                part = dot(scaled, bbuf[idx[2 * T + 128 + base + d]])
                total = part if total is None else total + part
            numer[slot * 2 + i] = total
            return c

        lax.fori_loop(0, 2, body, 0)

    halves = []

    def send_half(piece, slot, dim, order):
        start, size = PIECES[piece]
        two, rows = pl.ds(slot * 2, 2), pl.ds(start, size)
        ship[two, rows, :] = numer[two, rows, :].astype(bf16)
        there = slot ^ (1 << dim)
        copy = remote(
            ship.at[two, rows], landed.at[order, pl.ds(there * 2, 2), rows], out_sem.at[2], half_sem.at[order, piece, there],
            member(at, flip_a, 1 << dim, core),
        )
        copy.start()
        halves.append(copy)

    def add_half(piece, slot, order):
        start, size = PIECES[piece]
        two, rows = pl.ds(slot * 2, 2), pl.ds(start, size)
        here = landed.at[order, two, rows]
        pltpu.make_async_copy(here, here, half_sem.at[order, piece, slot]).wait()
        numer[two, rows, :] = numer[two, rows, :] + landed[order, two, rows, :].astype(f32)

    for slot in (7, 3, 5, 6, 1, 2, 4, 0):
        partial(slot)
        for r in range(3):
            if (slot >> r) & 1:
                send_half(r, slot, r, 0)
    for r in range(3):
        k1, k2 = 1 << ((r + 1) % 3), 1 << ((r + 2) % 3)
        add_half(r, k1 | k2, 0)
        send_half(r, k1 | k2, (r + 1) % 3, 1)
    sweep(True)
    row_copies = row_exchange(ITERS)
    for r in range(3):
        k1, k2 = 1 << ((r + 1) % 3), 1 << ((r + 2) % 3)
        add_half(r, k1, 0)
        send_half(r, k1, (r + 1) % 3, 1)
    for r in range(3):
        k1, k2 = 1 << ((r + 1) % 3), 1 << ((r + 2) % 3)
        add_half(r, k2, 0)
        add_half(r, k2, 1)
        send_half(r, k2, (r + 2) % 3, 2)
    sums[pl.ds(0, 16), :] = row_result(ITERS, row_copies)
    own_a = x % 2 + 2 * (y % 2) + 4 * (z % 2)
    near_rows = sums[pl.ds(pl.multiple_of((own_a // 4) * 8, 8), 8), :]
    mine = near_rows[0:2]
    for k in range(1, 4):
        mine = jnp.where(own_a % 4 == k, near_rows[2 * k : 2 * k + 2], mine)
    column = jnp.transpose(jnp.broadcast_to(1.0 / mine[:, None, :], (2, 128, 256)).reshape(256, 256))
    for r in range(3):
        for order in range(3):
            add_half(r, 0, order)
    for i in range(2):
        inverse = column[:, i * 128 : i * 128 + 1]
        mapped_ref[i] = (numer[i] * inverse).astype(bf16)
    for copy in halves:
        copy.wait_send()


def listing(T, partners, counts):
    core, (x, y, z) = place()
    m = jnp.arange(8, dtype=jnp.int32)
    chip = (y ^ ((m >> 1) & 1)) * 16 + (x ^ (m & 1)) * 4 + (z ^ (m >> 2))
    rows = (chip[:, None] * 4 + 2 * core + jnp.arange(2, dtype=jnp.int32)[None, :]).reshape(16)
    named = jnp.take(partners, rows, axis=0)
    limit = jnp.take(counts, rows, axis=0)
    owner = named // 4
    ox, oy, oz = (owner // 4) % 4, owner // 16, owner % 4

    def near(p, q):
        return (p == q) | (p == 3 - q)

    active = near(ox, x) & near(oy, y) & near(oz, z)
    active &= jnp.arange(32, dtype=jnp.int32)[None, :] < limit[:, None]
    jb = ox // 2 + 2 * (oy // 2) + 4 * (oz // 2)
    pick = jnp.max(
        jnp.where(active[:, :, None] & (jb[:, :, None] == m), (named % 4 + 1)[:, :, None], 0), axis=1
    ).reshape(128)
    e = jnp.arange(128, dtype=jnp.int32)
    used = pick > 0
    before = jnp.sum((used[:, None] & (e[:, None] < e[None, :])).astype(jnp.int32), axis=0)
    total = jnp.sum(used.astype(jnp.int32))
    t = jnp.arange(T, dtype=jnp.int32)
    hot = (before[None, :] == t[:, None]) & used[None, :]
    own_a = (x % 2) + 2 * (y % 2) + 4 * (z % 2)
    own_b = (x // 2) + 2 * (y // 2) + 4 * (z // 2)
    a_rel = e // 8
    a_abs = ((e // 16) ^ own_a) * 2 + a_rel % 2
    b_abs = (e % 8) * 4 + jnp.maximum(pick - 1, 0)
    b_rel = ((e % 8) ^ own_b) * 4 + jnp.maximum(pick - 1, 0)

    def chosen(values):
        return jnp.sum(jnp.where(hot, values[None, :], 0), axis=1)

    where = jnp.where(used, before, 0)
    idx = jnp.concatenate([chosen(a_rel), chosen(b_rel), where, b_rel]).astype(jnp.int32)
    shift = jnp.where(t < total, GAIN, 1e30).astype(f32)
    a_t, b_t = chosen(a_abs), chosen(b_abs)
    oa = (a_t[None, :] == jnp.arange(16)[:, None]).astype(bf16)
    ob = (b_t[None, :] == jnp.arange(32)[:, None]).astype(bf16)
    oat = (a_t[:, None] == jnp.arange(16)[None, :]).astype(bf16)
    obt = (b_t[:, None] == jnp.arange(32)[None, :]).astype(bf16)
    obd = ((b_abs[:, None] == jnp.arange(32)[None, :]) & used[:, None]).astype(bf16)
    return idx, shift, oa, oat, ob, obt, obd


def transport(T, cid, own, partners, counts):
    idx, shift, oa, oat, ob, obt, obd = listing(T, partners, counts)
    smem = pl.BlockSpec(memory_space=pltpu.SMEM)
    vmem = pl.BlockSpec(memory_space=pltpu.VMEM)
    dma = pltpu.SemaphoreType.DMA
    return pl.pallas_call(
        functools.partial(kernel, T),
        out_shape=(jax.ShapeDtypeStruct((2, 256, 256), bf16), jax.ShapeDtypeStruct((4, 256), f32)),
        in_specs=[
            smem, smem, pl.BlockSpec(memory_space=pl.ANY), vmem, vmem, vmem, vmem, vmem,
        ],
        out_specs=(vmem, vmem),
        scratch_shapes=[
            pltpu.VMEM((16, 256, 256), bf16),
            pltpu.VMEM((32, 256, 256), bf16),
            pltpu.VMEM((T, 256, 256), bf16),
            pltpu.VMEM((16, 256, 1), f32),
            pltpu.VMEM((32, 8, 256), f32),
            pltpu.VMEM((T, 256), f32),
            pltpu.VMEM((T, 256), f32),
            pltpu.VMEM((128, 256), f32),
            pltpu.VMEM((4, 16, 256), bf16),
            pltpu.VMEM((3, 32, 256), bf16),
            pltpu.VMEM((4, 8, 16, 256), bf16),
            pltpu.VMEM((3, 16, 32, 256), bf16),
            pltpu.VMEM((16, 256, 256), f32),
            pltpu.VMEM((16, 256, 256), bf16),
            pltpu.VMEM((3, 16, 256, 256), bf16),
            dma((1,)),
            dma((2,)),
            dma((2, 3, 8)),
            dma((1,)),
            dma((3,)),
            dma((2, 4)),
            dma((2, 3)),
            dma((3, 3, 8)),
        ],
        compiler_params=pltpu.CompilerParams(
            collective_id=cid, has_side_effects=True, vmem_limit_bytes=60 << 20
        ),
        name=f"transport_{T}",
    )(idx, shift, own, oa, oat, ob, obt, obd)


def most_tiles(partners, counts):
    named = jnp.arange(32, dtype=jnp.int32)[None, :] < counts[:, None]
    owner = partners // 4
    parts = [(owner // 4) % 4, owner // 16, owner % 4]
    kind = sum(((p == 1) | (p == 2)).astype(jnp.int32) * (1 << k) for k, p in enumerate(parts))
    each = jnp.stack([jnp.sum((named & (kind == k)).astype(jnp.int32), axis=1) for k in range(8)])
    return jnp.max(jnp.sum(each.reshape(8, 2, 2, 2, 2, 2, 2, 2, 2), axis=(2, 4, 6, 8)))


def shards(embeds, partners, counts):
    own = embeds.reshape(4, 256, 256)
    mapped, scale = lax.cond(
        most_tiles(partners, counts) <= 64,
        functools.partial(transport, 64, 0),
        functools.partial(transport, 128, 1),
        own,
        partners,
        counts,
    )
    return mapped.reshape(1, 1, 2, 256, 256), scale


def solution(mesh):
    in_specs = (P("side", ("grp", "dev"), None, None), P(), P())
    out_specs = (P(("grp", "dev"), "side", None, None, None), P(("grp", "dev"), None))
    return jax.shard_map(shards, mesh=mesh, in_specs=in_specs, out_specs=out_specs, check_vma=False)
```

```python
import functools
import math

import jax
import jax.numpy as jnp
from jax import lax
from jax.experimental import pallas as pl
from jax.experimental.pallas import tpu as pltpu
from jax.sharding import PartitionSpec as P

ITERS = 3
GAIN = 20.0 * math.log2(math.e)
MESH = pl.DeviceIdType.MESH
NT = (((1,), (1,)), ((), ()))
f32 = jnp.float32
bf16 = jnp.bfloat16
PIECES = ((0, 96), (96, 80), (176, 80))


def place():
    d = lax.axis_index("dev")
    return lax.axis_index("side"), (d // 4, lax.axis_index("grp"), d % 4)


def flip_a(p):
    return p + 1 - 2 * (p % 2)


def flip_b(p):
    return 3 - p


def member(at, flip, bits, core):
    x, y, z = [flip(p) if (bits >> k) & 1 else p for k, p in enumerate(at)]
    return (core, y, x * 4 + z)


def dot(a, b):
    return jnp.dot(a, b, preferred_element_type=f32)


def dot_nt(a, b):
    return lax.dot_general(a, b, NT, preferred_element_type=f32)


def split_dot(onehot, values):
    high = values.astype(bf16)
    low = (values - high.astype(f32)).astype(bf16)
    return dot(onehot, high) + dot(onehot, low)


def kernel(
    T,
    x_ref,
    partners_ref,
    counts_ref,
    mapped_ref,
    scale_ref,
    most_ref,
    oa,
    oat,
    ob,
    obt,
    obd,
    index,
    idx,
    final,
    abuf,
    bbuf,
    tiles,
    row_norm,
    col_norm,
    sums,
    spread,
    dense,
    row_send,
    col_send,
    row_recv,
    col_recv,
    numer,
    ship,
    landed,
    own_sem,
    sib_sem,
    gather_sem,
    relay_sem,
    out_sem,
    row_sem,
    col_sem,
    half_sem,
    index_sem,
):
    core, at = place()
    other = 1 - core
    sibling = member(at, flip_a, 0, other)
    flips = (flip_a, flip_b)
    bufs = (abuf, bbuf)

    barrier = pltpu.get_barrier_semaphore()
    greeted = [sibling]
    for m in range(1, 8):
        greeted += [member(at, flip_a, m, core), member(at, flip_b, m, core), member(at, flip_b, m, other)]
    for peer in greeted:
        pl.semaphore_signal(barrier, inc=1, device_id=peer, device_id_type=MESH)
    pl.semaphore_wait(barrier, len(greeted))

    def remote(src, dst, send, recv, peer):
        return pltpu.make_async_remote_copy(
            src_ref=src, dst_ref=dst, send_sem=send, recv_sem=recv, device_id=peer, device_id_type=MESH
        )

    def unit(cat, slot, piece):
        start, size = PIECES[piece]
        if cat == 0:
            return abuf.at[pl.ds(slot * 2, 2), pl.ds(start, size)]
        return bbuf.at[slot, pl.ds(core * 2, 2), pl.ds(start, size)]

    def unit_copy(cat, dim, piece, slot, src=None):
        there = slot ^ (1 << dim)
        return remote(
            unit(cat, slot, piece) if src is None else src,
            unit(cat, there, piece),
            out_sem.at[0],
            gather_sem.at[cat, piece, there],
            member(at, flips[cat], 1 << dim, core),
        )

    def send_unit(cat, dim, piece, slot):
        copy = unit_copy(cat, dim, piece, slot)
        copy.start()
        return copy

    def send_own(cat, src):
        for step in range(3):
            for dim in range(3):
                piece = (dim - step) % 3
                start, size = PIECES[piece]
                unit_copy(cat, dim, piece, 0, None if src is None else src.at[:, pl.ds(start, size)]).start()

    own_a_half, own_b = abuf.at[pl.ds(0, 2)], bbuf.at[0]

    @pl.when(core == 0)
    def _():
        give = remote(x_ref.at[pl.ds(2, 2)], own_a_half, sib_sem.at[0], sib_sem.at[1], sibling)
        give.start()
        send_own(0, x_ref.at[pl.ds(0, 2)])
        mine = pltpu.make_async_copy(x_ref.at[pl.ds(0, 2)], own_a_half, own_sem.at[0])
        mine.start()
        mine.wait()
        give.wait_send()
        pltpu.make_async_copy(own_b, own_b, sib_sem.at[1]).wait()
        send_own(1, None)

    @pl.when(core == 1)
    def _():
        give = remote(x_ref, own_b, sib_sem.at[0], sib_sem.at[1], sibling)
        give.start()
        send_own(1, x_ref.at[pl.ds(2, 2)])
        mine = pltpu.make_async_copy(x_ref, own_b, own_sem.at[0])
        mine.start()
        mine.wait()
        give.wait_send()
        pltpu.make_async_copy(own_a_half, own_a_half, sib_sem.at[1]).wait()
        send_own(0, None)

    sent = []
    relays = []

    def arrived(cat, piece, slot):
        here = unit(cat, slot, piece)
        pltpu.make_async_copy(here, here, gather_sem.at[cat, piece, slot]).wait()
        if cat == 1:
            copy = remote(here, here, out_sem.at[1], relay_sem.at[slot], sibling)
            copy.start()
            relays.append(copy)

    def iota(shape, dim):
        return lax.broadcasted_iota(jnp.int32, shape, dim)

    diagonal = iota((128, 128), 0) == iota((128, 128), 1)

    def norms(slot):
        if slot:
            here = bbuf.at[slot, pl.ds(other * 2, 2)]
            pltpu.make_async_copy(here, here, relay_sem.at[slot]).wait()

        def a_body(i, c):
            x = abuf[slot * 2 + i].astype(f32)
            total = jnp.sum(x * x, axis=1, keepdims=True)
            row_norm[slot * 2 + i] = lax.rsqrt(total * (1.0 / 256.0) + 1e-06) * (GAIN / 16.0)
            return c

        def b_body(i, c):
            for h in range(2):
                y = bbuf[slot, i, pl.ds(h * 128, 128), :]
                total = jnp.sum(jnp.where(diagonal, dot_nt(y, y), 0.0), axis=0, keepdims=True)
                norm = lax.rsqrt(total * (1.0 / 256.0) + 1e-06) * (1.0 / 16.0)
                col_norm[slot * 4 + i, :, pl.ds(h * 128, 128)] = jnp.broadcast_to(norm, (8, 128))
            return c

        lax.fori_loop(0, 2, a_body, 0)
        lax.fori_loop(0, 4, b_body, 0)

    def bits_of(values, shifts):
        return [(values >> k) & 1 for k in shifts]

    def flipped(bits, by):
        return sum((b + f - 2 * b * f) * (1 << k) for k, (b, f) in enumerate(zip(bits, by)))

    def make_list():
        x, y, z = at
        own_low = [p % 2 for p in at]
        own_high = [p // 2 for p in at]
        named_all = partners_ref[...]
        limit_row = counts_ref[...]
        r = iota((16, 256), 0)
        cx, cy, cz = [flipped([b], [p % 2]) + 2 * (p // 2) for b, p in zip(bits_of(r, (1, 2, 3)), at)]
        chosen = iota((16, 256), 1) == (cy * 16 + cx * 4 + cz) * 4 + 2 * core + (r & 1)
        named = dot(chosen.astype(f32).astype(bf16), named_all.astype(f32).astype(bf16)).astype(jnp.int32)
        limit = jnp.sum(jnp.where(chosen, jnp.broadcast_to(limit_row, (16, 256)), 0).astype(f32), axis=1, keepdims=True)
        slot_at = iota((16, 32), 1).astype(f32)

        def coords(entry):
            owner = entry >> 2
            return (owner >> 2) & 3, owner >> 4, owner & 3

        parts = coords(named)
        active = slot_at < limit
        for p, q in zip(parts, at):
            active &= (p == q) | (p == 3 - q)
        jb = sum((p >> 1) * (1 << k) for k, p in enumerate(parts))
        pick = (named & 3) + 1
        lane = iota((16, 128), 1)
        bp = jnp.zeros((16, 128), f32)
        for k in range(8):
            best = jnp.max(jnp.where(active & (jb == k), pick, 0).astype(f32), axis=1, keepdims=True)
            bp = jnp.where(lane == k, best, bp)
        used = jnp.where(bp > 0, 1.0, 0.0).astype(bf16)
        i128, j128 = iota((128, 128), 0), iota((128, 128), 1)

        def mask(m):
            return jnp.where(m, 1.0, 0.0).astype(bf16)

        in_row = dot(used, mask(i128 < j128))
        of_row = dot(used, mask(i128 < 128))
        above = dot(mask(iota((16, 16), 1) < iota((16, 16), 0)), of_row.astype(bf16))
        pos = above + in_row
        k3 = bits_of(lane, (0, 1, 2))
        b_rel = flipped(k3, own_high) * 4 + jnp.maximum(bp.astype(jnp.int32) - 1, 0)
        index[pl.ds(0, 16), :] = jnp.where(bp > 0, jnp.minimum(pos, T - 1.0), 0.0).astype(jnp.int32)
        index[pl.ds(16, 16), :] = jnp.where(lane < 8, b_rel, 0)

        spread_out = mask(i128 == (j128 & 7))
        own_lane = (lane >> 3) == iota((16, 128), 0)

        def flat(values):
            return jnp.sum(jnp.where(own_lane, dot(values.astype(bf16), spread_out), 0.0), axis=0, keepdims=True)

        bp_row, pos_row = flat(bp), flat(pos)
        hot = mask((iota((T, 128), 0).astype(f32) == pos_row) & (bp_row > 0))
        e = iota((8, 128), 1)
        pick_row = jnp.maximum(jnp.broadcast_to(bp_row, (8, 128)).astype(jnp.int32) - 1, 0)
        b_e = flipped(bits_of(e, (0, 1, 2)), own_high) * 4 + pick_row
        values = jnp.where(iota((8, 128), 0) == 0, e >> 3, b_e).astype(f32).astype(bf16)
        index[pl.ds(32, 8), pl.ds(0, T)] = dot_nt(values, hot).astype(jnp.int32)
        fetch = pltpu.make_async_copy(index, idx, index_sem.at[0])
        fetch.start()
        e16, e32 = iota((16, 128), 1), iota((32, 128), 1)
        a_abs = flipped(bits_of(e16, (4, 5, 6)), own_low) * 2 + ((e16 >> 3) & 1)
        a_hot = mask(iota((16, 128), 0) == a_abs)
        b_abs = (e32 & 7) * 4 + jnp.broadcast_to(bp_row, (32, 128)).astype(jnp.int32) - 1
        b_hot = mask((iota((32, 128), 0) == b_abs) & (bp_row > 0))
        oa[...] = dot_nt(a_hot, hot).astype(bf16)
        oat[...] = dot_nt(hot, a_hot).astype(bf16)
        ob[...] = dot_nt(b_hot, hot).astype(bf16)
        obt[...] = dot_nt(hot, b_hot).astype(bf16)
        obd[...] = dot_nt(mask(i128 == j128), b_hot).astype(bf16)

        limit_all = jnp.transpose(jnp.broadcast_to(limit_row.astype(f32), (128, 256)))[:, 0:32]
        active = iota((256, 32), 1).astype(f32) < limit_all
        kind = sum((((p + 1) >> 1) & 1) * (1 << k) for k, p in enumerate(coords(named_all)))
        g, row = iota((16, 256), 0), iota((16, 256), 1)
        group = ((row >> 7) & 1) * 8 + ((row >> 5) & 1) * 4 + ((row >> 3) & 1) * 2 + ((row >> 1) & 1)
        members = mask(g == group)
        most = jnp.zeros((16, 1), f32)
        for k in range(8):
            most = jnp.maximum(
                most, jnp.sum(dot(members, mask(active & (kind == k))), axis=1, keepdims=True)
            )
        most_ref[...] = jnp.broadcast_to(jnp.max(most, axis=0, keepdims=True), (8, 128))
        fetch.wait()

    def received(steps):
        for r in range(3):
            slot = steps(1 << r, 1 << ((r + 1) % 3), 1 << ((r + 2) % 3))
            for cat in range(2):
                arrived(cat, r, slot)
                yield cat, r, slot

    for cat, r, slot in received(lambda k0, k1, k2: k0):
        sent.append(send_unit(cat, (r + 1) % 3, r, slot))
    for r in range(3):
        for cat in range(2):
            sent.append(send_unit(cat, (r + 2) % 3, r, 1 << r))
    norms(0)
    for cat, r, slot in received(lambda k0, k1, k2: k1):
        sent.append(send_unit(cat, (r + 2) % 3, r, slot))
    make_list()
    for _ in received(lambda k0, k1, k2: k2):
        pass
    for cat, r, slot in received(lambda k0, k1, k2: k0 | k1):
        sent.append(send_unit(cat, (r + 2) % 3, r, slot))
    for slot in (1, 2, 4):
        norms(slot)
    for _ in received(lambda k0, k1, k2: k2 | k0):
        pass
    for _ in received(lambda k0, k1, k2: k2 | k1):
        pass
    for slot in (3, 5, 6):
        norms(slot)
    for _ in received(lambda k0, k1, k2: 7):
        pass
    norms(7)
    for cat in range(2):
        for step in range(3):
            for dim in range(3):
                sent.append(unit_copy(cat, dim, (dim - step) % 3, 0))
    for copy in sent:
        copy.wait_send()
    for copy in relays:
        copy.wait_send()
    ones = jnp.ones((8, 256), bf16)

    row_id = lax.broadcasted_iota(jnp.int32, (8, 256), 0)

    def build(i, c):
        total = jnp.zeros((8, 256), f32)
        for u in range(8):
            t = i * 8 + u
            a, b = jnp.clip(idx[32, t], 0, 15), jnp.clip(idx[33, t], 0, 31)
            scores = dot_nt(abuf[a], bbuf[b // 4, b % 4])
            tile = jnp.exp2(scores * row_norm[a] * col_norm[b][0:1] - GAIN).astype(bf16)
            tiles[t] = tile
            total = jnp.where(row_id == u, dot_nt(ones, tile), total)
        sums[pl.ds(pl.multiple_of(i * 8, 8), 8), :] = total
        return c

    lax.fori_loop(0, T // 8, build, 0)

    def sweep(transposed):
        def body(i, c):
            rows = pl.ds(pl.multiple_of(i * 8, 8), 8)
            left = spread[rows, :].astype(bf16)
            total = jnp.zeros((8, 256), f32)
            for u in range(8):
                tile = tiles[i * 8 + u]
                part = dot_nt(left, tile) if transposed else dot(left, tile)
                total = jnp.where(row_id == u, part, total)
            sums[rows, :] = total
            return c

        lax.fori_loop(0, T // 8, body, 0)

    def row_exchange(phase, partial):
        row_send[phase] = partial.astype(bf16)
        copies = []
        for m in range(1, 8):
            copy = remote(
                row_send.at[phase], row_recv.at[phase, m], row_sem.at[0, phase], row_sem.at[1, phase],
                member(at, flip_a, m, core),
            )
            copy.start()
            copies.append(copy)
        return copies

    def row_result(phase, copies):
        got = row_recv.at[phase, pl.ds(1, 7)]
        pltpu.make_async_copy(got, got, row_sem.at[1, phase]).wait()
        total = row_send[phase].astype(f32)
        for m in range(1, 8):
            total += row_recv[phase, m].astype(f32)
        for copy in copies:
            copy.wait_send()
        return total

    def col_exchange(phase):
        col_send[phase] = split_dot(ob[...], sums[...]).astype(bf16)
        copies = []
        for far in range(2):
            for m in range(8):
                if far + m:
                    copy = remote(
                        col_send.at[phase], col_recv.at[phase, far * 8 + m], col_sem.at[0, phase],
                        col_sem.at[1, phase], member(at, flip_b, m, other if far else core),
                    )
                    copy.start()
                    copies.append(copy)
        got = col_recv.at[phase, pl.ds(1, 15)]
        pltpu.make_async_copy(got, got, col_sem.at[1, phase]).wait()
        total = col_send[phase].astype(f32)
        for m in range(1, 16):
            total += col_recv[phase, m].astype(f32)
        for copy in copies:
            copy.wait_send()
        return total

    for phase in range(ITERS):
        if phase:
            sweep(True)
        scale_a = 1.0 / row_result(phase, row_exchange(phase, split_dot(oa[...], sums[...])))
        spread[...] = dot(oat[...], scale_a.astype(bf16))
        sweep(False)
        scale_b = 1.0 / (1.0 + col_exchange(phase))
        spread[...] = dot(obt[...], scale_b.astype(bf16))
    x, y, z = at
    member_b = x // 2 + 2 * (y // 2) + 4 * (z // 2)
    sums[pl.ds(0, 32), :] = scale_b
    near_rows = sums[pl.ds(pl.multiple_of((member_b // 2) * 8, 8), 8), :]
    scale_ref[...] = jnp.where(member_b % 2 == 0, near_rows[0:4], near_rows[4:8])
    dense[...] = dot(obd[...], scale_b.astype(bf16))

    def partial(slot):
        def body(i, c):
            total, mass = None, None
            a = slot * 2 + i
            rows = dense[pl.ds(pl.multiple_of(a * 8, 8), 8), :]
            for d in range(8):
                weights = tiles[jnp.clip(idx[a, d], 0, T - 1)].astype(f32) * rows[d : d + 1]
                b = jnp.clip(idx[16 + a, d], 0, 31)
                part = dot(weights.astype(bf16), bbuf[b // 4, b % 4])
                half = weights[:, 0:128] + weights[:, 128:256]
                total = part if total is None else total + part
                mass = half if mass is None else mass + half
            numer[a] = total
            column = jnp.sum(mass, axis=1, keepdims=True)
            a_at = flipped([(slot >> k) & 1 for k in range(3)], [p % 2 for p in at]) * 2 + i
            final[...] = jnp.where(iota((256, 128), 1) == a_at, column, final[...])
            return c

        lax.fori_loop(0, 2, body, 0)

    halves = []
    final[...] = jnp.zeros((256, 128), f32)

    def send_half(piece, slot, dim, order):
        start, size = PIECES[piece]
        two, rows = pl.ds(slot * 2, 2), pl.ds(start, size)
        ship[two, rows, :] = numer[two, rows, :].astype(bf16)
        there = slot ^ (1 << dim)
        copy = remote(
            ship.at[two, rows], landed.at[order, pl.ds(there * 2, 2), rows], out_sem.at[2], half_sem.at[order, piece, there],
            member(at, flip_a, 1 << dim, core),
        )
        copy.start()
        halves.append(copy)

    def add_half(piece, slot, order):
        start, size = PIECES[piece]
        two, rows = pl.ds(slot * 2, 2), pl.ds(start, size)
        here = landed.at[order, two, rows]
        pltpu.make_async_copy(here, here, half_sem.at[order, piece, slot]).wait()
        numer[two, rows, :] = numer[two, rows, :] + landed[order, two, rows, :].astype(f32)

    for slot in (7, 3, 5, 6, 1, 2, 4, 0):
        partial(slot)
        for r in range(3):
            if (slot >> r) & 1:
                send_half(r, slot, r, 0)
    for r in range(3):
        k1, k2 = 1 << ((r + 1) % 3), 1 << ((r + 2) % 3)
        add_half(r, k1 | k2, 0)
        send_half(r, k1 | k2, (r + 1) % 3, 1)
    row_copies = row_exchange(ITERS, jnp.transpose(final[...])[0:16])
    for r in range(3):
        k1, k2 = 1 << ((r + 1) % 3), 1 << ((r + 2) % 3)
        add_half(r, k1, 0)
        send_half(r, k1, (r + 1) % 3, 1)
    for r in range(3):
        k1, k2 = 1 << ((r + 1) % 3), 1 << ((r + 2) % 3)
        add_half(r, k2, 0)
        add_half(r, k2, 1)
        send_half(r, k2, (r + 2) % 3, 2)
    sums[pl.ds(0, 16), :] = row_result(ITERS, row_copies)
    own_a = x % 2 + 2 * (y % 2) + 4 * (z % 2)
    near_rows = sums[pl.ds(pl.multiple_of((own_a // 4) * 8, 8), 8), :]
    mine = near_rows[0:2]
    for k in range(1, 4):
        mine = jnp.where(own_a % 4 == k, near_rows[2 * k : 2 * k + 2], mine)
    column = jnp.transpose(jnp.broadcast_to(1.0 / mine[:, None, :], (2, 128, 256)).reshape(256, 256))
    for r in range(3):
        for order in range(3):
            add_half(r, 0, order)
    for i in range(2):
        inverse = column[:, i * 128 : i * 128 + 1]
        mapped_ref[i] = (numer[i] * inverse).astype(bf16)
    for copy in halves:
        copy.wait_send()


def transport(T, cid, own, partners, counts):
    vmem = pl.BlockSpec(memory_space=pltpu.VMEM)
    dma = pltpu.SemaphoreType.DMA
    return pl.pallas_call(
        functools.partial(kernel, T),
        out_shape=(
            jax.ShapeDtypeStruct((2, 256, 256), bf16),
            jax.ShapeDtypeStruct((4, 256), f32),
            jax.ShapeDtypeStruct((8, 128), f32),
        ),
        in_specs=[pl.BlockSpec(memory_space=pl.ANY), vmem, vmem],
        out_specs=(vmem, vmem, vmem),
        scratch_shapes=[
            pltpu.VMEM((16, T), bf16),
            pltpu.VMEM((T, 16), bf16),
            pltpu.VMEM((32, T), bf16),
            pltpu.VMEM((T, 32), bf16),
            pltpu.VMEM((128, 32), bf16),
            pltpu.VMEM((40, 128), jnp.int32),
            pltpu.SMEM((40, 128), jnp.int32),
            pltpu.VMEM((256, 128), f32),
            pltpu.VMEM((16, 256, 256), bf16),
            pltpu.VMEM((8, 4, 256, 256), bf16),
            pltpu.VMEM((T, 256, 256), bf16),
            pltpu.VMEM((16, 256, 1), f32),
            pltpu.VMEM((32, 8, 256), f32),
            pltpu.VMEM((T, 256), f32),
            pltpu.VMEM((T, 256), f32),
            pltpu.VMEM((128, 256), f32),
            pltpu.VMEM((4, 16, 256), bf16),
            pltpu.VMEM((3, 32, 256), bf16),
            pltpu.VMEM((4, 8, 16, 256), bf16),
            pltpu.VMEM((3, 16, 32, 256), bf16),
            pltpu.VMEM((16, 256, 256), f32),
            pltpu.VMEM((16, 256, 256), bf16),
            pltpu.VMEM((3, 16, 256, 256), bf16),
            dma((1,)),
            dma((2,)),
            dma((2, 3, 8)),
            dma((8,)),
            dma((3,)),
            dma((2, 4)),
            dma((2, 3)),
            dma((3, 3, 8)),
            dma((1,)),
        ],
        compiler_params=pltpu.CompilerParams(
            collective_id=cid, has_side_effects=True, vmem_limit_bytes=60 << 20
        ),
        name=f"transport_{T}",
    )(own, partners, counts)


def shards(embeds, partners, counts):
    args = embeds.reshape(4, 256, 256), partners, counts.reshape(1, 256)
    mapped, scale, most = transport(64, 0, *args)
    mapped, scale = lax.cond(
        most[0, 0] <= 64.0,
        lambda mapped, scale, *args: (mapped, scale),
        lambda mapped, scale, *args: transport(128, 1, *args)[:2],
        mapped,
        scale,
        *args,
    )
    return mapped.reshape(1, 1, 2, 256, 256), scale


def solution(mesh):
    in_specs = (P("side", ("grp", "dev"), None, None), P(), P())
    out_specs = (P(("grp", "dev"), "side", None, None, None), P(("grp", "dev"), None))
    return jax.shard_map(shards, mesh=mesh, in_specs=in_specs, out_specs=out_specs, check_vma=False)
```

```python
import functools
import math

import jax
import jax.numpy as jnp
from jax import lax
from jax.experimental import pallas as pl
from jax.experimental.pallas import tpu as pltpu
from jax.sharding import PartitionSpec as P

ITERS = 3
TURN = 32
GAIN = 20.0 * math.log2(math.e)
MESH = pl.DeviceIdType.MESH
NT = (((1,), (1,)), ((), ()))
f32 = jnp.float32
bf16 = jnp.bfloat16
PIECES = ((0, 96), (96, 80), (176, 80))


def place():
    d = lax.axis_index("dev")
    return lax.axis_index("side"), (d // 4, lax.axis_index("grp"), d % 4)


def flip_a(p):
    return p + 1 - 2 * (p % 2)


def flip_b(p):
    return 3 - p


def member(at, flip, bits, core):
    x, y, z = [flip(p) if (bits >> k) & 1 else p for k, p in enumerate(at)]
    return (core, y, x * 4 + z)


def dot(a, b):
    return jnp.dot(a, b, preferred_element_type=f32)


def dot_nt(a, b):
    return lax.dot_general(a, b, NT, preferred_element_type=f32)


def split_dot(onehot, values):
    high = values.astype(bf16)
    low = (values - high.astype(f32)).astype(bf16)
    return dot(onehot, high) + dot(onehot, low)


def kernel(
    T,
    x_ref,
    partners_ref,
    counts_ref,
    mapped_ref,
    scale_ref,
    most_ref,
    oa,
    oat,
    ob,
    obt,
    obd,
    index,
    idx,
    final,
    norms_a,
    norms_b,
    norm_sem,
    abuf,
    bbuf,
    tiles,
    row_norm,
    col_norm,
    sums,
    columns,
    spread,
    dense,
    row_send,
    col_send,
    row_recv,
    col_recv,
    numer,
    ship,
    landed,
    own_sem,
    sib_sem,
    gather_sem,
    relay_sem,
    out_sem,
    row_sem,
    col_sem,
    half_sem,
    index_sem,
):
    core, at = place()
    other = 1 - core
    sibling = member(at, flip_a, 0, other)
    flips = (flip_a, flip_b)
    norm_bufs = (norms_a, norms_b)
    bufs = (abuf, bbuf)

    barrier = pltpu.get_barrier_semaphore()
    greeted = [sibling]
    for m in range(1, 8):
        greeted += [member(at, flip_a, m, core), member(at, flip_b, m, core), member(at, flip_b, m, other)]
    for peer in greeted:
        pl.semaphore_signal(barrier, inc=1, device_id=peer, device_id_type=MESH)
    pl.semaphore_wait(barrier, len(greeted))

    def remote(src, dst, send, recv, peer):
        return pltpu.make_async_remote_copy(
            src_ref=src, dst_ref=dst, send_sem=send, recv_sem=recv, device_id=peer, device_id_type=MESH
        )

    def unit(cat, slot, piece):
        start, size = PIECES[piece]
        if cat == 0:
            return abuf.at[pl.ds(slot * 2, 2), pl.ds(start, size)]
        return bbuf.at[slot, pl.ds(core * 2, 2), pl.ds(start, size)]

    def unit_copy(cat, dim, piece, slot, src=None):
        there = slot ^ (1 << dim)
        return remote(
            unit(cat, slot, piece) if src is None else src,
            unit(cat, there, piece),
            out_sem.at[0],
            gather_sem.at[cat, piece, there],
            member(at, flips[cat], 1 << dim, core),
        )

    def send_unit(cat, dim, piece, slot):
        copy = unit_copy(cat, dim, piece, slot)
        copy.start()
        return copy

    def send_own(cat, src):
        for step in range(3):
            for dim in range(3):
                piece = (dim - step) % 3
                start, size = PIECES[piece]
                unit_copy(cat, dim, piece, 0, None if src is None else src.at[:, pl.ds(start, size)]).start()

    own_a_half, own_b = abuf.at[pl.ds(0, 2)], bbuf.at[0]

    @pl.when(core == 0)
    def _():
        give = remote(x_ref.at[pl.ds(2, 2)], own_a_half, sib_sem.at[0], sib_sem.at[1], sibling)
        give.start()
        send_own(0, x_ref.at[pl.ds(0, 2)])
        mine = pltpu.make_async_copy(x_ref.at[pl.ds(0, 2)], own_a_half, own_sem.at[0])
        mine.start()
        mine.wait()
        give.wait_send()
        pltpu.make_async_copy(own_b, own_b, sib_sem.at[1]).wait()
        send_own(1, None)

    @pl.when(core == 1)
    def _():
        give = remote(x_ref, own_b, sib_sem.at[0], sib_sem.at[1], sibling)
        give.start()
        send_own(1, x_ref.at[pl.ds(2, 2)])
        mine = pltpu.make_async_copy(x_ref, own_b, own_sem.at[0])
        mine.start()
        mine.wait()
        give.wait_send()
        pltpu.make_async_copy(own_a_half, own_a_half, sib_sem.at[1]).wait()
        send_own(0, None)

    sent = []
    relays = []

    def arrived(cat, piece, slot):
        here = unit(cat, slot, piece)
        pltpu.make_async_copy(here, here, gather_sem.at[cat, piece, slot]).wait()
        if cat == 1:
            copy = remote(here, here, out_sem.at[1], relay_sem.at[slot], sibling)
            copy.start()
            relays.append(copy)

    def iota(shape, dim):
        return lax.broadcasted_iota(jnp.int32, shape, dim)

    diagonal = iota((128, 128), 0) == iota((128, 128), 1)

    norm_copies = []

    def send_norms():
        def inverse_norm(block, scale):
            halves = []
            for h in range(2):
                y = block[h * 128 : h * 128 + 128]
                total = jnp.sum(jnp.where(diagonal, dot_nt(y, y), 0.0), axis=0, keepdims=True)
                halves.append(lax.rsqrt(total * (1.0 / 256.0) + 1e-06) * scale)
            return jnp.concatenate(halves, axis=1)

        for i in range(2):
            norm_bufs[0][0, i : i + 1] = inverse_norm(abuf[i], GAIN / 16.0)
        for i in range(4):
            norm_bufs[1][0, i : i + 1] = inverse_norm(bbuf[0, i], 1.0 / 16.0)
        for cat in range(2):
            for m in range(1, 8):
                copy = remote(
                    norm_bufs[cat].at[0], norm_bufs[cat].at[m], norm_sem.at[0, cat], norm_sem.at[1, cat],
                    member(at, flips[cat], m, core),
                )
                copy.start()
                norm_copies.append(copy)

    def take_norms():
        for cat in range(2):
            got = norm_bufs[cat].at[pl.ds(1, 7)]
            pltpu.make_async_copy(got, got, norm_sem.at[1, cat]).wait()
        for copy in norm_copies:
            copy.wait_send()
        flipped_norms = jnp.transpose(
            jnp.concatenate([norm_bufs[0][m] for m in range(8)] + [jnp.zeros((64, 256), f32)], axis=0)
        )
        for a in range(16):
            lane = (a // 2) * 8 + a % 2
            row_norm[a] = flipped_norms[:, lane : lane + 1]
        for b in range(32):
            col_norm[b] = jnp.broadcast_to(norm_bufs[1][b // 4, b % 4 : b % 4 + 1], (8, 256))

    def bits_of(values, shifts):
        return [(values >> k) & 1 for k in shifts]

    def flipped(bits, by):
        return sum((b + f - 2 * b * f) * (1 << k) for k, (b, f) in enumerate(zip(bits, by)))

    def make_list():
        x, y, z = at
        own_low = [p % 2 for p in at]
        own_high = [p // 2 for p in at]
        named_all = partners_ref[...]
        limit_row = counts_ref[...]
        r = iota((16, 256), 0)
        cx, cy, cz = [flipped([b], [p % 2]) + 2 * (p // 2) for b, p in zip(bits_of(r, (1, 2, 3)), at)]
        chosen = iota((16, 256), 1) == (cy * 16 + cx * 4 + cz) * 4 + 2 * core + (r & 1)
        named = dot_nt(chosen.astype(f32).astype(bf16), named_all.astype(f32).astype(bf16)).astype(jnp.int32)
        limit = jnp.sum(jnp.where(chosen, jnp.broadcast_to(limit_row, (16, 256)), 0).astype(f32), axis=1, keepdims=True)
        slot_at = iota((16, 32), 1).astype(f32)

        def coords(entry):
            owner = entry >> 2
            return (owner >> 2) & 3, owner >> 4, owner & 3

        parts = coords(named)
        active = slot_at < limit
        for p, q in zip(parts, at):
            active &= (p == q) | (p == 3 - q)
        jb = sum((p >> 1) * (1 << k) for k, p in enumerate(parts))
        pick = (named & 3) + 1
        lane = iota((16, 128), 1)
        bp = jnp.zeros((16, 128), f32)
        for k in range(8):
            best = jnp.max(jnp.where(active & (jb == k), pick, 0).astype(f32), axis=1, keepdims=True)
            bp = jnp.where(lane == k, best, bp)
        used = jnp.where(bp > 0, 1.0, 0.0).astype(bf16)
        i128, j128 = iota((128, 128), 0), iota((128, 128), 1)

        def mask(m):
            return jnp.where(m, 1.0, 0.0).astype(bf16)

        in_row = dot(used, mask(i128 < j128))
        of_row = dot(used, mask(i128 < 128))
        above = dot(mask(iota((16, 16), 1) < iota((16, 16), 0)), of_row.astype(bf16))
        pos = above + in_row
        k3 = bits_of(lane, (0, 1, 2))
        b_rel = flipped(k3, own_high) * 4 + jnp.maximum(bp.astype(jnp.int32) - 1, 0)
        index[pl.ds(0, 16), :] = jnp.where(bp > 0, jnp.minimum(pos, T - 1.0), 0.0).astype(jnp.int32)
        index[pl.ds(16, 16), :] = jnp.where(lane < 8, b_rel, 0)

        spread_out = mask(i128 == (j128 & 7))
        own_lane = (lane >> 3) == iota((16, 128), 0)

        def flat(values):
            return jnp.sum(jnp.where(own_lane, dot(values.astype(bf16), spread_out), 0.0), axis=0, keepdims=True)

        bp_row, pos_row = flat(bp), flat(pos)
        hot = mask((iota((T, 128), 0).astype(f32) == pos_row) & (bp_row > 0))
        e = iota((8, 128), 1)
        pick_row = jnp.maximum(jnp.broadcast_to(bp_row, (8, 128)).astype(jnp.int32) - 1, 0)
        b_e = flipped(bits_of(e, (0, 1, 2)), own_high) * 4 + pick_row
        values = jnp.where(iota((8, 128), 0) == 0, e >> 3, b_e).astype(f32).astype(bf16)
        index[pl.ds(32, 8), pl.ds(0, T)] = dot_nt(values, hot).astype(jnp.int32)
        fetch = pltpu.make_async_copy(index, idx, index_sem.at[0])
        fetch.start()
        e16, e32 = iota((16, 128), 1), iota((32, 128), 1)
        a_abs = flipped(bits_of(e16, (4, 5, 6)), own_low) * 2 + ((e16 >> 3) & 1)
        a_hot = mask(iota((16, 128), 0) == a_abs)
        b_abs = (e32 & 7) * 4 + jnp.broadcast_to(bp_row, (32, 128)).astype(jnp.int32) - 1
        b_hot = mask((iota((32, 128), 0) == b_abs) & (bp_row > 0))
        oa[...] = dot_nt(a_hot, hot).astype(bf16)
        oat[...] = dot_nt(hot, a_hot).astype(bf16)
        ob[...] = dot_nt(b_hot, hot).astype(bf16)
        obt[...] = dot_nt(hot, b_hot).astype(bf16)
        obd[...] = dot_nt(mask(i128 == j128), b_hot).astype(bf16)

        active = iota((32, 256), 0) < limit_row
        kind = sum((((p + 1) >> 1) & 1) * (1 << k) for k, p in enumerate(coords(named_all)))
        g, row = iota((16, 256), 0), iota((16, 256), 1)
        group = ((row >> 7) & 1) * 8 + ((row >> 5) & 1) * 4 + ((row >> 3) & 1) * 2 + ((row >> 1) & 1)
        members = mask(g == group)
        most = jnp.zeros((16, 1), f32)
        for k in range(8):
            most = jnp.maximum(
                most, jnp.sum(dot_nt(members, mask(active & (kind == k))), axis=1, keepdims=True)
            )
        most_ref[0, 0] = jnp.max(most)
        fetch.wait()

    def received(steps):
        for r in range(3):
            slot = steps(1 << r, 1 << ((r + 1) % 3), 1 << ((r + 2) % 3))
            for cat in range(2):
                arrived(cat, r, slot)
                yield cat, r, slot

    send_norms()
    for cat, r, slot in received(lambda k0, k1, k2: k0):
        sent.append(send_unit(cat, (r + 1) % 3, r, slot))
    for r in range(3):
        for cat in range(2):
            sent.append(send_unit(cat, (r + 2) % 3, r, 1 << r))
    for cat, r, slot in received(lambda k0, k1, k2: k1):
        sent.append(send_unit(cat, (r + 2) % 3, r, slot))
    make_list()
    for cat, r, slot in received(lambda k0, k1, k2: k0 | k1):
        sent.append(send_unit(cat, (r + 2) % 3, r, slot))
    for _ in received(lambda k0, k1, k2: k2):
        pass
    take_norms()
    for _ in received(lambda k0, k1, k2: k2 | k0):
        pass
    for _ in received(lambda k0, k1, k2: k2 | k1):
        pass
    for _ in received(lambda k0, k1, k2: 7):
        pass
    for cat in range(2):
        for step in range(3):
            for dim in range(3):
                sent.append(unit_copy(cat, dim, (dim - step) % 3, 0))
    for copy in sent:
        copy.wait_send()
    for copy in relays:
        copy.wait_send()
    for slot in range(1, 8):
        here = bbuf.at[slot, pl.ds(other * 2, 2)]
        pltpu.make_async_copy(here, here, relay_sem.at[slot]).wait()

    def build(i, c):
        for u in range(TURN):
            t = i * TURN + u
            a, b = jnp.clip(idx[32, t], 0, 15), jnp.clip(idx[33, t], 0, 31)
            scores = dot_nt(abuf[a], bbuf[b // 4, b % 4])
            tiles[t] = jnp.exp2(scores * row_norm[a] * col_norm[b][0:1] - GAIN).astype(bf16)
        return c

    lax.fori_loop(0, T // TURN, build, 0)

    row_id = iota((8, 256), 0)
    lane_id = iota((256, T), 1)

    def row_sweep():
        def body(i, c):
            beside = columns[...]
            for g in range(TURN // 8):
                base = i * TURN + g * 8
                rows = pl.ds(pl.multiple_of(base, 8), 8)
                left = spread[rows, :]
                left_bf = left.astype(bf16)
                total = jnp.zeros((8, 256), f32)
                for u in range(8):
                    tile = tiles[base + u]
                    if u % 2 == 0:
                        total = jnp.where(row_id == u, dot_nt(left_bf, tile), total)
                    else:
                        scaled = tile.astype(f32) * left[u : u + 1]
                        mass = jnp.sum(scaled[:, 0:128] + scaled[:, 128:256], axis=1, keepdims=True)
                        beside = jnp.where(lane_id == base + u, mass, beside)
                sums[rows, :] = total
            columns[...] = beside
            return c

        columns[...] = jnp.zeros((256, T), f32)
        lax.fori_loop(0, T // TURN, body, 0)
        beside = columns[...]
        high = beside.astype(bf16)
        low = (beside - high.astype(f32)).astype(bf16)
        return split_dot(oa[...], sums[...]) + dot_nt(oa[...], high) + dot_nt(oa[...], low)

    def col_sweep():
        def body(i, c):
            for g in range(TURN // 8):
                base = i * TURN + g * 8
                rows = pl.ds(pl.multiple_of(base, 8), 8)
                left = spread[rows, :].astype(bf16)
                total = jnp.zeros((8, 256), f32)
                for u in range(8):
                    total = jnp.where(row_id == u, dot(left, tiles[base + u]), total)
                sums[rows, :] = total
            return c

        lax.fori_loop(0, T // TURN, body, 0)
        return split_dot(ob[...], sums[...])

    def row_exchange(phase, partial):
        row_send[phase] = partial.astype(bf16)
        copies = []
        for m in range(1, 8):
            copy = remote(
                row_send.at[phase], row_recv.at[phase, m], row_sem.at[0, phase], row_sem.at[1, phase],
                member(at, flip_a, m, core),
            )
            copy.start()
            copies.append(copy)
        return copies

    def row_result(phase, copies):
        got = row_recv.at[phase, pl.ds(1, 7)]
        pltpu.make_async_copy(got, got, row_sem.at[1, phase]).wait()
        total = row_send[phase].astype(f32)
        for m in range(1, 8):
            total += row_recv[phase, m].astype(f32)
        for copy in copies:
            copy.wait_send()
        return total

    def col_exchange(phase, partial):
        col_send[phase] = partial.astype(bf16)
        copies = []
        for far in range(2):
            for m in range(8):
                if far + m:
                    copy = remote(
                        col_send.at[phase], col_recv.at[phase, far * 8 + m], col_sem.at[0, phase],
                        col_sem.at[1, phase], member(at, flip_b, m, other if far else core),
                    )
                    copy.start()
                    copies.append(copy)
        got = col_recv.at[phase, pl.ds(1, 15)]
        pltpu.make_async_copy(got, got, col_sem.at[1, phase]).wait()
        total = col_send[phase].astype(f32)
        for m in range(1, 16):
            total += col_recv[phase, m].astype(f32)
        for copy in copies:
            copy.wait_send()
        return total

    spread[...] = jnp.ones((T, 256), f32)
    for phase in range(ITERS):
        scale_a = 1.0 / row_result(phase, row_exchange(phase, row_sweep()))
        spread[...] = dot(oat[...], scale_a.astype(bf16))
        scale_b = 1.0 / (1.0 + col_exchange(phase, col_sweep()))
        spread[...] = dot(obt[...], scale_b.astype(bf16))
    x, y, z = at
    member_b = x // 2 + 2 * (y // 2) + 4 * (z // 2)
    sums[pl.ds(0, 32), :] = scale_b
    near_rows = sums[pl.ds(pl.multiple_of((member_b // 2) * 8, 8), 8), :]
    scale_ref[...] = jnp.where(member_b % 2 == 0, near_rows[0:4], near_rows[4:8])
    dense[...] = dot(obd[...], scale_b.astype(bf16))

    def partial(slot):
        def body(i, c):
            total, mass = None, None
            a = slot * 2 + i
            rows = dense[pl.ds(pl.multiple_of(a * 8, 8), 8), :]
            for d in range(8):
                weights = tiles[jnp.clip(idx[a, d], 0, T - 1)].astype(f32) * rows[d : d + 1]
                b = jnp.clip(idx[16 + a, d], 0, 31)
                part = dot(weights.astype(bf16), bbuf[b // 4, b % 4])
                half = weights[:, 0:128] + weights[:, 128:256]
                total = part if total is None else total + part
                mass = half if mass is None else mass + half
            numer[a] = total
            column = jnp.sum(mass, axis=1, keepdims=True)
            a_at = flipped([(slot >> k) & 1 for k in range(3)], [p % 2 for p in at]) * 2 + i
            final[...] = jnp.where(iota((256, 128), 1) == a_at, column, final[...])
            return c

        lax.fori_loop(0, 2, body, 0)

    halves = []
    final[...] = jnp.zeros((256, 128), f32)

    def send_half(piece, slot, dim, order):
        start, size = PIECES[piece]
        two, rows = pl.ds(slot * 2, 2), pl.ds(start, size)
        ship[two, rows, :] = numer[two, rows, :].astype(bf16)
        there = slot ^ (1 << dim)
        copy = remote(
            ship.at[two, rows], landed.at[order, pl.ds(there * 2, 2), rows], out_sem.at[2], half_sem.at[order, piece, there],
            member(at, flip_a, 1 << dim, core),
        )
        copy.start()
        halves.append(copy)

    def add_half(piece, slot, order):
        start, size = PIECES[piece]
        two, rows = pl.ds(slot * 2, 2), pl.ds(start, size)
        here = landed.at[order, two, rows]
        pltpu.make_async_copy(here, here, half_sem.at[order, piece, slot]).wait()
        numer[two, rows, :] = numer[two, rows, :] + landed[order, two, rows, :].astype(f32)

    for slot in (7, 3, 5, 6, 1, 2, 4, 0):
        partial(slot)
        for r in range(3):
            if (slot >> r) & 1:
                send_half(r, slot, r, 0)
    for r in range(3):
        k1, k2 = 1 << ((r + 1) % 3), 1 << ((r + 2) % 3)
        add_half(r, k1 | k2, 0)
        send_half(r, k1 | k2, (r + 1) % 3, 1)
    row_copies = row_exchange(ITERS, jnp.transpose(final[...])[0:16])
    for r in range(3):
        k1, k2 = 1 << ((r + 1) % 3), 1 << ((r + 2) % 3)
        add_half(r, k1, 0)
        send_half(r, k1, (r + 1) % 3, 1)
    for r in range(3):
        k1, k2 = 1 << ((r + 1) % 3), 1 << ((r + 2) % 3)
        add_half(r, k2, 0)
        add_half(r, k2, 1)
        send_half(r, k2, (r + 2) % 3, 2)
    sums[pl.ds(0, 16), :] = row_result(ITERS, row_copies)
    own_a = x % 2 + 2 * (y % 2) + 4 * (z % 2)
    near_rows = sums[pl.ds(pl.multiple_of((own_a // 4) * 8, 8), 8), :]
    mine = near_rows[0:2]
    for k in range(1, 4):
        mine = jnp.where(own_a % 4 == k, near_rows[2 * k : 2 * k + 2], mine)
    column = jnp.transpose(jnp.broadcast_to(1.0 / mine[:, None, :], (2, 128, 256)).reshape(256, 256))
    for r in range(3):
        for order in range(3):
            add_half(r, 0, order)
    for i in range(2):
        inverse = column[:, i * 128 : i * 128 + 1]
        mapped_ref[i] = (numer[i] * inverse).astype(bf16)
    for copy in halves:
        copy.wait_send()


def transport(T, cid, own, partners, counts):
    vmem = pl.BlockSpec(memory_space=pltpu.VMEM)
    dma = pltpu.SemaphoreType.DMA
    return pl.pallas_call(
        functools.partial(kernel, T),
        out_shape=(
            jax.ShapeDtypeStruct((2, 256, 256), bf16),
            jax.ShapeDtypeStruct((4, 256), f32),
            jax.ShapeDtypeStruct((1, 1), f32),
        ),
        in_specs=[pl.BlockSpec(memory_space=pl.ANY), vmem, vmem],
        out_specs=(vmem, vmem, pl.BlockSpec(memory_space=pltpu.SMEM)),
        scratch_shapes=[
            pltpu.VMEM((16, T), bf16),
            pltpu.VMEM((T, 16), bf16),
            pltpu.VMEM((32, T), bf16),
            pltpu.VMEM((T, 32), bf16),
            pltpu.VMEM((128, 32), bf16),
            pltpu.VMEM((40, 128), jnp.int32),
            pltpu.SMEM((40, 128), jnp.int32),
            pltpu.VMEM((256, 128), f32),
            pltpu.VMEM((8, 8, 256), f32),
            pltpu.VMEM((8, 8, 256), f32),
            dma((2, 2)),
            pltpu.VMEM((16, 256, 256), bf16),
            pltpu.VMEM((8, 4, 256, 256), bf16),
            pltpu.VMEM((T, 256, 256), bf16),
            pltpu.VMEM((16, 256, 1), f32),
            pltpu.VMEM((32, 8, 256), f32),
            pltpu.VMEM((T, 256), f32),
            pltpu.VMEM((256, T), f32),
            pltpu.VMEM((T, 256), f32),
            pltpu.VMEM((128, 256), f32),
            pltpu.VMEM((4, 16, 256), bf16),
            pltpu.VMEM((3, 32, 256), bf16),
            pltpu.VMEM((4, 8, 16, 256), bf16),
            pltpu.VMEM((3, 16, 32, 256), bf16),
            pltpu.VMEM((16, 256, 256), f32),
            pltpu.VMEM((16, 256, 256), bf16),
            pltpu.VMEM((3, 16, 256, 256), bf16),
            dma((1,)),
            dma((2,)),
            dma((2, 3, 8)),
            dma((8,)),
            dma((3,)),
            dma((2, 4)),
            dma((2, 3)),
            dma((3, 3, 8)),
            dma((1,)),
        ],
        compiler_params=pltpu.CompilerParams(
            collective_id=cid, has_side_effects=True, vmem_limit_bytes=60 << 20
        ),
        name=f"transport_{T}",
    )(own, partners, counts)


def shards(embeds, partners, counts):
    args = embeds.reshape(4, 256, 256), partners.T, counts.reshape(1, 256)
    mapped, scale, most = transport(64, 0, *args)
    mapped, scale = lax.cond(
        most.reshape(()) <= 64.0,
        lambda mapped, scale, *args: (mapped, scale),
        lambda mapped, scale, *args: transport(128, 1, *args)[:2],
        mapped,
        scale,
        *args,
    )
    return mapped.reshape(1, 1, 2, 256, 256), scale


def solution(mesh):
    in_specs = (P("side", ("grp", "dev"), None, None), P(), P())
    out_specs = (P(("grp", "dev"), "side", None, None, None), P(("grp", "dev"), None))
    return jax.shard_map(shards, mesh=mesh, in_specs=in_specs, out_specs=out_specs, check_vma=False)
```

```python
import functools
import math

import jax
import jax.numpy as jnp
from jax import lax
from jax.experimental import pallas as pl
from jax.experimental.pallas import tpu as pltpu
from jax.sharding import PartitionSpec as P

ITERS = 3
TURN = 32
GAIN = 20.0 * math.log2(math.e)
MESH = pl.DeviceIdType.MESH
NT = (((1,), (1,)), ((), ()))
f32 = jnp.float32
bf16 = jnp.bfloat16
PIECES = ((0, 96), (96, 80), (176, 80))


def place():
    d = lax.axis_index("dev")
    return lax.axis_index("side"), (d // 4, lax.axis_index("grp"), d % 4)


def flip_a(p):
    return p + 1 - 2 * (p % 2)


def flip_b(p):
    return 3 - p


def member(at, flip, bits, core):
    x, y, z = [flip(p) if (bits >> k) & 1 else p for k, p in enumerate(at)]
    return (core, y, x * 4 + z)


def dot(a, b):
    return jnp.dot(a, b, preferred_element_type=f32)


def dot_nt(a, b):
    return lax.dot_general(a, b, NT, preferred_element_type=f32)


def kernel(
    T,
    x_ref,
    partners_ref,
    counts_ref,
    mapped_ref,
    scale_ref,
    most_ref,
    oa,
    oat,
    ob,
    obt,
    obd,
    partners,
    counts,
    index,
    idx,
    final,
    norms_a,
    norms_b,
    norm_sem,
    abuf,
    bbuf,
    tiles,
    row_norm,
    col_norm,
    sums,
    columns,
    spread,
    dense,
    row_send,
    col_send,
    row_recv,
    col_recv,
    scales,
    half_swap,
    numer,
    ship,
    landed,
    own_sem,
    sib_sem,
    gather_sem,
    relay_sem,
    out_sem,
    row_sem,
    col_sem,
    half_sem,
    index_sem,
):
    core, at = place()
    other = 1 - core
    sibling = member(at, flip_a, 0, other)
    flips = (flip_a, flip_b)
    norm_bufs = (norms_a, norms_b)
    bufs = (abuf, bbuf)

    barrier = pltpu.get_barrier_semaphore()
    greeted = [sibling]
    for m in range(1, 8):
        greeted += [member(at, flip_a, m, core), member(at, flip_b, m, core), member(at, flip_b, m, other)]
        if m in (1, 2, 4):
            greeted.append(member(at, flip_a, m, other))
    for peer in greeted:
        pl.semaphore_signal(barrier, inc=1, device_id=peer, device_id_type=MESH)
    pl.semaphore_wait(barrier, len(greeted))

    def remote(src, dst, send, recv, peer):
        return pltpu.make_async_remote_copy(
            src_ref=src, dst_ref=dst, send_sem=send, recv_sem=recv, device_id=peer, device_id_type=MESH
        )

    def unit(cat, slot, piece):
        start, size = PIECES[piece]
        if cat == 0:
            return abuf.at[pl.ds(slot * 2, 2), pl.ds(start, size)]
        return bbuf.at[slot, pl.ds(core * 2, 2), pl.ds(start, size)]

    def send_unit(cat, dim, piece, slot):
        there = slot ^ (1 << dim)
        remote(
            unit(cat, slot, piece),
            unit(cat, there, piece),
            out_sem.at[0],
            gather_sem.at[cat, piece, there],
            member(at, flips[cat], 1 << dim, core),
        ).start()

    def send_own(cat):
        for step in range(3):
            for dim in range(3):
                piece = (dim - step) % 3
                start, size = PIECES[piece]
                rows, there = pl.ds(start, size), 1 << dim
                for half in range(2):
                    two = pl.ds(half * 2, 2)
                    remote(
                        x_ref.at[two, rows],
                        abuf.at[pl.ds(there * 2, 2), rows] if cat == 0 else bbuf.at[there, two, rows],
                        out_sem.at[0],
                        gather_sem.at[cat, piece, there],
                        member(at, flips[cat], there, half),
                    ).start()

    own_a_half, own_b = abuf.at[pl.ds(0, 2)], bbuf.at[0]

    def landed_at(ref, sem):
        pltpu.make_async_copy(ref, ref, sem).wait()

    fetches = [
        pltpu.make_async_copy(partners_ref, partners, own_sem.at[1]),
        pltpu.make_async_copy(counts_ref, counts, own_sem.at[2]),
    ]

    @pl.when(core == 0)
    def _():
        give = remote(x_ref.at[pl.ds(2, 2)], own_a_half, sib_sem.at[0], sib_sem.at[1], sibling)
        give.start()
        mine = pltpu.make_async_copy(x_ref.at[pl.ds(0, 2)], own_a_half, own_sem.at[0])
        mine.start()
        send_own(0)
        mine.wait()
        give.wait_send()
        landed_at(own_b, sib_sem.at[1])

    @pl.when(core == 1)
    def _():
        give = remote(x_ref, own_b, sib_sem.at[0], sib_sem.at[1], sibling)
        give.start()
        mine = pltpu.make_async_copy(x_ref, own_b, own_sem.at[0])
        mine.start()
        send_own(1)
        mine.wait()
        give.wait_send()
        landed_at(own_a_half, sib_sem.at[1])

    for fetch in fetches:
        fetch.start()

    def arrived(cat, piece, slot):
        here = unit(cat, slot, piece)
        pltpu.make_async_copy(here, here, gather_sem.at[cat, piece, slot]).wait()
        if cat == 1:
            remote(here, here, out_sem.at[1], relay_sem.at[slot], sibling).start()

    def iota(shape, dim):
        return lax.broadcasted_iota(jnp.int32, shape, dim)

    diagonal = iota((128, 128), 0) == iota((128, 128), 1)

    def send_norms():
        def inverse_norm(block, scale):
            halves = []
            for h in range(2):
                y = block[h * 128 : h * 128 + 128]
                total = jnp.sum(jnp.where(diagonal, dot_nt(y, y), 0.0), axis=0, keepdims=True)
                halves.append(lax.rsqrt(total * (1.0 / 256.0) + 1e-06) * scale)
            return jnp.concatenate(halves, axis=1)

        for i in range(2):
            norm_bufs[0][0, i : i + 1] = inverse_norm(abuf[i], GAIN / 16.0)
        for i in range(4):
            norm_bufs[1][0, i : i + 1] = inverse_norm(bbuf[0, i], 1.0 / 16.0)
        for cat in range(2):
            for m in range(1, 8):
                remote(
                    norm_bufs[cat].at[0], norm_bufs[cat].at[m], norm_sem.at[0, cat], norm_sem.at[1, cat],
                    member(at, flips[cat], m, core),
                ).start()

    def take_norms():
        for cat in range(2):
            landed_at(norm_bufs[cat].at[pl.ds(1, 7)], norm_sem.at[1, cat])
        flipped_norms = jnp.transpose(
            jnp.concatenate([norm_bufs[0][m] for m in range(8)] + [jnp.zeros((64, 256), f32)], axis=0)
        )
        for a in range(16):
            lane = (a // 2) * 8 + a % 2
            row_norm[a] = flipped_norms[:, lane : lane + 1]
        for b in range(32):
            col_norm[b] = jnp.broadcast_to(norm_bufs[1][b // 4, b % 4 : b % 4 + 1], (8, 256))

    def bits_of(values, shifts):
        return [(values >> k) & 1 for k in shifts]

    def flipped(bits, by):
        return sum((b + f - 2 * b * f) * (1 << k) for k, (b, f) in enumerate(zip(bits, by)))

    def make_list():
        x, y, z = at
        own_low = [p % 2 for p in at]
        own_high = [p // 2 for p in at]
        for fetch in fetches:
            fetch.wait()
        named_all = partners[...]
        limit_row = counts[...]
        r = iota((16, 256), 0)
        cx, cy, cz = [flipped([b], [p % 2]) + 2 * (p // 2) for b, p in zip(bits_of(r, (1, 2, 3)), at)]
        chosen = iota((16, 256), 1) == (cy * 16 + cx * 4 + cz) * 4 + 2 * core + (r & 1)
        named = dot_nt(chosen.astype(f32).astype(bf16), named_all.astype(f32).astype(bf16)).astype(jnp.int32)
        limit = jnp.sum(jnp.where(chosen, jnp.broadcast_to(limit_row, (16, 256)), 0).astype(f32), axis=1, keepdims=True)
        slot_at = iota((16, 32), 1).astype(f32)

        def coords(entry):
            owner = entry >> 2
            return (owner >> 2) & 3, owner >> 4, owner & 3

        parts = coords(named)
        active = slot_at < limit
        for p, q in zip(parts, at):
            active &= (p == q) | (p == 3 - q)
        jb = sum((p >> 1) * (1 << k) for k, p in enumerate(parts))
        pick = (named & 3) + 1
        lane = iota((16, 128), 1)
        bp = jnp.zeros((16, 128), f32)
        for k in range(8):
            best = jnp.max(jnp.where(active & (jb == k), pick, 0).astype(f32), axis=1, keepdims=True)
            bp = jnp.where(lane == k, best, bp)
        used = jnp.where(bp > 0, 1.0, 0.0).astype(bf16)
        i128, j128 = iota((128, 128), 0), iota((128, 128), 1)

        def mask(m):
            return jnp.where(m, 1.0, 0.0).astype(bf16)

        in_row = dot(used, mask(i128 < j128))
        of_row = dot(used, mask(i128 < 128))
        above = dot(mask(iota((16, 16), 1) < iota((16, 16), 0)), of_row.astype(bf16))
        pos = above + in_row
        k3 = bits_of(lane, (0, 1, 2))
        b_rel = flipped(k3, own_high) * 4 + jnp.maximum(bp.astype(jnp.int32) - 1, 0)
        index[pl.ds(0, 16), :] = jnp.where(bp > 0, jnp.minimum(pos, T - 1.0), 0.0).astype(jnp.int32)
        index[pl.ds(16, 16), :] = jnp.where(lane < 8, b_rel, 0)

        spread_out = mask(i128 == (j128 & 7))
        own_lane = (lane >> 3) == iota((16, 128), 0)

        def flat(values):
            return jnp.sum(jnp.where(own_lane, dot(values.astype(bf16), spread_out), 0.0), axis=0, keepdims=True)

        bp_row, pos_row = flat(bp), flat(pos)
        hot = mask((iota((T, 128), 0).astype(f32) == pos_row) & (bp_row > 0))
        e = iota((8, 128), 1)
        pick_row = jnp.maximum(jnp.broadcast_to(bp_row, (8, 128)).astype(jnp.int32) - 1, 0)
        b_e = flipped(bits_of(e, (0, 1, 2)), own_high) * 4 + pick_row
        values = jnp.where(iota((8, 128), 0) == 0, e >> 3, b_e).astype(f32).astype(bf16)
        index[pl.ds(32, 8), pl.ds(0, T)] = dot_nt(values, hot).astype(jnp.int32)
        fetch = pltpu.make_async_copy(index, idx, index_sem.at[0])
        fetch.start()
        e16, e32 = iota((16, 128), 1), iota((32, 128), 1)
        a_abs = flipped(bits_of(e16, (4, 5, 6)), own_low) * 2 + ((e16 >> 3) & 1)
        a_hot = mask(iota((16, 128), 0) == a_abs)
        b_abs = (e32 & 7) * 4 + jnp.broadcast_to(bp_row, (32, 128)).astype(jnp.int32) - 1
        b_hot = mask((iota((32, 128), 0) == b_abs) & (bp_row > 0))
        oa[...] = dot_nt(a_hot, hot).astype(bf16)
        oat[...] = dot_nt(hot, a_hot).astype(bf16)
        ob[...] = dot_nt(b_hot, hot).astype(bf16)
        obt[...] = dot_nt(hot, b_hot).astype(bf16)
        obd[...] = dot_nt(mask(i128 == j128), b_hot).astype(bf16)

        active = iota((32, 256), 0) < limit_row
        kind = sum((((p + 1) >> 1) & 1) * (1 << k) for k, p in enumerate(coords(named_all)))
        g, row = iota((16, 256), 0), iota((16, 256), 1)
        group = ((row >> 7) & 1) * 8 + ((row >> 5) & 1) * 4 + ((row >> 3) & 1) * 2 + ((row >> 1) & 1)
        members = mask(g == group)
        most = jnp.zeros((16, 1), f32)
        for k in range(8):
            most = jnp.maximum(
                most, jnp.sum(dot_nt(members, mask(active & (kind == k))), axis=1, keepdims=True)
            )
        most_ref[0, 0] = jnp.max(most)
        fetch.wait()

    def received(steps):
        for r in range(3):
            slot = steps(1 << r, 1 << ((r + 1) % 3), 1 << ((r + 2) % 3))
            for cat in range(2):
                arrived(cat, r, slot)
                yield cat, r, slot

    send_norms()
    for cat, r, slot in received(lambda k0, k1, k2: k0):
        send_unit(cat, (r + 1) % 3, r, slot)
    for r in range(3):
        for cat in range(2):
            send_unit(cat, (r + 2) % 3, r, 1 << r)
    for cat, r, slot in received(lambda k0, k1, k2: k1):
        send_unit(cat, (r + 2) % 3, r, slot)
    make_list()
    for cat, r, slot in received(lambda k0, k1, k2: k0 | k1):
        send_unit(cat, (r + 2) % 3, r, slot)
    for _ in received(lambda k0, k1, k2: k2):
        pass
    take_norms()
    for _ in received(lambda k0, k1, k2: k2 | k0):
        pass
    for _ in received(lambda k0, k1, k2: k2 | k1):
        pass
    for _ in received(lambda k0, k1, k2: 7):
        pass
    for slot in range(1, 8):
        landed_at(bbuf.at[slot, pl.ds(other * 2, 2)], relay_sem.at[slot])

    def build(i, c):
        for u in range(TURN):
            t = i * TURN + u
            a, b = jnp.clip(idx[32, t], 0, 15), jnp.clip(idx[33, t], 0, 31)
            scores = dot_nt(abuf[a], bbuf[b // 4, b % 4])
            tiles[t] = jnp.exp2(scores * row_norm[a] * col_norm[b][0:1] - GAIN).astype(bf16)
        return c

    lax.fori_loop(0, T // TURN, build, 0)

    row_id = iota((8, 256), 0)
    lane_id = iota((256, T), 1)

    def row_sweep():
        def body(i, c):
            beside = columns[...]
            for g in range(TURN // 8):
                base = i * TURN + g * 8
                rows = pl.ds(pl.multiple_of(base, 8), 8)
                left = spread[rows, :]
                left_bf = left.astype(bf16)
                total = jnp.zeros((8, 256), f32)
                for u in range(8):
                    tile = tiles[base + u]
                    if u % 2 == 0:
                        total = jnp.where(row_id == u, dot_nt(left_bf, tile), total)
                    else:
                        scaled = tile.astype(f32) * left[u : u + 1]
                        mass = jnp.sum(scaled[:, 0:128] + scaled[:, 128:256], axis=1, keepdims=True)
                        beside = jnp.where(lane_id == base + u, mass, beside)
                sums[rows, :] = total
            columns[...] = beside
            return c

        columns[...] = jnp.zeros((256, T), f32)
        lax.fori_loop(0, T // TURN, body, 0)
        return dot(oa[...], sums[...].astype(bf16)) + dot_nt(oa[...], columns[...].astype(bf16))

    def col_sweep():
        def body(i, c):
            for g in range(TURN // 8):
                base = i * TURN + g * 8
                rows = pl.ds(pl.multiple_of(base, 8), 8)
                left = spread[rows, :].astype(bf16)
                total = jnp.zeros((8, 256), f32)
                for u in range(8):
                    total = jnp.where(row_id == u, dot(left, tiles[base + u]), total)
                sums[rows, :] = total
            return c

        lax.fori_loop(0, T // TURN, body, 0)
        return dot(ob[...], sums[...].astype(bf16))

    def row_exchange(phase, partial):
        row_send[phase] = partial.astype(bf16)
        for m in range(1, 8):
            remote(
                row_send.at[phase], row_recv.at[phase, m], row_sem.at[0, phase], row_sem.at[1, phase],
                member(at, flip_a, m, core),
            ).start()

    def row_result(phase):
        landed_at(row_recv.at[phase, pl.ds(1, 7)], row_sem.at[1, phase])
        total = row_send[phase].astype(f32)
        for m in range(1, 8):
            total += row_recv[phase, m].astype(f32)
        return total

    def col_exchange(phase, partial):
        col_send[phase] = partial.astype(bf16)
        for far, to in enumerate((core, other)):
            for m in range(8):
                if far + m:
                    remote(
                        col_send.at[phase, pl.ds(pl.multiple_of(to * 16, 16), 16)],
                        col_recv.at[phase, far * 8 + m],
                        col_sem.at[0, phase],
                        col_sem.at[1, phase],
                        member(at, flip_b, m, to),
                    ).start()
        landed_at(col_recv.at[phase, pl.ds(1, 15)], col_sem.at[1, phase])
        mine = pl.ds(pl.multiple_of(core * 16, 16), 16)
        total = col_send[phase, mine].astype(f32)
        for m in range(1, 16):
            total += col_recv[phase, m].astype(f32)
        scales[phase, mine] = 1.0 / (1.0 + total)
        here = scales.at[phase, mine]
        remote(here, here, half_swap.at[0, phase], half_swap.at[1, phase], sibling).start()
        landed_at(scales.at[phase, pl.ds(pl.multiple_of(other * 16, 16), 16)], half_swap.at[1, phase])
        return scales[phase]

    spread[...] = jnp.ones((T, 256), f32)
    for phase in range(ITERS):
        row_exchange(phase, row_sweep())
        scale_a = 1.0 / row_result(phase)
        spread[...] = dot(oat[...], scale_a.astype(bf16))
        scale_b = col_exchange(phase, col_sweep())
        spread[...] = dot(obt[...], scale_b.astype(bf16))
    x, y, z = at
    member_b = x // 2 + 2 * (y // 2) + 4 * (z // 2)
    near_rows = scales[ITERS - 1, pl.ds(pl.multiple_of((member_b // 2) * 8, 8), 8), :]
    scale_ref[...] = jnp.where(member_b % 2 == 0, near_rows[0:4], near_rows[4:8])
    dense[...] = dot(obd[...], scale_b.astype(bf16))

    def partial(slot):
        def body(i, c):
            total, mass = None, None
            a = slot * 2 + i
            rows = dense[pl.ds(pl.multiple_of(a * 8, 8), 8), :]
            for d in range(8):
                weights = tiles[jnp.clip(idx[a, d], 0, T - 1)].astype(f32) * rows[d : d + 1]
                b = jnp.clip(idx[16 + a, d], 0, 31)
                part = dot(weights.astype(bf16), bbuf[b // 4, b % 4])
                half = weights[:, 0:128] + weights[:, 128:256]
                total = part if total is None else total + part
                mass = half if mass is None else mass + half
            numer[a] = total
            column = jnp.sum(mass, axis=1, keepdims=True)
            a_at = flipped([(slot >> k) & 1 for k in range(3)], [p % 2 for p in at]) * 2 + i
            final[...] = jnp.where(iota((256, 128), 1) == a_at, column, final[...])
            return c

        lax.fori_loop(0, 2, body, 0)

    final[...] = jnp.zeros((256, 128), f32)

    def send_half(piece, slot, dim, order):
        start, size = PIECES[piece]
        two, rows = pl.ds(slot * 2, 2), pl.ds(start, size)
        ship[two, rows, :] = numer[two, rows, :].astype(bf16)
        there = slot ^ (1 << dim)
        remote(
            ship.at[two, rows], landed.at[order, pl.ds(there * 2, 2), rows], out_sem.at[2], half_sem.at[order, piece, there],
            member(at, flip_a, 1 << dim, core),
        ).start()

    def add_half(piece, slot, order):
        start, size = PIECES[piece]
        two, rows = pl.ds(slot * 2, 2), pl.ds(start, size)
        here = landed.at[order, two, rows]
        pltpu.make_async_copy(here, here, half_sem.at[order, piece, slot]).wait()
        numer[two, rows, :] = numer[two, rows, :] + landed[order, two, rows, :].astype(f32)

    def map_slots(slots):
        for slot in slots:
            partial(slot)
            for r in range(3):
                if (slot >> r) & 1:
                    send_half(r, slot, r, 0)

    near_dims = [(r, 1 << ((r + 1) % 3), 1 << ((r + 2) % 3)) for r in range(3)]
    map_slots((7, 3, 5, 6))
    for r, k1, k2 in near_dims:
        add_half(r, k1 | k2, 0)
        send_half(r, k1 | k2, (r + 1) % 3, 1)
    map_slots((1, 2, 4))
    for r, k1, k2 in near_dims:
        add_half(r, k1, 0)
        send_half(r, k1, (r + 1) % 3, 1)
    map_slots((0,))
    row_exchange(ITERS, jnp.transpose(final[...])[0:16])
    for r, k1, k2 in near_dims:
        add_half(r, k2, 0)
        add_half(r, k2, 1)
        send_half(r, k2, (r + 2) % 3, 2)
    sums[pl.ds(0, 16), :] = row_result(ITERS)
    own_a = x % 2 + 2 * (y % 2) + 4 * (z % 2)
    near_rows = sums[pl.ds(pl.multiple_of((own_a // 4) * 8, 8), 8), :]
    mine = near_rows[0:2]
    for k in range(1, 4):
        mine = jnp.where(own_a % 4 == k, near_rows[2 * k : 2 * k + 2], mine)
    column = jnp.transpose(jnp.broadcast_to(1.0 / mine[:, None, :], (2, 128, 256)).reshape(256, 256))
    for r in range(3):
        for order in range(3):
            add_half(r, 0, order)
    for i in range(2):
        inverse = column[:, i * 128 : i * 128 + 1]
        mapped_ref[i] = (numer[i] * inverse).astype(bf16)
    landed_at(abuf.at[pl.ds(2, 14)], out_sem.at[0])
    landed_at(bbuf.at[pl.ds(1, 7), pl.ds(0, 2)], out_sem.at[0])
    landed_at(bbuf.at[pl.ds(1, 7), pl.ds(0, 2)], out_sem.at[1])
    landed_at(ship.at[pl.ds(2, 14)], out_sem.at[2])
    for cat in range(2):
        landed_at(norm_bufs[cat].at[pl.ds(1, 7)], norm_sem.at[0, cat])
    for phase in range(ITERS + 1):
        landed_at(row_recv.at[phase, pl.ds(1, 7)], row_sem.at[0, phase])
    for phase in range(ITERS):
        landed_at(col_recv.at[phase, pl.ds(1, 15)], col_sem.at[0, phase])
        landed_at(scales.at[phase, pl.ds(0, 16)], half_swap.at[0, phase])


def transport(T, cid, own, partners, counts):
    vmem = pl.BlockSpec(memory_space=pltpu.VMEM)
    dma = pltpu.SemaphoreType.DMA
    return pl.pallas_call(
        functools.partial(kernel, T),
        out_shape=(
            jax.ShapeDtypeStruct((2, 256, 256), bf16),
            jax.ShapeDtypeStruct((4, 256), f32),
            jax.ShapeDtypeStruct((1, 1), f32),
        ),
        in_specs=[pl.BlockSpec(memory_space=pltpu.HBM)] * 3,
        out_specs=(vmem, vmem, pl.BlockSpec(memory_space=pltpu.SMEM)),
        scratch_shapes=[
            pltpu.VMEM((16, T), bf16),
            pltpu.VMEM((T, 16), bf16),
            pltpu.VMEM((32, T), bf16),
            pltpu.VMEM((T, 32), bf16),
            pltpu.VMEM((128, 32), bf16),
            pltpu.VMEM((32, 256), jnp.int32),
            pltpu.VMEM((1, 256), jnp.int32),
            pltpu.VMEM((40, 128), jnp.int32),
            pltpu.SMEM((40, 128), jnp.int32),
            pltpu.VMEM((256, 128), f32),
            pltpu.VMEM((8, 8, 256), f32),
            pltpu.VMEM((8, 8, 256), f32),
            dma((2, 2)),
            pltpu.VMEM((16, 256, 256), bf16),
            pltpu.VMEM((8, 4, 256, 256), bf16),
            pltpu.VMEM((T, 256, 256), bf16),
            pltpu.VMEM((16, 256, 1), f32),
            pltpu.VMEM((32, 8, 256), f32),
            pltpu.VMEM((T, 256), f32),
            pltpu.VMEM((256, T), f32),
            pltpu.VMEM((T, 256), f32),
            pltpu.VMEM((128, 256), f32),
            pltpu.VMEM((4, 16, 256), bf16),
            pltpu.VMEM((3, 32, 256), bf16),
            pltpu.VMEM((4, 8, 16, 256), bf16),
            pltpu.VMEM((3, 16, 16, 256), bf16),
            pltpu.VMEM((3, 32, 256), f32),
            dma((2, 3)),
            pltpu.VMEM((16, 256, 256), f32),
            pltpu.VMEM((16, 256, 256), bf16),
            pltpu.VMEM((3, 16, 256, 256), bf16),
            dma((3,)),
            dma((2,)),
            dma((2, 3, 8)),
            dma((8,)),
            dma((3,)),
            dma((2, 4)),
            dma((2, 3)),
            dma((3, 3, 8)),
            dma((1,)),
        ],
        compiler_params=pltpu.CompilerParams(
            collective_id=cid, has_side_effects=True, vmem_limit_bytes=60 << 20
        ),
        name=f"transport_{T}",
    )(own, partners, counts)


def shards(embeds, partners, counts):
    args = embeds.reshape(4, 256, 256), partners.T, counts.reshape(1, 256)
    mapped, scale, most = transport(64, 0, *args)
    mapped, scale = lax.cond(
        most.reshape(()) <= 64.0,
        lambda mapped, scale, *args: (mapped, scale),
        lambda mapped, scale, *args: transport(128, 1, *args)[:2],
        mapped,
        scale,
        *args,
    )
    return mapped.reshape(1, 1, 2, 256, 256), scale


def solution(mesh):
    in_specs = (P("side", ("grp", "dev"), None, None), P(), P())
    out_specs = (P(("grp", "dev"), "side", None, None, None), P(("grp", "dev"), None))
    return jax.shard_map(shards, mesh=mesh, in_specs=in_specs, out_specs=out_specs, check_vma=False)
```

```python
import functools
import math

import jax
import jax.numpy as jnp
from jax import lax
from jax.experimental import pallas as pl
from jax.experimental.pallas import tpu as pltpu
from jax.sharding import PartitionSpec as P

ITERS = 3
TURN = 64
FAR_FIRST = (7, 3, 5, 6, 1, 2, 4)
GAIN = 20.0 * math.log2(math.e)
MESH = pl.DeviceIdType.MESH
NT = (((1,), (1,)), ((), ()))
f32 = jnp.float32
bf16 = jnp.bfloat16
PIECES = ((0, 96), (96, 80), (176, 80))


def place():
    d = lax.axis_index("dev")
    return lax.axis_index("side"), (d // 4, lax.axis_index("grp"), d % 4)


def flip_a(p):
    return p + 1 - 2 * (p % 2)


def flip_b(p):
    return 3 - p


def member(at, flip, bits, core):
    x, y, z = [flip(p) if (bits >> k) & 1 else p for k, p in enumerate(at)]
    return (core, y, x * 4 + z)


def dot(a, b):
    return jnp.dot(a, b, preferred_element_type=f32)


def dot_nt(a, b):
    return lax.dot_general(a, b, NT, preferred_element_type=f32)


def kernel(
    T,
    x_ref,
    partners_ref,
    counts_ref,
    mapped_ref,
    scale_ref,
    most_ref,
    counts_out,
    oa,
    oat,
    ob,
    obt,
    obd,
    partners,
    counts,
    index,
    idx,
    final,
    norms_a,
    norms_b,
    norm_sem,
    abuf,
    bbuf,
    tiles,
    row_norm,
    col_norm,
    sums,
    columns,
    spread,
    dense,
    row_send,
    col_send,
    row_recv,
    col_recv,
    scales,
    numer,
    ship,
    landed,
    own_sem,
    sib_sem,
    gather_sem,
    relay_sem,
    out_sem,
    row_sem,
    col_sem,
    half_sem,
    index_sem,
):
    core, at = place()
    other = 1 - core
    sibling = member(at, flip_a, 0, other)
    flips = (flip_a, flip_b)
    norm_bufs = (norms_a, norms_b)
    bufs = (abuf, bbuf)

    barrier = pltpu.get_barrier_semaphore()
    greeted = [sibling]
    for m in range(1, 8):
        greeted += [member(at, flip_a, m, core), member(at, flip_b, m, core), member(at, flip_b, m, other)]
        if m in (1, 2, 4):
            greeted.append(member(at, flip_a, m, other))
    for peer in greeted:
        pl.semaphore_signal(barrier, inc=1, device_id=peer, device_id_type=MESH)
    fetches = [
        pltpu.make_async_copy(partners_ref, partners, own_sem.at[1]),
        pltpu.make_async_copy(counts_ref, counts, own_sem.at[2]),
    ]
    for fetch in fetches:
        fetch.start()
    pl.semaphore_wait(barrier, len(greeted))

    def remote(src, dst, send, recv, peer):
        return pltpu.make_async_remote_copy(
            src_ref=src, dst_ref=dst, send_sem=send, recv_sem=recv, device_id=peer, device_id_type=MESH
        )

    def unit(cat, slot, piece):
        start, size = PIECES[piece]
        if cat == 0:
            return abuf.at[pl.ds(slot * 2, 2), pl.ds(start, size)]
        return bbuf.at[slot, pl.ds(core * 2, 2), pl.ds(start, size)]

    def send_unit(cat, dim, piece, slot):
        there = slot ^ (1 << dim)
        remote(
            unit(cat, slot, piece),
            unit(cat, there, piece),
            out_sem.at[0],
            gather_sem.at[cat, piece, there],
            member(at, flips[cat], 1 << dim, core),
        ).start()

    def send_own(cat):
        for step in range(3):
            for dim in range(3):
                piece = (dim - step) % 3
                start, size = PIECES[piece]
                rows, there = pl.ds(start, size), 1 << dim
                for half in range(2):
                    two = pl.ds(half * 2, 2)
                    remote(
                        x_ref.at[two, rows],
                        abuf.at[pl.ds(there * 2, 2), rows] if cat == 0 else bbuf.at[there, two, rows],
                        out_sem.at[0],
                        gather_sem.at[cat, piece, there],
                        member(at, flips[cat], there, half),
                    ).start()

    own_a_half, own_b = abuf.at[pl.ds(0, 2)], bbuf.at[0]

    def landed_at(ref, sem):
        pltpu.make_async_copy(ref, ref, sem).wait()

    @pl.when(core == 0)
    def _():
        give = remote(x_ref.at[pl.ds(2, 2)], own_a_half, sib_sem.at[0], sib_sem.at[1], sibling)
        give.start()
        mine = pltpu.make_async_copy(x_ref.at[pl.ds(0, 2)], own_a_half, own_sem.at[0])
        mine.start()
        send_own(0)
        mine.wait()
        give.wait_send()
        landed_at(own_b, sib_sem.at[1])

    @pl.when(core == 1)
    def _():
        give = remote(x_ref, own_b, sib_sem.at[0], sib_sem.at[1], sibling)
        give.start()
        mine = pltpu.make_async_copy(x_ref, own_b, own_sem.at[0])
        mine.start()
        send_own(1)
        mine.wait()
        give.wait_send()
        landed_at(own_a_half, sib_sem.at[1])


    def arrived(cat, piece, slot):
        here = unit(cat, slot, piece)
        pltpu.make_async_copy(here, here, gather_sem.at[cat, piece, slot]).wait()
        if cat == 1:
            remote(here, here, out_sem.at[1], relay_sem.at[slot], sibling).start()

    def iota(shape, dim):
        return lax.broadcasted_iota(jnp.int32, shape, dim)

    diagonal = iota((128, 128), 0) == iota((128, 128), 1)

    def send_norms():
        def inverse_norm(block, scale):
            halves = []
            for h in range(2):
                y = block[h * 128 : h * 128 + 128]
                total = jnp.sum(jnp.where(diagonal, dot_nt(y, y), 0.0), axis=0, keepdims=True)
                halves.append(lax.rsqrt(total * (1.0 / 256.0) + 1e-06) * scale)
            return jnp.concatenate(halves, axis=1)

        for i in range(2):
            norm_bufs[0][0, i : i + 1] = inverse_norm(abuf[i], GAIN / 16.0)
        for i in range(4):
            norm_bufs[1][0, i : i + 1] = inverse_norm(bbuf[0, i], 1.0 / 16.0)
        for cat in range(2):
            for m in range(1, 8):
                remote(
                    norm_bufs[cat].at[0], norm_bufs[cat].at[m], norm_sem.at[0, cat], norm_sem.at[1, cat],
                    member(at, flips[cat], m, core),
                ).start()

    def take_norms():
        for cat in range(2):
            landed_at(norm_bufs[cat].at[pl.ds(1, 7)], norm_sem.at[1, cat])
        flipped_norms = jnp.transpose(
            jnp.concatenate([norm_bufs[0][m] for m in range(8)] + [jnp.zeros((64, 256), f32)], axis=0)
        )
        for a in range(16):
            lane = (a // 2) * 8 + a % 2
            row_norm[a] = flipped_norms[:, lane : lane + 1]
        for b in range(32):
            col_norm[b] = jnp.broadcast_to(norm_bufs[1][b // 4, b % 4 : b % 4 + 1], (8, 256))

    def bits_of(values, shifts):
        return [(values >> k) & 1 for k in shifts]

    def flipped(bits, by):
        return sum((b + f - 2 * b * f) * (1 << k) for k, (b, f) in enumerate(zip(bits, by)))

    def make_list():
        x, y, z = at
        own_low = [p % 2 for p in at]
        own_high = [p // 2 for p in at]
        for fetch in fetches:
            fetch.wait()
        named_all = partners[...]
        limit_row = counts[...]
        counts_out[...] = limit_row
        r = iota((16, 256), 0)
        cx, cy, cz = [flipped([b], [p % 2]) + 2 * (p // 2) for b, p in zip(bits_of(r, (1, 2, 3)), at)]
        chosen = iota((16, 256), 1) == (cy * 16 + cx * 4 + cz) * 4 + 2 * core + (r & 1)
        named = dot_nt(chosen.astype(f32).astype(bf16), named_all.astype(f32).astype(bf16)).astype(jnp.int32)
        limit = jnp.sum(jnp.where(chosen, jnp.broadcast_to(limit_row, (16, 256)), 0).astype(f32), axis=1, keepdims=True)
        slot_at = iota((16, 32), 1).astype(f32)

        def coords(entry):
            owner = entry >> 2
            return (owner >> 2) & 3, owner >> 4, owner & 3

        parts = coords(named)
        active = slot_at < limit
        for p, q in zip(parts, at):
            active &= (p == q) | (p == 3 - q)
        jb = sum((p >> 1) * (1 << k) for k, p in enumerate(parts))
        pick = (named & 3) + 1
        lane = iota((16, 128), 1)
        bp = jnp.zeros((16, 128), f32)
        for k in range(8):
            best = jnp.max(jnp.where(active & (jb == k), pick, 0).astype(f32), axis=1, keepdims=True)
            bp = jnp.where(lane == k, best, bp)
        used = jnp.where(bp > 0, 1.0, 0.0).astype(bf16)
        i128, j128 = iota((128, 128), 0), iota((128, 128), 1)

        def mask(m):
            return jnp.where(m, 1.0, 0.0).astype(bf16)

        in_row = dot(used, mask(i128 < j128))
        of_row = dot(used, mask(i128 < 128))
        above = dot(mask(iota((16, 16), 1) < iota((16, 16), 0)), of_row.astype(bf16))
        pos = above + in_row
        k3 = bits_of(lane, (0, 1, 2))
        b_rel = flipped(k3, own_high) * 4 + jnp.maximum(bp.astype(jnp.int32) - 1, 0)
        index[pl.ds(0, 16), :] = jnp.where(bp > 0, jnp.minimum(pos, T - 1.0), 0.0).astype(jnp.int32)
        index[pl.ds(16, 16), :] = jnp.where(lane < 8, b_rel, 0)

        spread_out = mask(i128 == (j128 & 7))
        own_lane = (lane >> 3) == iota((16, 128), 0)

        def flat(values):
            return jnp.sum(jnp.where(own_lane, dot(values.astype(bf16), spread_out), 0.0), axis=0, keepdims=True)

        bp_row, pos_row = flat(bp), flat(pos)
        hot = mask((iota((T, 128), 0).astype(f32) == pos_row) & (bp_row > 0))
        e = iota((8, 128), 1)
        pick_row = jnp.maximum(jnp.broadcast_to(bp_row, (8, 128)).astype(jnp.int32) - 1, 0)
        b_e = flipped(bits_of(e, (0, 1, 2)), own_high) * 4 + pick_row
        values = jnp.where(iota((8, 128), 0) == 0, e >> 3, b_e).astype(f32).astype(bf16)
        index[pl.ds(32, 8), pl.ds(0, T)] = dot_nt(values, hot).astype(jnp.int32)
        fetch = pltpu.make_async_copy(index, idx, index_sem.at[0])
        fetch.start()
        e16, e32 = iota((16, 128), 1), iota((32, 128), 1)
        a_abs = flipped(bits_of(e16, (4, 5, 6)), own_low) * 2 + ((e16 >> 3) & 1)
        a_hot = mask(iota((16, 128), 0) == a_abs)
        b_abs = (e32 & 7) * 4 + jnp.broadcast_to(bp_row, (32, 128)).astype(jnp.int32) - 1
        b_hot = mask((iota((32, 128), 0) == b_abs) & (bp_row > 0))
        oa[...] = dot_nt(a_hot, hot).astype(bf16)
        oat[...] = dot_nt(hot, a_hot).astype(bf16)
        ob[...] = dot_nt(b_hot, hot).astype(bf16)
        obt[...] = dot_nt(hot, b_hot).astype(bf16)
        obd[...] = dot_nt(mask(i128 == j128), b_hot).astype(bf16)

        active = iota((32, 256), 0) < limit_row
        kind = sum((((p + 1) >> 1) & 1) * (1 << k) for k, p in enumerate(coords(named_all)))
        g, row = iota((16, 256), 0), iota((16, 256), 1)
        group = ((row >> 7) & 1) * 8 + ((row >> 5) & 1) * 4 + ((row >> 3) & 1) * 2 + ((row >> 1) & 1)
        members = mask(g == group)
        most = jnp.zeros((16, 1), f32)
        for k in range(8):
            most = jnp.maximum(
                most, jnp.sum(dot_nt(members, mask(active & (kind == k))), axis=1, keepdims=True)
            )
        most_ref[0, 0] = jnp.max(most)
        fetch.wait()

    def received(steps):
        for r in range(3):
            slot = steps(1 << r, 1 << ((r + 1) % 3), 1 << ((r + 2) % 3))
            for cat in range(2):
                arrived(cat, r, slot)
                yield cat, r, slot

    make_list()
    send_norms()
    for cat, r, slot in received(lambda k0, k1, k2: k0):
        send_unit(cat, (r + 1) % 3, r, slot)
    for r in range(3):
        for cat in range(2):
            send_unit(cat, (r + 2) % 3, r, 1 << r)
    for cat, r, slot in received(lambda k0, k1, k2: k1):
        send_unit(cat, (r + 2) % 3, r, slot)
    for cat, r, slot in received(lambda k0, k1, k2: k0 | k1):
        send_unit(cat, (r + 2) % 3, r, slot)
    for _ in received(lambda k0, k1, k2: k2):
        pass
    take_norms()
    for _ in received(lambda k0, k1, k2: k2 | k0):
        pass
    for _ in received(lambda k0, k1, k2: k2 | k1):
        pass
    for _ in received(lambda k0, k1, k2: 7):
        pass
    for slot in range(1, 8):
        landed_at(bbuf.at[slot, pl.ds(other * 2, 2)], relay_sem.at[slot])

    def build(i, c):
        for u in range(TURN):
            t = i * TURN + u
            a, b = jnp.clip(idx[32, t], 0, 15), jnp.clip(idx[33, t], 0, 31)
            scores = dot_nt(abuf[a], bbuf[b // 4, b % 4])
            tiles[t] = jnp.exp2(scores * row_norm[a] * col_norm[b][0:1] - GAIN).astype(bf16)
        return c

    lax.fori_loop(0, T // TURN, build, 0)

    row_id = iota((8, 256), 0)
    lane_id = iota((256, T), 1)

    def row_sweep():
        def body(i, c):
            beside = columns[...]
            for g in range(TURN // 8):
                base = i * TURN + g * 8
                rows = pl.ds(pl.multiple_of(base, 8), 8)
                left = spread[rows, :]
                left_bf = left.astype(bf16)
                total = jnp.zeros((8, 256), f32)
                for u in range(8):
                    tile = tiles[base + u]
                    if u % 2 == 0:
                        total = jnp.where(row_id == u, dot_nt(left_bf, tile), total)
                    else:
                        scaled = tile.astype(f32) * left[u : u + 1]
                        mass = jnp.sum(scaled[:, 0:128] + scaled[:, 128:256], axis=1, keepdims=True)
                        beside = jnp.where(lane_id == base + u, mass, beside)
                sums[rows, :] = total
            columns[...] = beside
            return c

        columns[...] = jnp.zeros((256, T), f32)
        lax.fori_loop(0, T // TURN, body, 0)
        return dot(oa[...], sums[...].astype(bf16)) + dot_nt(oa[...], columns[...].astype(bf16))

    def col_sweep():
        def body(i, c):
            for g in range(TURN // 8):
                base = i * TURN + g * 8
                rows = pl.ds(pl.multiple_of(base, 8), 8)
                left = spread[rows, :].astype(bf16)
                total = jnp.zeros((8, 256), f32)
                for u in range(8):
                    total = jnp.where(row_id == u, dot(left, tiles[base + u]), total)
                sums[rows, :] = total
            return c

        lax.fori_loop(0, T // TURN, body, 0)
        return dot(ob[...], sums[...].astype(bf16))

    def row_exchange(phase, partial):
        row_send[phase] = partial.astype(bf16)
        for m in FAR_FIRST:
            remote(
                row_send.at[phase], row_recv.at[phase, m], row_sem.at[0, phase], row_sem.at[1, phase],
                member(at, flip_a, m, core),
            ).start()

    def row_result(phase):
        landed_at(row_recv.at[phase, pl.ds(1, 7)], row_sem.at[1, phase])
        total = row_send[phase].astype(f32)
        for m in range(1, 8):
            total += row_recv[phase, m].astype(f32)
        return total

    def col_exchange(phase, partial):
        col_send[phase] = partial.astype(bf16)
        for m in FAR_FIRST + (0,):
            for far, to in ((1, other), (0, core)):
                if far + m:
                    remote(
                        col_send.at[phase], col_recv.at[phase, far * 8 + m], col_sem.at[0, phase],
                        col_sem.at[1, phase], member(at, flip_b, m, to),
                    ).start()
        landed_at(col_recv.at[phase, pl.ds(1, 15)], col_sem.at[1, phase])
        total = col_send[phase].astype(f32)
        for m in range(1, 16):
            total += col_recv[phase, m].astype(f32)
        return 1.0 / (1.0 + total)

    spread[...] = jnp.ones((T, 256), f32)
    for phase in range(ITERS):
        row_exchange(phase, row_sweep())
        scale_a = 1.0 / row_result(phase)
        spread[...] = dot(oat[...], scale_a.astype(bf16))
        scale_b = col_exchange(phase, col_sweep())
        spread[...] = dot(obt[...], scale_b.astype(bf16))
    x, y, z = at
    member_b = x // 2 + 2 * (y // 2) + 4 * (z // 2)
    scales[...] = scale_b
    near_rows = scales[pl.ds(pl.multiple_of((member_b // 2) * 8, 8), 8), :]
    scale_ref[...] = jnp.where(member_b % 2 == 0, near_rows[0:4], near_rows[4:8])
    dense[...] = dot(obd[...], scale_b.astype(bf16))

    def partial(slot):
        def body(i, c):
            total, mass = None, None
            a = slot * 2 + i
            rows = dense[pl.ds(pl.multiple_of(a * 8, 8), 8), :]
            for d in range(8):
                weights = tiles[jnp.clip(idx[a, d], 0, T - 1)].astype(f32) * rows[d : d + 1]
                b = jnp.clip(idx[16 + a, d], 0, 31)
                part = dot(weights.astype(bf16), bbuf[b // 4, b % 4])
                half = weights[:, 0:128] + weights[:, 128:256]
                total = part if total is None else total + part
                mass = half if mass is None else mass + half
            numer[a] = total
            column = jnp.sum(mass, axis=1, keepdims=True)
            a_at = flipped([(slot >> k) & 1 for k in range(3)], [p % 2 for p in at]) * 2 + i
            final[...] = jnp.where(iota((256, 128), 1) == a_at, column, final[...])
            return c

        lax.fori_loop(0, 2, body, 0)

    final[...] = jnp.zeros((256, 128), f32)

    def send_half(piece, slot, dim, order):
        start, size = PIECES[piece]
        two, rows = pl.ds(slot * 2, 2), pl.ds(start, size)
        ship[two, rows, :] = numer[two, rows, :].astype(bf16)
        there = slot ^ (1 << dim)
        remote(
            ship.at[two, rows], landed.at[order, pl.ds(there * 2, 2), rows], out_sem.at[2], half_sem.at[order, piece, there],
            member(at, flip_a, 1 << dim, core),
        ).start()

    def add_half(piece, slot, order):
        start, size = PIECES[piece]
        two, rows = pl.ds(slot * 2, 2), pl.ds(start, size)
        here = landed.at[order, two, rows]
        pltpu.make_async_copy(here, here, half_sem.at[order, piece, slot]).wait()
        numer[two, rows, :] = numer[two, rows, :] + landed[order, two, rows, :].astype(f32)

    def map_slots(slots):
        for slot in slots:
            partial(slot)
            for r in range(3):
                if (slot >> r) & 1:
                    send_half(r, slot, r, 0)

    near_dims = [(r, 1 << ((r + 1) % 3), 1 << ((r + 2) % 3)) for r in range(3)]
    map_slots((7, 3, 5, 6))
    for r, k1, k2 in near_dims:
        add_half(r, k1 | k2, 0)
        send_half(r, k1 | k2, (r + 1) % 3, 1)
    map_slots((1, 2, 4))
    for r, k1, k2 in near_dims:
        add_half(r, k1, 0)
        send_half(r, k1, (r + 1) % 3, 1)
    map_slots((0,))
    row_exchange(ITERS, jnp.transpose(final[...])[0:16])
    for r, k1, k2 in near_dims:
        add_half(r, k2, 0)
        add_half(r, k2, 1)
        send_half(r, k2, (r + 2) % 3, 2)
    sums[pl.ds(0, 16), :] = row_result(ITERS)
    own_a = x % 2 + 2 * (y % 2) + 4 * (z % 2)
    near_rows = sums[pl.ds(pl.multiple_of((own_a // 4) * 8, 8), 8), :]
    mine = near_rows[0:2]
    for k in range(1, 4):
        mine = jnp.where(own_a % 4 == k, near_rows[2 * k : 2 * k + 2], mine)
    column = jnp.transpose(jnp.broadcast_to(1.0 / mine[:, None, :], (2, 128, 256)).reshape(256, 256))
    for r in range(3):
        for order in range(3):
            add_half(r, 0, order)
    for i in range(2):
        inverse = column[:, i * 128 : i * 128 + 1]
        mapped_ref[i] = (numer[i] * inverse).astype(bf16)
    landed_at(abuf.at[pl.ds(2, 14)], out_sem.at[0])
    landed_at(bbuf.at[pl.ds(1, 7), pl.ds(0, 2)], out_sem.at[0])
    landed_at(bbuf.at[pl.ds(1, 7), pl.ds(0, 2)], out_sem.at[1])
    landed_at(ship.at[pl.ds(2, 14)], out_sem.at[2])
    for cat in range(2):
        landed_at(norm_bufs[cat].at[pl.ds(1, 7)], norm_sem.at[0, cat])
    for phase in range(ITERS + 1):
        landed_at(row_recv.at[phase, pl.ds(1, 7)], row_sem.at[0, phase])
    for phase in range(ITERS):
        landed_at(col_recv.at[phase, pl.ds(1, 15)], col_sem.at[0, phase])


def transport(T, cid, own, partners, counts):
    vmem = pl.BlockSpec(memory_space=pltpu.VMEM)
    dma = pltpu.SemaphoreType.DMA
    return pl.pallas_call(
        functools.partial(kernel, T),
        out_shape=(
            jax.ShapeDtypeStruct((2, 256, 256), bf16),
            jax.ShapeDtypeStruct((4, 256), f32),
            jax.ShapeDtypeStruct((1, 1), f32),
            jax.ShapeDtypeStruct((1, 256), jnp.int32),
        ),
        in_specs=[pl.BlockSpec(memory_space=pltpu.HBM)] * 3,
        out_specs=(vmem, vmem, pl.BlockSpec(memory_space=pltpu.SMEM), vmem),
        scratch_shapes=[
            pltpu.VMEM((16, T), bf16),
            pltpu.VMEM((T, 16), bf16),
            pltpu.VMEM((32, T), bf16),
            pltpu.VMEM((T, 32), bf16),
            pltpu.VMEM((128, 32), bf16),
            pltpu.VMEM((32, 256), jnp.int32),
            pltpu.VMEM((1, 256), jnp.int32),
            pltpu.VMEM((40, 128), jnp.int32),
            pltpu.SMEM((40, 128), jnp.int32),
            pltpu.VMEM((256, 128), f32),
            pltpu.VMEM((8, 8, 256), f32),
            pltpu.VMEM((8, 8, 256), f32),
            dma((2, 2)),
            pltpu.VMEM((16, 256, 256), bf16),
            pltpu.VMEM((8, 4, 256, 256), bf16),
            pltpu.VMEM((T, 256, 256), bf16),
            pltpu.VMEM((16, 256, 1), f32),
            pltpu.VMEM((32, 8, 256), f32),
            pltpu.VMEM((T, 256), f32),
            pltpu.VMEM((256, T), f32),
            pltpu.VMEM((T, 256), f32),
            pltpu.VMEM((128, 256), f32),
            pltpu.VMEM((4, 16, 256), bf16),
            pltpu.VMEM((3, 32, 256), bf16),
            pltpu.VMEM((4, 8, 16, 256), bf16),
            pltpu.VMEM((3, 16, 32, 256), bf16),
            pltpu.VMEM((32, 256), f32),
            pltpu.VMEM((16, 256, 256), f32),
            pltpu.VMEM((16, 256, 256), bf16),
            pltpu.VMEM((3, 16, 256, 256), bf16),
            dma((3,)),
            dma((2,)),
            dma((2, 3, 8)),
            dma((8,)),
            dma((3,)),
            dma((2, 4)),
            dma((2, 3)),
            dma((3, 3, 8)),
            dma((1,)),
        ],
        compiler_params=pltpu.CompilerParams(
            collective_id=cid, has_side_effects=True, vmem_limit_bytes=60 << 20
        ),
        name=f"transport_{T}",
    )(own, partners, counts)


def shards(embeds, partners, counts):
    args = embeds.reshape(4, 256, 256), partners.T, counts.reshape(1, 256)
    mapped, scale, most, limits = transport(64, 0, *args)
    mapped, scale = lax.cond(
        most.reshape(()) <= 64.0,
        lambda mapped, scale, *args: (mapped, scale),
        lambda mapped, scale, *args: transport(128, 1, *args)[:2],
        mapped,
        scale,
        *args[:2],
        limits,
    )
    return mapped.reshape(1, 1, 2, 256, 256), scale


def solution(mesh):
    in_specs = (P("side", ("grp", "dev"), None, None), P(), P())
    out_specs = (P(("grp", "dev"), "side", None, None, None), P(("grp", "dev"), None))
    return jax.shard_map(shards, mesh=mesh, in_specs=in_specs, out_specs=out_specs, check_vma=False)
```

```python
import functools
import math

import jax
import jax.numpy as jnp
from jax import lax
from jax.experimental import pallas as pl
from jax.experimental.pallas import tpu as pltpu
from jax.sharding import PartitionSpec as P

ITERS = 3
TURN = 64
FAR_FIRST = (7, 3, 5, 6, 1, 2, 4)
GAIN = 20.0 * math.log2(math.e)
MESH = pl.DeviceIdType.MESH
NT = (((1,), (1,)), ((), ()))
f32 = jnp.float32
bf16 = jnp.bfloat16
PIECES = ((0, 96), (96, 80), (176, 80))


def place():
    d = lax.axis_index("dev")
    return lax.axis_index("side"), (d // 4, lax.axis_index("grp"), d % 4)


def flip_a(p):
    return p + 1 - 2 * (p % 2)


def flip_b(p):
    return 3 - p


def member(at, flip, bits, core):
    x, y, z = [flip(p) if (bits >> k) & 1 else p for k, p in enumerate(at)]
    return (core, y, x * 4 + z)


def dot(a, b):
    return jnp.dot(a, b, preferred_element_type=f32)


def dot_nt(a, b):
    return lax.dot_general(a, b, NT, preferred_element_type=f32)


def kernel(
    T,
    x_ref,
    partners_ref,
    counts_ref,
    mapped_ref,
    scale_ref,
    most_ref,
    counts_out,
    oa,
    oat,
    ob,
    obt,
    obd,
    partners,
    counts,
    index,
    idx,
    final,
    norms_a,
    norms_b,
    norm_sem,
    abuf,
    bbuf,
    tiles,
    row_norm,
    col_norm,
    sums,
    columns,
    spread,
    dense,
    row_send,
    col_send,
    row_recv,
    col_recv,
    scales,
    numer,
    ship,
    landed,
    own_sem,
    sib_sem,
    gather_sem,
    relay_sem,
    out_sem,
    row_sem,
    col_sem,
    half_sem,
    index_sem,
    ready,
):
    core, at = place()
    other = 1 - core
    sibling = member(at, flip_a, 0, other)
    flips = (flip_a, flip_b)
    norm_bufs = (norms_a, norms_b)
    bufs = (abuf, bbuf)

    barrier = pltpu.get_barrier_semaphore()
    greeted = []
    for m in (1, 2, 4):
        greeted += [member(at, flip, m, to) for flip in (flip_a, flip_b) for to in (other, core)]
    greeted.append(sibling)
    for peer in greeted:
        pl.semaphore_signal(barrier, inc=1, device_id=peer, device_id_type=MESH)
    fetches = [
        pltpu.make_async_copy(partners_ref, partners, own_sem.at[1]),
        pltpu.make_async_copy(counts_ref, counts, own_sem.at[2]),
    ]
    for fetch in fetches:
        fetch.start()
    pl.semaphore_wait(barrier, len(greeted))

    def greet(level):
        for peer in greeted:
            pl.semaphore_signal(ready.at[level], inc=1, device_id=peer, device_id_type=MESH)

    def greeted_by_all(level):
        pl.semaphore_wait(ready.at[level], len(greeted))

    def remote(src, dst, send, recv, peer):
        return pltpu.make_async_remote_copy(
            src_ref=src, dst_ref=dst, send_sem=send, recv_sem=recv, device_id=peer, device_id_type=MESH
        )

    def unit(cat, slot, piece):
        start, size = PIECES[piece]
        if cat == 0:
            return abuf.at[pl.ds(slot * 2, 2), pl.ds(start, size)]
        return bbuf.at[slot, pl.ds(core * 2, 2), pl.ds(start, size)]

    def send_unit(cat, dim, piece, slot):
        there = slot ^ (1 << dim)
        remote(
            unit(cat, slot, piece),
            unit(cat, there, piece),
            out_sem.at[0],
            gather_sem.at[cat, piece, there],
            member(at, flips[cat], 1 << dim, core),
        ).start()

    def send_own(cat):
        for step in range(3):
            for dim in range(3):
                piece = (dim - step) % 3
                start, size = PIECES[piece]
                rows, there = pl.ds(start, size), 1 << dim
                for half in range(2):
                    two = pl.ds(half * 2, 2)
                    remote(
                        x_ref.at[two, rows],
                        abuf.at[pl.ds(there * 2, 2), rows] if cat == 0 else bbuf.at[there, two, rows],
                        out_sem.at[0],
                        gather_sem.at[cat, piece, there],
                        member(at, flips[cat], there, half),
                    ).start()

    own_a_half, own_b = abuf.at[pl.ds(0, 2)], bbuf.at[0]

    def landed_at(ref, sem):
        pltpu.make_async_copy(ref, ref, sem).wait()

    @pl.when(core == 0)
    def _():
        give = remote(x_ref.at[pl.ds(2, 2)], own_a_half, sib_sem.at[0], sib_sem.at[1], sibling)
        give.start()
        mine = pltpu.make_async_copy(x_ref.at[pl.ds(0, 2)], own_a_half, own_sem.at[0])
        mine.start()
        send_own(0)
        greet(0)
        mine.wait()
        give.wait_send()
        landed_at(own_b, sib_sem.at[1])

    @pl.when(core == 1)
    def _():
        give = remote(x_ref, own_b, sib_sem.at[0], sib_sem.at[1], sibling)
        give.start()
        mine = pltpu.make_async_copy(x_ref, own_b, own_sem.at[0])
        mine.start()
        send_own(1)
        greet(0)
        mine.wait()
        give.wait_send()
        landed_at(own_a_half, sib_sem.at[1])


    def arrived(cat, piece, slot):
        here = unit(cat, slot, piece)
        pltpu.make_async_copy(here, here, gather_sem.at[cat, piece, slot]).wait()
        if cat == 1:
            remote(here, here, out_sem.at[1], relay_sem.at[slot], sibling).start()

    def iota(shape, dim):
        return lax.broadcasted_iota(jnp.int32, shape, dim)

    diagonal = iota((128, 128), 0) == iota((128, 128), 1)

    def own_norms():
        def inverse_norm(block, scale):
            halves = []
            for h in range(2):
                y = block[h * 128 : h * 128 + 128]
                total = jnp.sum(jnp.where(diagonal, dot_nt(y, y), 0.0), axis=0, keepdims=True)
                halves.append(lax.rsqrt(total * (1.0 / 256.0) + 1e-06) * scale)
            return jnp.concatenate(halves, axis=1)

        for i in range(2):
            norm_bufs[0][0, i : i + 1] = inverse_norm(abuf[i], GAIN / 16.0)
        for i in range(4):
            norm_bufs[1][0, i : i + 1] = inverse_norm(bbuf[0, i], 1.0 / 16.0)

    def share_norms():
        for cat in range(2):
            for m in range(1, 8):
                remote(
                    norm_bufs[cat].at[0], norm_bufs[cat].at[m], norm_sem.at[0, cat], norm_sem.at[1, cat],
                    member(at, flips[cat], m, core),
                ).start()

    def take_norms():
        for cat in range(2):
            landed_at(norm_bufs[cat].at[pl.ds(1, 7)], norm_sem.at[1, cat])
        flipped_norms = jnp.transpose(
            jnp.concatenate([norm_bufs[0][m] for m in range(8)] + [jnp.zeros((64, 256), f32)], axis=0)
        )
        for a in range(16):
            lane = (a // 2) * 8 + a % 2
            row_norm[a] = flipped_norms[:, lane : lane + 1]
        for b in range(32):
            col_norm[b] = jnp.broadcast_to(norm_bufs[1][b // 4, b % 4 : b % 4 + 1], (8, 256))

    def bits_of(values, shifts):
        return [(values >> k) & 1 for k in shifts]

    def flipped(bits, by):
        return sum((b + f - 2 * b * f) * (1 << k) for k, (b, f) in enumerate(zip(bits, by)))

    def make_list():
        x, y, z = at
        own_low = [p % 2 for p in at]
        own_high = [p // 2 for p in at]
        for fetch in fetches:
            fetch.wait()
        named_all = partners[...]
        limit_row = counts[...]
        counts_out[...] = limit_row
        r = iota((16, 256), 0)
        cx, cy, cz = [flipped([b], [p % 2]) + 2 * (p // 2) for b, p in zip(bits_of(r, (1, 2, 3)), at)]
        chosen = iota((16, 256), 1) == (cy * 16 + cx * 4 + cz) * 4 + 2 * core + (r & 1)
        named = dot_nt(chosen.astype(f32).astype(bf16), named_all.astype(f32).astype(bf16)).astype(jnp.int32)
        limit = jnp.sum(jnp.where(chosen, jnp.broadcast_to(limit_row, (16, 256)), 0).astype(f32), axis=1, keepdims=True)
        slot_at = iota((16, 32), 1).astype(f32)

        def coords(entry):
            owner = entry >> 2
            return (owner >> 2) & 3, owner >> 4, owner & 3

        parts = coords(named)
        active = slot_at < limit
        for p, q in zip(parts, at):
            active &= (p == q) | (p == 3 - q)
        jb = sum((p >> 1) * (1 << k) for k, p in enumerate(parts))
        pick = (named & 3) + 1
        lane = iota((16, 128), 1)
        bp = jnp.zeros((16, 128), f32)
        for k in range(8):
            best = jnp.max(jnp.where(active & (jb == k), pick, 0).astype(f32), axis=1, keepdims=True)
            bp = jnp.where(lane == k, best, bp)
        used = jnp.where(bp > 0, 1.0, 0.0).astype(bf16)
        i128, j128 = iota((128, 128), 0), iota((128, 128), 1)

        def mask(m):
            return jnp.where(m, 1.0, 0.0).astype(bf16)

        in_row = dot(used, mask(i128 < j128))
        of_row = dot(used, mask(i128 < 128))
        above = dot(mask(iota((16, 16), 1) < iota((16, 16), 0)), of_row.astype(bf16))
        pos = above + in_row
        k3 = bits_of(lane, (0, 1, 2))
        b_rel = flipped(k3, own_high) * 4 + jnp.maximum(bp.astype(jnp.int32) - 1, 0)
        index[pl.ds(0, 16), :] = jnp.where(bp > 0, jnp.minimum(pos, T - 1.0), 0.0).astype(jnp.int32)
        index[pl.ds(16, 16), :] = jnp.where(lane < 8, b_rel, 0)

        spread_out = mask(i128 == (j128 & 7))
        own_lane = (lane >> 3) == iota((16, 128), 0)

        def flat(values):
            return jnp.sum(jnp.where(own_lane, dot(values.astype(bf16), spread_out), 0.0), axis=0, keepdims=True)

        bp_row, pos_row = flat(bp), flat(pos)
        hot = mask((iota((T, 128), 0).astype(f32) == pos_row) & (bp_row > 0))
        e = iota((8, 128), 1)
        pick_row = jnp.maximum(jnp.broadcast_to(bp_row, (8, 128)).astype(jnp.int32) - 1, 0)
        b_e = flipped(bits_of(e, (0, 1, 2)), own_high) * 4 + pick_row
        values = jnp.where(iota((8, 128), 0) == 0, e >> 3, b_e).astype(f32).astype(bf16)
        index[pl.ds(32, 8), pl.ds(0, T)] = dot_nt(values, hot).astype(jnp.int32)
        fetch = pltpu.make_async_copy(index, idx, index_sem.at[0])
        fetch.start()
        e16, e32 = iota((16, 128), 1), iota((32, 128), 1)
        a_abs = flipped(bits_of(e16, (4, 5, 6)), own_low) * 2 + ((e16 >> 3) & 1)
        a_hot = mask(iota((16, 128), 0) == a_abs)
        b_abs = (e32 & 7) * 4 + jnp.broadcast_to(bp_row, (32, 128)).astype(jnp.int32) - 1
        b_hot = mask((iota((32, 128), 0) == b_abs) & (bp_row > 0))
        oa[...] = dot_nt(a_hot, hot).astype(bf16)
        oat[...] = dot_nt(hot, a_hot).astype(bf16)
        ob[...] = dot_nt(b_hot, hot).astype(bf16)
        obt[...] = dot_nt(hot, b_hot).astype(bf16)
        obd[...] = dot_nt(mask(i128 == j128), b_hot).astype(bf16)

        active = iota((32, 256), 0) < limit_row
        kind = sum((((p + 1) >> 1) & 1) * (1 << k) for k, p in enumerate(coords(named_all)))
        g, row = iota((16, 256), 0), iota((16, 256), 1)
        group = ((row >> 7) & 1) * 8 + ((row >> 5) & 1) * 4 + ((row >> 3) & 1) * 2 + ((row >> 1) & 1)
        members = mask(g == group)
        most = jnp.zeros((16, 1), f32)
        for k in range(8):
            most = jnp.maximum(
                most, jnp.sum(dot_nt(members, mask(active & (kind == k))), axis=1, keepdims=True)
            )
        most_ref[0, 0] = jnp.max(most)
        fetch.wait()

    def received(steps):
        for r in range(3):
            slot = steps(1 << r, 1 << ((r + 1) % 3), 1 << ((r + 2) % 3))
            for cat in range(2):
                arrived(cat, r, slot)
                yield cat, r, slot

    make_list()
    greeted_by_all(0)
    greet(1)
    own_norms()
    for cat, r, slot in received(lambda k0, k1, k2: k0):
        send_unit(cat, (r + 1) % 3, r, slot)
    for r in range(3):
        for cat in range(2):
            send_unit(cat, (r + 2) % 3, r, 1 << r)
    greeted_by_all(1)
    share_norms()
    for cat, r, slot in received(lambda k0, k1, k2: k1):
        send_unit(cat, (r + 2) % 3, r, slot)
    for cat, r, slot in received(lambda k0, k1, k2: k0 | k1):
        send_unit(cat, (r + 2) % 3, r, slot)
    for cat in (1, 0):
        for rest in (0, 1, 2, 3):
            for r in range(3):
                near, far = (rest & 1) << r, (rest >> 1) << ((r + 1) % 3)
                arrived(cat, r, near | far | (1 << ((r + 2) % 3)))
    take_norms()
    for slot in range(1, 8):
        landed_at(bbuf.at[slot, pl.ds(other * 2, 2)], relay_sem.at[slot])

    def build(i, c):
        for u in range(TURN):
            t = i * TURN + u
            a, b = jnp.clip(idx[32, t], 0, 15), jnp.clip(idx[33, t], 0, 31)
            scores = dot_nt(abuf[a], bbuf[b // 4, b % 4])
            tiles[t] = jnp.exp2(scores * row_norm[a] * col_norm[b][0:1] - GAIN).astype(bf16)
        return c

    lax.fori_loop(0, T // TURN, build, 0)

    row_id = iota((8, 256), 0)
    lane_id = iota((256, T), 1)

    def row_sweep():
        def body(i, c):
            beside = columns[...]
            for g in range(TURN // 8):
                base = i * TURN + g * 8
                rows = pl.ds(pl.multiple_of(base, 8), 8)
                left = spread[rows, :]
                left_bf = left.astype(bf16)
                total = jnp.zeros((8, 256), f32)
                for u in range(8):
                    tile = tiles[base + u]
                    if u % 2 == 0:
                        total = jnp.where(row_id == u, dot_nt(left_bf, tile), total)
                    else:
                        scaled = tile.astype(f32) * left[u : u + 1]
                        mass = jnp.sum(scaled[:, 0:128] + scaled[:, 128:256], axis=1, keepdims=True)
                        beside = jnp.where(lane_id == base + u, mass, beside)
                sums[rows, :] = total
            columns[...] = beside
            return c

        columns[...] = jnp.zeros((256, T), f32)
        lax.fori_loop(0, T // TURN, body, 0)
        return dot(oa[...], sums[...].astype(bf16)) + dot_nt(oa[...], columns[...].astype(bf16))

    def col_sweep():
        def body(i, c):
            for g in range(TURN // 8):
                base = i * TURN + g * 8
                rows = pl.ds(pl.multiple_of(base, 8), 8)
                left = spread[rows, :].astype(bf16)
                total = jnp.zeros((8, 256), f32)
                for u in range(8):
                    total = jnp.where(row_id == u, dot(left, tiles[base + u]), total)
                sums[rows, :] = total
            return c

        lax.fori_loop(0, T // TURN, body, 0)
        return dot(ob[...], sums[...].astype(bf16))

    def row_exchange(phase, partial):
        row_send[phase] = partial.astype(bf16)
        for m in FAR_FIRST:
            remote(
                row_send.at[phase], row_recv.at[phase, m], row_sem.at[0, phase], row_sem.at[1, phase],
                member(at, flip_a, m, core),
            ).start()

    def row_result(phase):
        landed_at(row_recv.at[phase, pl.ds(1, 7)], row_sem.at[1, phase])
        total = row_send[phase].astype(f32)
        for m in range(1, 8):
            total += row_recv[phase, m].astype(f32)
        return total

    def col_exchange(phase, partial):
        col_send[phase] = partial.astype(bf16)
        for m in FAR_FIRST + (0,):
            for far, to in ((1, other), (0, core)):
                if far + m:
                    remote(
                        col_send.at[phase], col_recv.at[phase, far * 8 + m], col_sem.at[0, phase],
                        col_sem.at[1, phase], member(at, flip_b, m, to),
                    ).start()
        landed_at(col_recv.at[phase, pl.ds(1, 15)], col_sem.at[1, phase])
        total = col_send[phase].astype(f32)
        for m in range(1, 16):
            total += col_recv[phase, m].astype(f32)
        return 1.0 / (1.0 + total)

    spread[...] = jnp.ones((T, 256), f32)
    for phase in range(ITERS):
        row_exchange(phase, row_sweep())
        scale_a = 1.0 / row_result(phase)
        spread[...] = dot(oat[...], scale_a.astype(bf16))
        scale_b = col_exchange(phase, col_sweep())
        spread[...] = dot(obt[...], scale_b.astype(bf16))
    x, y, z = at
    member_b = x // 2 + 2 * (y // 2) + 4 * (z // 2)
    scales[...] = scale_b
    near_rows = scales[pl.ds(pl.multiple_of((member_b // 2) * 8, 8), 8), :]
    scale_ref[...] = jnp.where(member_b % 2 == 0, near_rows[0:4], near_rows[4:8])
    dense[...] = dot(obd[...], scale_b.astype(bf16))

    def partial(slot):
        def body(i, c):
            total, mass = None, None
            a = slot * 2 + i
            rows = dense[pl.ds(pl.multiple_of(a * 8, 8), 8), :]
            for d in range(8):
                weights = tiles[jnp.clip(idx[a, d], 0, T - 1)].astype(f32) * rows[d : d + 1]
                b = jnp.clip(idx[16 + a, d], 0, 31)
                part = dot(weights.astype(bf16), bbuf[b // 4, b % 4])
                half = weights[:, 0:128] + weights[:, 128:256]
                total = part if total is None else total + part
                mass = half if mass is None else mass + half
            if slot != 7:
                numer[a] = total
            if slot:
                ship[a] = total.astype(bf16)
            column = jnp.sum(mass, axis=1, keepdims=True)
            a_at = flipped([(slot >> k) & 1 for k in range(3)], [p % 2 for p in at]) * 2 + i
            final[...] = jnp.where(iota((256, 128), 1) == a_at, column, final[...])
            return c

        lax.fori_loop(0, 2, body, 0)

    final[...] = jnp.zeros((256, 128), f32)

    def send_half(piece, slot, dim, order):
        start, size = PIECES[piece]
        two, rows = pl.ds(slot * 2, 2), pl.ds(start, size)
        if order:
            ship[two, rows, :] = numer[two, rows, :].astype(bf16)
        there = slot ^ (1 << dim)
        remote(
            ship.at[two, rows], landed.at[order, pl.ds(there * 2, 2), rows], out_sem.at[2], half_sem.at[order, piece, there],
            member(at, flip_a, 1 << dim, core),
        ).start()

    def add_half(piece, slot, order):
        start, size = PIECES[piece]
        two, rows = pl.ds(slot * 2, 2), pl.ds(start, size)
        here = landed.at[order, two, rows]
        pltpu.make_async_copy(here, here, half_sem.at[order, piece, slot]).wait()
        numer[two, rows, :] = numer[two, rows, :] + landed[order, two, rows, :].astype(f32)

    def map_slots(slots):
        for slot in slots:
            partial(slot)
            for r in range(3):
                if (slot >> r) & 1:
                    send_half(r, slot, r, 0)

    near_dims = [(r, 1 << ((r + 1) % 3), 1 << ((r + 2) % 3)) for r in range(3)]
    map_slots((7, 3, 5, 6))
    for r, k1, k2 in near_dims:
        add_half(r, k1 | k2, 0)
        send_half(r, k1 | k2, (r + 1) % 3, 1)
    map_slots((1, 2, 4))
    for r, k1, k2 in near_dims:
        add_half(r, k1, 0)
        send_half(r, k1, (r + 1) % 3, 1)
    map_slots((0,))
    row_exchange(ITERS, jnp.transpose(final[...])[0:16])

    landed_at(abuf.at[pl.ds(2, 14)], out_sem.at[0])
    landed_at(bbuf.at[pl.ds(1, 7), pl.ds(0, 2)], out_sem.at[0])
    landed_at(bbuf.at[pl.ds(1, 7), pl.ds(0, 2)], out_sem.at[1])
    for cat in range(2):
        landed_at(norm_bufs[cat].at[pl.ds(1, 7)], norm_sem.at[0, cat])
    for phase in range(ITERS):
        landed_at(row_recv.at[phase, pl.ds(1, 7)], row_sem.at[0, phase])
        landed_at(col_recv.at[phase, pl.ds(1, 15)], col_sem.at[0, phase])

    for r, k1, k2 in near_dims:
        add_half(r, k2, 0)
        add_half(r, k2, 1)
        send_half(r, k2, (r + 2) % 3, 2)
    for r in range(3):
        add_half(r, 0, 0)
        add_half(r, 0, 1)
    sums[pl.ds(0, 16), :] = row_result(ITERS)
    own_a = x % 2 + 2 * (y % 2) + 4 * (z % 2)
    near_rows = sums[pl.ds(pl.multiple_of((own_a // 4) * 8, 8), 8), :]
    mine = near_rows[0:2]
    for k in range(1, 4):
        mine = jnp.where(own_a % 4 == k, near_rows[2 * k : 2 * k + 2], mine)
    column = jnp.transpose(jnp.broadcast_to(1.0 / mine[:, None, :], (2, 128, 256)).reshape(256, 256))
    for r in range(3):
        start, size = PIECES[r]
        rows = pl.ds(start, size)
        landed_at(landed.at[2, pl.ds(0, 2), rows], half_sem.at[2, r, 0])
        for i in range(2):
            inverse = column[start : start + size, i * 128 : i * 128 + 1]
            mapped_ref[i, rows, :] = ((numer[i, rows, :] + landed[2, i, rows, :].astype(f32)) * inverse).astype(bf16)
    landed_at(ship.at[pl.ds(2, 14)], out_sem.at[2])
    landed_at(row_recv.at[ITERS, pl.ds(1, 7)], row_sem.at[0, ITERS])


def transport(T, cid, own, partners, counts):
    vmem = pl.BlockSpec(memory_space=pltpu.VMEM)
    dma = pltpu.SemaphoreType.DMA
    return pl.pallas_call(
        functools.partial(kernel, T),
        out_shape=(
            jax.ShapeDtypeStruct((2, 256, 256), bf16),
            jax.ShapeDtypeStruct((4, 256), f32),
            jax.ShapeDtypeStruct((1, 1), f32),
            jax.ShapeDtypeStruct((1, 256), jnp.int32),
        ),
        in_specs=[pl.BlockSpec(memory_space=pltpu.HBM)] * 3,
        out_specs=(vmem, vmem, pl.BlockSpec(memory_space=pltpu.SMEM), vmem),
        scratch_shapes=[
            pltpu.VMEM((16, T), bf16),
            pltpu.VMEM((T, 16), bf16),
            pltpu.VMEM((32, T), bf16),
            pltpu.VMEM((T, 32), bf16),
            pltpu.VMEM((128, 32), bf16),
            pltpu.VMEM((32, 256), jnp.int32),
            pltpu.VMEM((1, 256), jnp.int32),
            pltpu.VMEM((40, 128), jnp.int32),
            pltpu.SMEM((40, 128), jnp.int32),
            pltpu.VMEM((256, 128), f32),
            pltpu.VMEM((8, 8, 256), f32),
            pltpu.VMEM((8, 8, 256), f32),
            dma((2, 2)),
            pltpu.VMEM((16, 256, 256), bf16),
            pltpu.VMEM((8, 4, 256, 256), bf16),
            pltpu.VMEM((T, 256, 256), bf16),
            pltpu.VMEM((16, 256, 1), f32),
            pltpu.VMEM((32, 8, 256), f32),
            pltpu.VMEM((T, 256), f32),
            pltpu.VMEM((256, T), f32),
            pltpu.VMEM((T, 256), f32),
            pltpu.VMEM((128, 256), f32),
            pltpu.VMEM((4, 16, 256), bf16),
            pltpu.VMEM((3, 32, 256), bf16),
            pltpu.VMEM((4, 8, 16, 256), bf16),
            pltpu.VMEM((3, 16, 32, 256), bf16),
            pltpu.VMEM((32, 256), f32),
            pltpu.VMEM((16, 256, 256), f32),
            pltpu.VMEM((16, 256, 256), bf16),
            pltpu.VMEM((3, 16, 256, 256), bf16),
            dma((3,)),
            dma((2,)),
            dma((2, 3, 8)),
            dma((8,)),
            dma((3,)),
            dma((2, 4)),
            dma((2, 3)),
            dma((3, 3, 8)),
            dma((1,)),
            pltpu.SemaphoreType.REGULAR((2,)),
        ],
        compiler_params=pltpu.CompilerParams(
            collective_id=cid, has_side_effects=True, vmem_limit_bytes=60 << 20
        ),
        name=f"transport_{T}",
    )(own, partners, counts)


def shards(embeds, partners, counts):
    args = embeds.reshape(4, 256, 256), partners.T, counts.reshape(1, 256)
    mapped, scale, most, limits = transport(64, 0, *args)
    mapped, scale = lax.cond(
        most.reshape(()) <= 64.0,
        lambda mapped, scale, *args: (mapped, scale),
        lambda mapped, scale, *args: transport(128, 1, *args)[:2],
        mapped,
        scale,
        *args[:2],
        limits,
    )
    return mapped.reshape(1, 1, 2, 256, 256), scale


def solution(mesh):
    in_specs = (P("side", ("grp", "dev"), None, None), P(), P())
    out_specs = (P(("grp", "dev"), "side", None, None, None), P(("grp", "dev"), None))
    return jax.shard_map(shards, mesh=mesh, in_specs=in_specs, out_specs=out_specs, check_vma=False)
```

```python
import functools
import math

import jax
import jax.numpy as jnp
from jax import lax
from jax.experimental import pallas as pl
from jax.experimental.pallas import tpu as pltpu
from jax.sharding import PartitionSpec as P

ITERS = 3
TURN = 64
FAR_FIRST = (7, 3, 5, 6, 1, 2, 4)
GAIN = 20.0 * math.log2(math.e)
MESH = pl.DeviceIdType.MESH
NT = (((1,), (1,)), ((), ()))
f32 = jnp.float32
bf16 = jnp.bfloat16
PIECES = (((0, 96), (0, 80)), ((96, 80), (80, 96)), ((176, 80), (176, 80)))


def total_rows(piece):
    return sum(size for _, size in PIECES[piece])


def place():
    d = lax.axis_index("dev")
    return lax.axis_index("side"), (d // 4, lax.axis_index("grp"), d % 4)


def flip_a(p):
    return p + 1 - 2 * (p % 2)


def flip_b(p):
    return 3 - p


def member(at, flip, bits, core):
    x, y, z = [flip(p) if (bits >> k) & 1 else p for k, p in enumerate(at)]
    return (core, y, x * 4 + z)


def dot(a, b):
    return jnp.dot(a, b, preferred_element_type=f32)


def dot_nt(a, b):
    return lax.dot_general(a, b, NT, preferred_element_type=f32)


def kernel(
    T,
    x_ref,
    partners_ref,
    counts_ref,
    mapped_ref,
    scale_ref,
    most_ref,
    counts_out,
    oa,
    oat,
    ob,
    obt,
    obd,
    partners,
    counts,
    index,
    idx,
    final,
    norms_a,
    norms_b,
    norm_sem,
    abuf,
    bbuf,
    tiles,
    row_norm,
    col_norm,
    sums,
    columns,
    spread,
    dense,
    row_send,
    col_send,
    row_recv,
    col_recv,
    scales,
    numer,
    ship,
    landed,
    own_sem,
    sib_sem,
    gather_sem,
    relay_sem,
    out_sem,
    row_sem,
    col_sem,
    half_sem,
    index_sem,
    ready,
):
    core, at = place()
    other = 1 - core
    sibling = member(at, flip_a, 0, other)
    flips = (flip_a, flip_b)
    norm_bufs = (norms_a, norms_b)
    bufs = (abuf, bbuf)

    barrier = pltpu.get_barrier_semaphore()
    greeted = []
    for m in (1, 2, 4):
        greeted += [member(at, flip, m, to) for flip in (flip_a, flip_b) for to in (other, core)]
    greeted.append(sibling)
    for peer in greeted:
        pl.semaphore_signal(barrier, inc=1, device_id=peer, device_id_type=MESH)
    fetches = [
        pltpu.make_async_copy(partners_ref, partners, own_sem.at[1]),
        pltpu.make_async_copy(counts_ref, counts, own_sem.at[2]),
    ]
    for fetch in fetches:
        fetch.start()
    pl.semaphore_wait(barrier, len(greeted))

    def greet(level):
        for peer in greeted:
            pl.semaphore_signal(ready.at[level], inc=1, device_id=peer, device_id_type=MESH)

    def greeted_by_all(level):
        pl.semaphore_wait(ready.at[level], len(greeted))

    def remote(src, dst, send, recv, peer):
        return pltpu.make_async_remote_copy(
            src_ref=src, dst_ref=dst, send_sem=send, recv_sem=recv, device_id=peer, device_id_type=MESH
        )

    def unit(cat, slot, piece):
        rows = [pl.ds(start, size) for start, size in PIECES[piece]]
        if cat == 0:
            return [abuf.at[slot * 2 + i, rows[i]] for i in range(2)]
        return [bbuf.at[slot, core * 2 + i, rows[i]] for i in range(2)]

    def send_unit(cat, dim, piece, slot):
        there = slot ^ (1 << dim)
        for src, dst in zip(unit(cat, slot, piece), unit(cat, there, piece)):
            remote(
                src, dst, out_sem.at[0], gather_sem.at[cat, piece, there], member(at, flips[cat], 1 << dim, core)
            ).start()

    def send_own(cat):
        for step in range(3):
            for dim in range(3):
                piece = (dim - step) % 3
                there = 1 << dim
                for half in range(2):
                    for i, (start, size) in enumerate(PIECES[piece]):
                        rows = pl.ds(start, size)
                        remote(
                            x_ref.at[half * 2 + i, rows],
                            abuf.at[there * 2 + i, rows] if cat == 0 else bbuf.at[there, half * 2 + i, rows],
                            out_sem.at[0],
                            gather_sem.at[cat, piece, there],
                            member(at, flips[cat], there, half),
                        ).start()

    own_a_half, own_b = abuf.at[pl.ds(0, 2)], bbuf.at[0]

    def landed_at(ref, sem):
        pltpu.make_async_copy(ref, ref, sem).wait()

    @pl.when(core == 0)
    def _():
        give = remote(x_ref.at[pl.ds(2, 2)], own_a_half, sib_sem.at[0], sib_sem.at[1], sibling)
        give.start()
        mine = pltpu.make_async_copy(x_ref.at[pl.ds(0, 2)], own_a_half, own_sem.at[0])
        mine.start()
        send_own(0)
        greet(0)
        mine.wait()
        give.wait_send()
        landed_at(own_b, sib_sem.at[1])

    @pl.when(core == 1)
    def _():
        give = remote(x_ref, own_b, sib_sem.at[0], sib_sem.at[1], sibling)
        give.start()
        mine = pltpu.make_async_copy(x_ref, own_b, own_sem.at[0])
        mine.start()
        send_own(1)
        greet(0)
        mine.wait()
        give.wait_send()
        landed_at(own_a_half, sib_sem.at[1])


    def arrived(cat, piece, slot):
        rows = pl.ds(0, total_rows(piece))
        landed_at(
            abuf.at[slot * 2, rows] if cat == 0 else bbuf.at[slot, core * 2, rows], gather_sem.at[cat, piece, slot]
        )
        if cat == 1:
            for here in unit(cat, slot, piece):
                remote(here, here, out_sem.at[1], relay_sem.at[slot], sibling).start()

    def iota(shape, dim):
        return lax.broadcasted_iota(jnp.int32, shape, dim)

    diagonal = iota((128, 128), 0) == iota((128, 128), 1)

    def own_norms():
        def inverse_norm(block, scale):
            halves = []
            for h in range(2):
                y = block[h * 128 : h * 128 + 128]
                total = jnp.sum(jnp.where(diagonal, dot_nt(y, y), 0.0), axis=0, keepdims=True)
                halves.append(lax.rsqrt(total * (1.0 / 256.0) + 1e-06) * scale)
            return jnp.concatenate(halves, axis=1)

        for i in range(2):
            norm_bufs[0][0, i : i + 1] = inverse_norm(abuf[i], GAIN / 16.0)
        for i in range(4):
            norm_bufs[1][0, i : i + 1] = inverse_norm(bbuf[0, i], 1.0 / 16.0)

    def share_norms():
        for cat in range(2):
            for m in range(1, 8):
                remote(
                    norm_bufs[cat].at[0], norm_bufs[cat].at[m], norm_sem.at[0, cat], norm_sem.at[1, cat],
                    member(at, flips[cat], m, core),
                ).start()

    def take_norms():
        for cat in range(2):
            landed_at(norm_bufs[cat].at[pl.ds(1, 7)], norm_sem.at[1, cat])
        flipped_norms = jnp.transpose(
            jnp.concatenate([norm_bufs[0][m] for m in range(8)] + [jnp.zeros((64, 256), f32)], axis=0)
        )
        for a in range(16):
            lane = (a // 2) * 8 + a % 2
            row_norm[a] = flipped_norms[:, lane : lane + 1]
        for b in range(32):
            col_norm[b] = jnp.broadcast_to(norm_bufs[1][b // 4, b % 4 : b % 4 + 1], (8, 256))

    def bits_of(values, shifts):
        return [(values >> k) & 1 for k in shifts]

    def flipped(bits, by):
        return sum((b + f - 2 * b * f) * (1 << k) for k, (b, f) in enumerate(zip(bits, by)))

    def make_list():
        x, y, z = at
        own_low = [p % 2 for p in at]
        own_high = [p // 2 for p in at]
        for fetch in fetches:
            fetch.wait()
        named_all = partners[...]
        limit_row = counts[...]
        counts_out[...] = limit_row
        r = iota((16, 256), 0)
        cx, cy, cz = [flipped([b], [p % 2]) + 2 * (p // 2) for b, p in zip(bits_of(r, (1, 2, 3)), at)]
        chosen = iota((16, 256), 1) == (cy * 16 + cx * 4 + cz) * 4 + 2 * core + (r & 1)
        named = dot_nt(chosen.astype(f32).astype(bf16), named_all.astype(f32).astype(bf16)).astype(jnp.int32)
        limit = jnp.sum(jnp.where(chosen, jnp.broadcast_to(limit_row, (16, 256)), 0).astype(f32), axis=1, keepdims=True)
        slot_at = iota((16, 32), 1).astype(f32)

        def coords(entry):
            owner = entry >> 2
            return (owner >> 2) & 3, owner >> 4, owner & 3

        parts = coords(named)
        active = slot_at < limit
        for p, q in zip(parts, at):
            active &= (p == q) | (p == 3 - q)
        jb = sum((p >> 1) * (1 << k) for k, p in enumerate(parts))
        pick = (named & 3) + 1
        lane = iota((16, 128), 1)
        bp = jnp.zeros((16, 128), f32)
        for k in range(8):
            best = jnp.max(jnp.where(active & (jb == k), pick, 0).astype(f32), axis=1, keepdims=True)
            bp = jnp.where(lane == k, best, bp)
        used = jnp.where(bp > 0, 1.0, 0.0).astype(bf16)
        i128, j128 = iota((128, 128), 0), iota((128, 128), 1)

        def mask(m):
            return jnp.where(m, 1.0, 0.0).astype(bf16)

        in_row = dot(used, mask(i128 < j128))
        of_row = dot(used, mask(i128 < 128))
        above = dot(mask(iota((16, 16), 1) < iota((16, 16), 0)), of_row.astype(bf16))
        pos = above + in_row
        k3 = bits_of(lane, (0, 1, 2))
        b_rel = flipped(k3, own_high) * 4 + jnp.maximum(bp.astype(jnp.int32) - 1, 0)
        index[pl.ds(0, 16), :] = jnp.where(bp > 0, jnp.minimum(pos, T - 1.0), 0.0).astype(jnp.int32)
        index[pl.ds(16, 16), :] = jnp.where(lane < 8, b_rel, 0)

        spread_out = mask(i128 == (j128 & 7))
        own_lane = (lane >> 3) == iota((16, 128), 0)

        def flat(values):
            return jnp.sum(jnp.where(own_lane, dot(values.astype(bf16), spread_out), 0.0), axis=0, keepdims=True)

        bp_row, pos_row = flat(bp), flat(pos)
        hot = mask((iota((T, 128), 0).astype(f32) == pos_row) & (bp_row > 0))
        e = iota((8, 128), 1)
        pick_row = jnp.maximum(jnp.broadcast_to(bp_row, (8, 128)).astype(jnp.int32) - 1, 0)
        b_e = flipped(bits_of(e, (0, 1, 2)), own_high) * 4 + pick_row
        values = jnp.where(iota((8, 128), 0) == 0, e >> 3, b_e).astype(f32).astype(bf16)
        index[pl.ds(32, 8), pl.ds(0, T)] = dot_nt(values, hot).astype(jnp.int32)
        fetch = pltpu.make_async_copy(index, idx, index_sem.at[0])
        fetch.start()
        e16, e32 = iota((16, 128), 1), iota((32, 128), 1)
        a_abs = flipped(bits_of(e16, (4, 5, 6)), own_low) * 2 + ((e16 >> 3) & 1)
        a_hot = mask(iota((16, 128), 0) == a_abs)
        b_abs = (e32 & 7) * 4 + jnp.broadcast_to(bp_row, (32, 128)).astype(jnp.int32) - 1
        b_hot = mask((iota((32, 128), 0) == b_abs) & (bp_row > 0))
        oa[...] = dot_nt(a_hot, hot).astype(bf16)
        oat[...] = dot_nt(hot, a_hot).astype(bf16)
        ob[...] = dot_nt(b_hot, hot).astype(bf16)
        obt[...] = dot_nt(hot, b_hot).astype(bf16)
        obd[...] = dot_nt(mask(i128 == j128), b_hot).astype(bf16)

        active = iota((32, 256), 0) < limit_row
        kind = sum((((p + 1) >> 1) & 1) * (1 << k) for k, p in enumerate(coords(named_all)))
        g, row = iota((16, 256), 0), iota((16, 256), 1)
        group = ((row >> 7) & 1) * 8 + ((row >> 5) & 1) * 4 + ((row >> 3) & 1) * 2 + ((row >> 1) & 1)
        members = mask(g == group)
        most = jnp.zeros((16, 1), f32)
        for k in range(8):
            most = jnp.maximum(
                most, jnp.sum(dot_nt(members, mask(active & (kind == k))), axis=1, keepdims=True)
            )
        most_ref[0, 0] = jnp.max(most)
        fetch.wait()

    def received(steps):
        for r in range(3):
            slot = steps(1 << r, 1 << ((r + 1) % 3), 1 << ((r + 2) % 3))
            for cat in range(2):
                arrived(cat, r, slot)
                yield cat, r, slot

    make_list()
    greeted_by_all(0)
    greet(1)
    own_norms()
    for cat, r, slot in received(lambda k0, k1, k2: k0):
        send_unit(cat, (r + 1) % 3, r, slot)
    for r in range(3):
        for cat in range(2):
            send_unit(cat, (r + 2) % 3, r, 1 << r)
    greeted_by_all(1)
    share_norms()
    for cat, r, slot in received(lambda k0, k1, k2: k1):
        send_unit(cat, (r + 2) % 3, r, slot)
    for cat, r, slot in received(lambda k0, k1, k2: k0 | k1):
        send_unit(cat, (r + 2) % 3, r, slot)
    for cat in (1, 0):
        for rest in (0, 1, 2, 3):
            for r in range(3):
                near, far = (rest & 1) << r, (rest >> 1) << ((r + 1) % 3)
                arrived(cat, r, near | far | (1 << ((r + 2) % 3)))
    take_norms()
    for slot in range(1, 8):
        landed_at(bbuf.at[slot, pl.ds(other * 2, 2)], relay_sem.at[slot])

    def build(i, c):
        for u in range(TURN):
            t = i * TURN + u
            a, b = jnp.clip(idx[32, t], 0, 15), jnp.clip(idx[33, t], 0, 31)
            scores = dot_nt(abuf[a], bbuf[b // 4, b % 4])
            tiles[t] = jnp.exp2(scores * row_norm[a] * col_norm[b][0:1] - GAIN).astype(bf16)
        return c

    lax.fori_loop(0, T // TURN, build, 0)

    row_id = iota((8, 256), 0)
    lane_id = iota((256, T), 1)

    def row_sweep():
        def body(i, c):
            beside = columns[...]
            for g in range(TURN // 8):
                base = i * TURN + g * 8
                rows = pl.ds(pl.multiple_of(base, 8), 8)
                left = spread[rows, :]
                left_bf = left.astype(bf16)
                total = jnp.zeros((8, 256), f32)
                for u in range(8):
                    tile = tiles[base + u]
                    if u % 2 == 0:
                        total = jnp.where(row_id == u, dot_nt(left_bf, tile), total)
                    else:
                        scaled = tile.astype(f32) * left[u : u + 1]
                        mass = jnp.sum(scaled[:, 0:128] + scaled[:, 128:256], axis=1, keepdims=True)
                        beside = jnp.where(lane_id == base + u, mass, beside)
                sums[rows, :] = total
            columns[...] = beside
            return c

        columns[...] = jnp.zeros((256, T), f32)
        lax.fori_loop(0, T // TURN, body, 0)
        return dot(oa[...], sums[...].astype(bf16)) + dot_nt(oa[...], columns[...].astype(bf16))

    def col_sweep():
        def body(i, c):
            for g in range(TURN // 8):
                base = i * TURN + g * 8
                rows = pl.ds(pl.multiple_of(base, 8), 8)
                left = spread[rows, :].astype(bf16)
                total = jnp.zeros((8, 256), f32)
                for u in range(8):
                    total = jnp.where(row_id == u, dot(left, tiles[base + u]), total)
                sums[rows, :] = total
            return c

        lax.fori_loop(0, T // TURN, body, 0)
        return dot(ob[...], sums[...].astype(bf16))

    def row_exchange(phase, partial):
        row_send[phase] = partial.astype(bf16)
        for m in FAR_FIRST:
            remote(
                row_send.at[phase], row_recv.at[phase, m], row_sem.at[0, phase], row_sem.at[1, phase],
                member(at, flip_a, m, core),
            ).start()

    def row_result(phase):
        landed_at(row_recv.at[phase, pl.ds(1, 7)], row_sem.at[1, phase])
        total = row_send[phase].astype(f32)
        for m in range(1, 8):
            total += row_recv[phase, m].astype(f32)
        return total

    def col_exchange(phase, partial):
        col_send[phase] = partial.astype(bf16)
        for m in FAR_FIRST + (0,):
            for far, to in ((1, other), (0, core)):
                if far + m:
                    remote(
                        col_send.at[phase], col_recv.at[phase, far * 8 + m], col_sem.at[0, phase],
                        col_sem.at[1, phase], member(at, flip_b, m, to),
                    ).start()
        landed_at(col_recv.at[phase, pl.ds(1, 15)], col_sem.at[1, phase])
        total = col_send[phase].astype(f32)
        for m in range(1, 16):
            total += col_recv[phase, m].astype(f32)
        return 1.0 / (1.0 + total)

    spread[...] = jnp.ones((T, 256), f32)
    for phase in range(ITERS):
        row_exchange(phase, row_sweep())
        scale_a = 1.0 / row_result(phase)
        spread[...] = dot(oat[...], scale_a.astype(bf16))
        scale_b = col_exchange(phase, col_sweep())
        spread[...] = dot(obt[...], scale_b.astype(bf16))
    x, y, z = at
    member_b = x // 2 + 2 * (y // 2) + 4 * (z // 2)
    scales[...] = scale_b
    near_rows = scales[pl.ds(pl.multiple_of((member_b // 2) * 8, 8), 8), :]
    scale_ref[...] = jnp.where(member_b % 2 == 0, near_rows[0:4], near_rows[4:8])
    dense[...] = dot(obd[...], scale_b.astype(bf16))

    def partial(slot):
        def body(i, c):
            total, mass = None, None
            a = slot * 2 + i
            rows = dense[pl.ds(pl.multiple_of(a * 8, 8), 8), :]
            for d in range(8):
                weights = tiles[jnp.clip(idx[a, d], 0, T - 1)].astype(f32) * rows[d : d + 1]
                b = jnp.clip(idx[16 + a, d], 0, 31)
                part = dot(weights.astype(bf16), bbuf[b // 4, b % 4])
                half = weights[:, 0:128] + weights[:, 128:256]
                total = part if total is None else total + part
                mass = half if mass is None else mass + half
            if slot != 7:
                numer[a] = total
            if slot:
                ship[a] = total.astype(bf16)
            column = jnp.sum(mass, axis=1, keepdims=True)
            a_at = flipped([(slot >> k) & 1 for k in range(3)], [p % 2 for p in at]) * 2 + i
            final[...] = jnp.where(iota((256, 128), 1) == a_at, column, final[...])
            return c

        lax.fori_loop(0, 2, body, 0)

    final[...] = jnp.zeros((256, 128), f32)

    def send_half(piece, slot, dim, order):
        there = slot ^ (1 << dim)
        for i, (start, size) in enumerate(PIECES[piece]):
            rows = pl.ds(start, size)
            if order:
                ship[slot * 2 + i, rows, :] = numer[slot * 2 + i, rows, :].astype(bf16)
            remote(
                ship.at[slot * 2 + i, rows],
                landed.at[order, there * 2 + i, rows],
                out_sem.at[2],
                half_sem.at[order, piece, there],
                member(at, flip_a, 1 << dim, core),
            ).start()

    def half_landed(piece, slot, order):
        landed_at(landed.at[order, slot * 2, pl.ds(0, total_rows(piece))], half_sem.at[order, piece, slot])

    def add_half(piece, slot, order):
        half_landed(piece, slot, order)
        for i, (start, size) in enumerate(PIECES[piece]):
            a, rows = slot * 2 + i, pl.ds(start, size)
            numer[a, rows, :] = numer[a, rows, :] + landed[order, a, rows, :].astype(f32)

    def map_slots(slots):
        for slot in slots:
            partial(slot)
            for r in range(3):
                if (slot >> r) & 1:
                    send_half(r, slot, r, 0)

    near_dims = [(r, 1 << ((r + 1) % 3), 1 << ((r + 2) % 3)) for r in range(3)]
    map_slots((7, 3, 5, 6))
    for r, k1, k2 in near_dims:
        add_half(r, k1 | k2, 0)
        send_half(r, k1 | k2, (r + 1) % 3, 1)
    map_slots((1, 2, 4))
    for r, k1, k2 in near_dims:
        add_half(r, k1, 0)
        send_half(r, k1, (r + 1) % 3, 1)
    map_slots((0,))
    row_exchange(ITERS, jnp.transpose(final[...])[0:16])

    landed_at(abuf.at[pl.ds(2, 14)], out_sem.at[0])
    landed_at(bbuf.at[pl.ds(1, 7), pl.ds(0, 2)], out_sem.at[0])
    landed_at(bbuf.at[pl.ds(1, 7), pl.ds(0, 2)], out_sem.at[1])
    for cat in range(2):
        landed_at(norm_bufs[cat].at[pl.ds(1, 7)], norm_sem.at[0, cat])
    for phase in range(ITERS):
        landed_at(row_recv.at[phase, pl.ds(1, 7)], row_sem.at[0, phase])
        landed_at(col_recv.at[phase, pl.ds(1, 15)], col_sem.at[0, phase])

    for r, k1, k2 in near_dims:
        add_half(r, k2, 0)
        add_half(r, k2, 1)
        send_half(r, k2, (r + 2) % 3, 2)
    for r in range(3):
        add_half(r, 0, 0)
        add_half(r, 0, 1)
    sums[pl.ds(0, 16), :] = row_result(ITERS)
    own_a = x % 2 + 2 * (y % 2) + 4 * (z % 2)
    near_rows = sums[pl.ds(pl.multiple_of((own_a // 4) * 8, 8), 8), :]
    mine = near_rows[0:2]
    for k in range(1, 4):
        mine = jnp.where(own_a % 4 == k, near_rows[2 * k : 2 * k + 2], mine)
    column = jnp.transpose(jnp.broadcast_to(1.0 / mine[:, None, :], (2, 128, 256)).reshape(256, 256))
    for r in range(3):
        half_landed(r, 0, 2)
        for i, (start, size) in enumerate(PIECES[r]):
            rows = pl.ds(start, size)
            inverse = column[start : start + size, i * 128 : i * 128 + 1]
            mapped_ref[i, rows, :] = ((numer[i, rows, :] + landed[2, i, rows, :].astype(f32)) * inverse).astype(bf16)
    landed_at(ship.at[pl.ds(2, 14)], out_sem.at[2])
    landed_at(row_recv.at[ITERS, pl.ds(1, 7)], row_sem.at[0, ITERS])


def transport(T, cid, own, partners, counts):
    vmem = pl.BlockSpec(memory_space=pltpu.VMEM)
    dma = pltpu.SemaphoreType.DMA
    return pl.pallas_call(
        functools.partial(kernel, T),
        out_shape=(
            jax.ShapeDtypeStruct((2, 256, 256), bf16),
            jax.ShapeDtypeStruct((4, 256), f32),
            jax.ShapeDtypeStruct((1, 1), f32),
            jax.ShapeDtypeStruct((1, 256), jnp.int32),
        ),
        in_specs=[pl.BlockSpec(memory_space=pltpu.HBM)] * 3,
        out_specs=(vmem, vmem, pl.BlockSpec(memory_space=pltpu.SMEM), vmem),
        scratch_shapes=[
            pltpu.VMEM((16, T), bf16),
            pltpu.VMEM((T, 16), bf16),
            pltpu.VMEM((32, T), bf16),
            pltpu.VMEM((T, 32), bf16),
            pltpu.VMEM((128, 32), bf16),
            pltpu.VMEM((32, 256), jnp.int32),
            pltpu.VMEM((1, 256), jnp.int32),
            pltpu.VMEM((40, 128), jnp.int32),
            pltpu.SMEM((40, 128), jnp.int32),
            pltpu.VMEM((256, 128), f32),
            pltpu.VMEM((8, 8, 256), f32),
            pltpu.VMEM((8, 8, 256), f32),
            dma((2, 2)),
            pltpu.VMEM((16, 256, 256), bf16),
            pltpu.VMEM((8, 4, 256, 256), bf16),
            pltpu.VMEM((T, 256, 256), bf16),
            pltpu.VMEM((16, 256, 1), f32),
            pltpu.VMEM((32, 8, 256), f32),
            pltpu.VMEM((T, 256), f32),
            pltpu.VMEM((256, T), f32),
            pltpu.VMEM((T, 256), f32),
            pltpu.VMEM((128, 256), f32),
            pltpu.VMEM((4, 16, 256), bf16),
            pltpu.VMEM((3, 32, 256), bf16),
            pltpu.VMEM((4, 8, 16, 256), bf16),
            pltpu.VMEM((3, 16, 32, 256), bf16),
            pltpu.VMEM((32, 256), f32),
            pltpu.VMEM((16, 256, 256), f32),
            pltpu.VMEM((16, 256, 256), bf16),
            pltpu.VMEM((3, 16, 256, 256), bf16),
            dma((3,)),
            dma((2,)),
            dma((2, 3, 8)),
            dma((8,)),
            dma((3,)),
            dma((2, 4)),
            dma((2, 3)),
            dma((3, 3, 8)),
            dma((1,)),
            pltpu.SemaphoreType.REGULAR((2,)),
        ],
        compiler_params=pltpu.CompilerParams(
            collective_id=cid, has_side_effects=True, vmem_limit_bytes=60 << 20
        ),
        name=f"transport_{T}",
    )(own, partners, counts)


def shards(embeds, partners, counts):
    args = embeds.reshape(4, 256, 256), partners.T, counts.reshape(1, 256)
    mapped, scale, most, limits = transport(64, 0, *args)
    mapped, scale = lax.cond(
        most.reshape(()) <= 64.0,
        lambda mapped, scale, *args: (mapped, scale),
        lambda mapped, scale, *args: transport(128, 1, *args)[:2],
        mapped,
        scale,
        *args[:2],
        limits,
    )
    return mapped.reshape(1, 1, 2, 256, 256), scale


def solution(mesh):
    in_specs = (P("side", ("grp", "dev"), None, None), P(), P())
    out_specs = (P(("grp", "dev"), "side", None, None, None), P(("grp", "dev"), None))
    return jax.shard_map(shards, mesh=mesh, in_specs=in_specs, out_specs=out_specs, check_vma=False)
```

```python
import functools
import math

import jax
import jax.numpy as jnp
from jax import lax
from jax.experimental import pallas as pl
from jax.experimental.pallas import tpu as pltpu
from jax.sharding import PartitionSpec as P

ITERS = 3
TURN = 64
FAR_FIRST = (7, 3, 5, 6, 1, 2, 4)
GAIN = 20.0 * math.log2(math.e)
MESH = pl.DeviceIdType.MESH
NT = (((1,), (1,)), ((), ()))
f32 = jnp.float32
bf16 = jnp.bfloat16
PIECES = (((0, 96), (0, 80)), ((96, 80), (80, 96)), ((176, 80), (176, 80)))


def total_rows(piece):
    return sum(size for _, size in PIECES[piece])


def place():
    d = lax.axis_index("dev")
    return lax.axis_index("side"), (d // 4, lax.axis_index("grp"), d % 4)


def flip_a(p):
    return p + 1 - 2 * (p % 2)


def flip_b(p):
    return 3 - p


def member(at, flip, bits, core):
    x, y, z = [flip(p) if (bits >> k) & 1 else p for k, p in enumerate(at)]
    return (core, y, x * 4 + z)


def dot(a, b):
    return jnp.dot(a, b, preferred_element_type=f32)


def dot_nt(a, b):
    return lax.dot_general(a, b, NT, preferred_element_type=f32)


def kernel(
    T,
    x_ref,
    partners_ref,
    counts_ref,
    mapped_ref,
    scale_ref,
    most_ref,
    counts_out,
    oa,
    oat,
    ob,
    obt,
    obd,
    partners,
    counts,
    index,
    idx,
    final,
    norms_a,
    norms_b,
    norm_sem,
    abuf,
    bbuf,
    tiles,
    row_norm,
    col_norm,
    sums,
    columns,
    spread,
    dense,
    row_send,
    col_send,
    row_recv,
    col_recv,
    scales,
    numer,
    ship,
    landed,
    own_sem,
    sib_sem,
    gather_sem,
    relay_sem,
    out_sem,
    row_sem,
    col_sem,
    half_sem,
    index_sem,
    ready,
):
    core, at = place()
    other = 1 - core
    sibling = member(at, flip_a, 0, other)
    flips = (flip_a, flip_b)
    norm_bufs = (norms_a, norms_b)
    bufs = (abuf, bbuf)

    barrier = pltpu.get_barrier_semaphore()
    greeted = []
    for m in (1, 2, 4):
        greeted += [member(at, flip, m, to) for flip in (flip_a, flip_b) for to in (other, core)]
    greeted.append(sibling)
    for peer in greeted:
        pl.semaphore_signal(barrier, inc=1, device_id=peer, device_id_type=MESH)
    fetches = [
        pltpu.make_async_copy(partners_ref, partners, own_sem.at[1]),
        pltpu.make_async_copy(counts_ref, counts, own_sem.at[2]),
    ]
    for fetch in fetches:
        fetch.start()
    pl.semaphore_wait(barrier, len(greeted))

    def greet(level):
        for peer in greeted:
            pl.semaphore_signal(ready.at[level], inc=1, device_id=peer, device_id_type=MESH)

    def greeted_by_all(level):
        pl.semaphore_wait(ready.at[level], len(greeted))

    def remote(src, dst, send, recv, peer):
        return pltpu.make_async_remote_copy(
            src_ref=src, dst_ref=dst, send_sem=send, recv_sem=recv, device_id=peer, device_id_type=MESH
        )

    def unit(cat, slot, piece):
        rows = [pl.ds(start, size) for start, size in PIECES[piece]]
        if cat == 0:
            return [abuf.at[slot * 2 + i, rows[i]] for i in range(2)]
        return [bbuf.at[slot, core * 2 + i, rows[i]] for i in range(2)]

    def send_unit(cat, dim, piece, slot):
        there = slot ^ (1 << dim)
        for src, dst in zip(unit(cat, slot, piece), unit(cat, there, piece)):
            remote(
                src, dst, out_sem.at[0], gather_sem.at[cat, piece, there], member(at, flips[cat], 1 << dim, core)
            ).start()

    def send_own(cat):
        for step in range(3):
            for dim in range(3):
                piece = (dim - step) % 3
                there = 1 << dim
                for half in range(2):
                    for i, (start, size) in enumerate(PIECES[piece]):
                        rows = pl.ds(start, size)
                        remote(
                            x_ref.at[half * 2 + i, rows],
                            abuf.at[there * 2 + i, rows] if cat == 0 else bbuf.at[there, half * 2 + i, rows],
                            out_sem.at[0],
                            gather_sem.at[cat, piece, there],
                            member(at, flips[cat], there, half),
                        ).start()

    own_a_half, own_b = abuf.at[pl.ds(0, 2)], bbuf.at[0]

    def landed_at(ref, sem):
        pltpu.make_async_copy(ref, ref, sem).wait()

    @pl.when(core == 0)
    def _():
        give = remote(x_ref.at[pl.ds(2, 2)], own_a_half, sib_sem.at[0], sib_sem.at[1], sibling)
        give.start()
        mine = pltpu.make_async_copy(x_ref.at[pl.ds(0, 2)], own_a_half, own_sem.at[0])
        mine.start()
        send_own(0)
        greet(0)
        mine.wait()
        give.wait_send()
        landed_at(own_b, sib_sem.at[1])

    @pl.when(core == 1)
    def _():
        give = remote(x_ref, own_b, sib_sem.at[0], sib_sem.at[1], sibling)
        give.start()
        mine = pltpu.make_async_copy(x_ref, own_b, own_sem.at[0])
        mine.start()
        send_own(1)
        greet(0)
        mine.wait()
        give.wait_send()
        landed_at(own_a_half, sib_sem.at[1])


    def arrived(cat, piece, slot):
        rows = pl.ds(0, total_rows(piece))
        landed_at(
            abuf.at[slot * 2, rows] if cat == 0 else bbuf.at[slot, core * 2, rows], gather_sem.at[cat, piece, slot]
        )
        if cat == 1:
            for here in unit(cat, slot, piece):
                remote(here, here, out_sem.at[1], relay_sem.at[slot], sibling).start()

    def iota(shape, dim):
        return lax.broadcasted_iota(jnp.int32, shape, dim)

    diagonal = iota((128, 128), 0) == iota((128, 128), 1)

    def own_norms():
        def inverse_norm(block, scale):
            halves = []
            for h in range(2):
                y = block[h * 128 : h * 128 + 128]
                total = jnp.sum(jnp.where(diagonal, dot_nt(y, y), 0.0), axis=0, keepdims=True)
                halves.append(lax.rsqrt(total * (1.0 / 256.0) + 1e-06) * scale)
            return jnp.concatenate(halves, axis=1)

        for i in range(2):
            norm_bufs[0][0, i : i + 1] = inverse_norm(abuf[i], GAIN / 16.0)
        for i in range(4):
            norm_bufs[1][0, i : i + 1] = inverse_norm(bbuf[0, i], 1.0 / 16.0)

    def share_norms():
        for cat in range(2):
            for m in range(1, 8):
                remote(
                    norm_bufs[cat].at[0], norm_bufs[cat].at[m], norm_sem.at[0, cat], norm_sem.at[1, cat],
                    member(at, flips[cat], m, core),
                ).start()

    def take_norms():
        for cat in range(2):
            landed_at(norm_bufs[cat].at[pl.ds(1, 7)], norm_sem.at[1, cat])
        flipped_norms = jnp.transpose(
            jnp.concatenate([norm_bufs[0][m] for m in range(8)] + [jnp.zeros((64, 256), f32)], axis=0)
        )
        for a in range(16):
            lane = (a // 2) * 8 + a % 2
            row_norm[a] = flipped_norms[:, lane : lane + 1]
        for b in range(32):
            col_norm[b] = jnp.broadcast_to(norm_bufs[1][b // 4, b % 4 : b % 4 + 1], (8, 256))

    def bits_of(values, shifts):
        return [(values >> k) & 1 for k in shifts]

    def flipped(bits, by):
        return sum((b + f - 2 * b * f) * (1 << k) for k, (b, f) in enumerate(zip(bits, by)))

    def make_list():
        x, y, z = at
        own_low = [p % 2 for p in at]
        own_high = [p // 2 for p in at]
        for fetch in fetches:
            fetch.wait()
        named_all = partners[...]
        limit_row = counts[...]
        counts_out[...] = limit_row
        r = iota((16, 256), 0)
        cx, cy, cz = [flipped([b], [p % 2]) + 2 * (p // 2) for b, p in zip(bits_of(r, (1, 2, 3)), at)]
        chosen = iota((16, 256), 1) == (cy * 16 + cx * 4 + cz) * 4 + 2 * core + (r & 1)
        named = dot_nt(chosen.astype(f32).astype(bf16), named_all.astype(f32).astype(bf16)).astype(jnp.int32)
        limit = jnp.sum(jnp.where(chosen, jnp.broadcast_to(limit_row, (16, 256)), 0).astype(f32), axis=1, keepdims=True)
        slot_at = iota((16, 32), 1).astype(f32)

        def coords(entry):
            owner = entry >> 2
            return (owner >> 2) & 3, owner >> 4, owner & 3

        parts = coords(named)
        active = slot_at < limit
        for p, q in zip(parts, at):
            active &= (p == q) | (p == 3 - q)
        jb = sum((p >> 1) * (1 << k) for k, p in enumerate(parts))
        pick = (named & 3) + 1
        lane = iota((16, 128), 1)
        bp = jnp.zeros((16, 128), f32)
        for k in range(8):
            best = jnp.max(jnp.where(active & (jb == k), pick, 0).astype(f32), axis=1, keepdims=True)
            bp = jnp.where(lane == k, best, bp)
        used = jnp.where(bp > 0, 1.0, 0.0).astype(bf16)
        i128, j128 = iota((128, 128), 0), iota((128, 128), 1)

        def mask(m):
            return jnp.where(m, 1.0, 0.0).astype(bf16)

        in_row = dot(used, mask(i128 < j128))
        of_row = dot(used, mask(i128 < 128))
        above = dot(mask(iota((16, 16), 1) < iota((16, 16), 0)), of_row.astype(bf16))
        pos = above + in_row
        k3 = bits_of(lane, (0, 1, 2))
        b_rel = flipped(k3, own_high) * 4 + jnp.maximum(bp.astype(jnp.int32) - 1, 0)
        index[pl.ds(0, 16), :] = jnp.where(bp > 0, jnp.minimum(pos, T - 1.0), 0.0).astype(jnp.int32)
        index[pl.ds(16, 16), :] = jnp.where(lane < 8, b_rel, 0)

        spread_out = mask(i128 == (j128 & 7))
        own_lane = (lane >> 3) == iota((16, 128), 0)

        def flat(values):
            return jnp.sum(jnp.where(own_lane, dot(values.astype(bf16), spread_out), 0.0), axis=0, keepdims=True)

        bp_row, pos_row = flat(bp), flat(pos)
        hot = mask((iota((T, 128), 0).astype(f32) == pos_row) & (bp_row > 0))
        e = iota((8, 128), 1)
        pick_row = jnp.maximum(jnp.broadcast_to(bp_row, (8, 128)).astype(jnp.int32) - 1, 0)
        b_e = flipped(bits_of(e, (0, 1, 2)), own_high) * 4 + pick_row
        values = jnp.where(iota((8, 128), 0) == 0, e >> 3, b_e).astype(f32).astype(bf16)
        index[pl.ds(32, 8), pl.ds(0, T)] = dot_nt(values, hot).astype(jnp.int32)
        fetch = pltpu.make_async_copy(index, idx, index_sem.at[0])
        fetch.start()
        e16, e32 = iota((16, 128), 1), iota((32, 128), 1)
        a_abs = flipped(bits_of(e16, (4, 5, 6)), own_low) * 2 + ((e16 >> 3) & 1)
        a_hot = mask(iota((16, 128), 0) == a_abs)
        b_abs = (e32 & 7) * 4 + jnp.broadcast_to(bp_row, (32, 128)).astype(jnp.int32) - 1
        b_hot = mask((iota((32, 128), 0) == b_abs) & (bp_row > 0))
        oa[...] = dot_nt(a_hot, hot).astype(bf16)
        oat[...] = dot_nt(hot, a_hot).astype(bf16)
        ob[...] = dot_nt(b_hot, hot).astype(bf16)
        obt[...] = dot_nt(hot, b_hot).astype(bf16)
        obd[...] = dot_nt(mask(i128 == j128), b_hot).astype(bf16)

        active = iota((32, 256), 0) < limit_row
        kind = sum((((p + 1) >> 1) & 1) * (1 << k) for k, p in enumerate(coords(named_all)))
        g, row = iota((16, 256), 0), iota((16, 256), 1)
        group = ((row >> 7) & 1) * 8 + ((row >> 5) & 1) * 4 + ((row >> 3) & 1) * 2 + ((row >> 1) & 1)
        members = mask(g == group)
        most = jnp.zeros((16, 1), f32)
        for k in range(8):
            most = jnp.maximum(
                most, jnp.sum(dot_nt(members, mask(active & (kind == k))), axis=1, keepdims=True)
            )
        most_ref[0, 0] = jnp.max(most)
        fetch.wait()

    def received(steps):
        for r in range(3):
            slot = steps(1 << r, 1 << ((r + 1) % 3), 1 << ((r + 2) % 3))
            for cat in range(2):
                arrived(cat, r, slot)
                yield cat, r, slot

    make_list()
    greeted_by_all(0)
    greet(1)
    own_norms()
    for cat, r, slot in received(lambda k0, k1, k2: k0):
        send_unit(cat, (r + 1) % 3, r, slot)
    for r in range(3):
        for cat in range(2):
            send_unit(cat, (r + 2) % 3, r, 1 << r)
    greeted_by_all(1)
    share_norms()
    for cat, r, slot in received(lambda k0, k1, k2: k1):
        send_unit(cat, (r + 2) % 3, r, slot)
    for cat, r, slot in received(lambda k0, k1, k2: k0 | k1):
        send_unit(cat, (r + 2) % 3, r, slot)
    for cat in (1, 0):
        for rest in (0, 1, 2, 3):
            for r in range(3):
                near, far = (rest & 1) << r, (rest >> 1) << ((r + 1) % 3)
                arrived(cat, r, near | far | (1 << ((r + 2) % 3)))
    take_norms()
    for slot in range(1, 8):
        landed_at(bbuf.at[slot, pl.ds(other * 2, 2)], relay_sem.at[slot])

    def build(i, c):
        for u in range(TURN):
            t = i * TURN + u
            a, b = jnp.clip(idx[32, t], 0, 15), jnp.clip(idx[33, t], 0, 31)
            scores = dot_nt(abuf[a], bbuf[b // 4, b % 4])
            tiles[t] = jnp.exp2(scores * row_norm[a] * col_norm[b][0:1] - GAIN).astype(bf16)
        return c

    lax.fori_loop(0, T // TURN, build, 0)

    row_id = iota((8, 256), 0)
    lane_id = iota((256, T), 1)

    def row_sweep():
        def body(i, c):
            beside = columns[...]
            for g in range(TURN // 8):
                base = i * TURN + g * 8
                rows = pl.ds(pl.multiple_of(base, 8), 8)
                left = spread[rows, :]
                left_bf = left.astype(bf16)
                total = jnp.zeros((8, 256), f32)
                for u in range(8):
                    tile = tiles[base + u]
                    if u % 2 == 0:
                        total = jnp.where(row_id == u, dot_nt(left_bf, tile), total)
                    else:
                        scaled = tile.astype(f32) * left[u : u + 1]
                        mass = jnp.sum(scaled[:, 0:128] + scaled[:, 128:256], axis=1, keepdims=True)
                        beside = jnp.where(lane_id == base + u, mass, beside)
                sums[rows, :] = total
            columns[...] = beside
            return c

        columns[...] = jnp.zeros((256, T), f32)
        lax.fori_loop(0, T // TURN, body, 0)
        return dot(oa[...], sums[...].astype(bf16)) + dot_nt(oa[...], columns[...].astype(bf16))

    def col_sweep():
        def body(i, c):
            for g in range(TURN // 8):
                base = i * TURN + g * 8
                rows = pl.ds(pl.multiple_of(base, 8), 8)
                left = spread[rows, :].astype(bf16)
                total = jnp.zeros((8, 256), f32)
                for u in range(8):
                    total = jnp.where(row_id == u, dot(left, tiles[base + u]), total)
                sums[rows, :] = total
            return c

        lax.fori_loop(0, T // TURN, body, 0)
        return dot(ob[...], sums[...].astype(bf16))

    def row_exchange(phase, partial):
        row_send[phase] = partial.astype(bf16)
        for m in FAR_FIRST:
            remote(
                row_send.at[phase], row_recv.at[phase, m], row_sem.at[0, phase], row_sem.at[1, phase],
                member(at, flip_a, m, core),
            ).start()

    def row_result(phase):
        landed_at(row_recv.at[phase, pl.ds(1, 7)], row_sem.at[1, phase])
        total = row_send[phase].astype(f32)
        for m in range(1, 8):
            total += row_recv[phase, m].astype(f32)
        return total

    def col_exchange(phase, partial):
        col_send[phase] = partial.astype(bf16)
        def give(far, m, to):
            remote(
                col_send.at[phase], col_recv.at[phase, far * 8 + m], col_sem.at[0, phase],
                col_sem.at[1, phase], member(at, flip_b, m, to),
            ).start()

        for m in FAR_FIRST:
            give(core, m, 0)
            give(other, m, 1)
        give(1, 0, other)
        landed_at(col_recv.at[phase, pl.ds(1, 15)], col_sem.at[1, phase])
        total = col_send[phase].astype(f32)
        for m in range(1, 16):
            total += col_recv[phase, m].astype(f32)
        return 1.0 / (1.0 + total)

    spread[...] = jnp.ones((T, 256), f32)
    for phase in range(ITERS):
        row_exchange(phase, row_sweep())
        scale_a = 1.0 / row_result(phase)
        spread[...] = dot(oat[...], scale_a.astype(bf16))
        scale_b = col_exchange(phase, col_sweep())
        spread[...] = dot(obt[...], scale_b.astype(bf16))
    x, y, z = at
    member_b = x // 2 + 2 * (y // 2) + 4 * (z // 2)
    scales[...] = scale_b
    near_rows = scales[pl.ds(pl.multiple_of((member_b // 2) * 8, 8), 8), :]
    scale_ref[...] = jnp.where(member_b % 2 == 0, near_rows[0:4], near_rows[4:8])
    dense[...] = dot(obd[...], scale_b.astype(bf16))

    def partial(slot):
        def body(i, c):
            total, mass = None, None
            a = slot * 2 + i
            rows = dense[pl.ds(pl.multiple_of(a * 8, 8), 8), :]
            for d in range(8):
                weights = tiles[jnp.clip(idx[a, d], 0, T - 1)].astype(f32) * rows[d : d + 1]
                b = jnp.clip(idx[16 + a, d], 0, 31)
                part = dot(weights.astype(bf16), bbuf[b // 4, b % 4])
                half = weights[:, 0:128] + weights[:, 128:256]
                total = part if total is None else total + part
                mass = half if mass is None else mass + half
            if slot != 7:
                numer[a] = total
            if slot:
                ship[a] = total.astype(bf16)
            column = jnp.sum(mass, axis=1, keepdims=True)
            a_at = flipped([(slot >> k) & 1 for k in range(3)], [p % 2 for p in at]) * 2 + i
            final[...] = jnp.where(iota((256, 128), 1) == a_at, column, final[...])
            return c

        lax.fori_loop(0, 2, body, 0)

    final[...] = jnp.zeros((256, 128), f32)

    def send_half(piece, slot, dim, order):
        there = slot ^ (1 << dim)
        for i, (start, size) in enumerate(PIECES[piece]):
            rows = pl.ds(start, size)
            if order:
                ship[slot * 2 + i, rows, :] = numer[slot * 2 + i, rows, :].astype(bf16)
            remote(
                ship.at[slot * 2 + i, rows],
                landed.at[order, there * 2 + i, rows],
                out_sem.at[2],
                half_sem.at[order, piece, there],
                member(at, flip_a, 1 << dim, core),
            ).start()

    def half_landed(piece, slot, order):
        landed_at(landed.at[order, slot * 2, pl.ds(0, total_rows(piece))], half_sem.at[order, piece, slot])

    def add_half(piece, slot, order):
        half_landed(piece, slot, order)
        for i, (start, size) in enumerate(PIECES[piece]):
            a, rows = slot * 2 + i, pl.ds(start, size)
            numer[a, rows, :] = numer[a, rows, :] + landed[order, a, rows, :].astype(f32)

    def map_slots(slots):
        for slot in slots:
            partial(slot)
            for r in range(3):
                if (slot >> r) & 1:
                    send_half(r, slot, r, 0)

    near_dims = [(r, 1 << ((r + 1) % 3), 1 << ((r + 2) % 3)) for r in range(3)]
    map_slots((7, 3, 5, 6))
    for r, k1, k2 in near_dims:
        add_half(r, k1 | k2, 0)
        send_half(r, k1 | k2, (r + 1) % 3, 1)
    map_slots((1, 2, 4))
    for r, k1, k2 in near_dims:
        add_half(r, k1, 0)
        send_half(r, k1, (r + 1) % 3, 1)
    map_slots((0,))
    row_exchange(ITERS, jnp.transpose(final[...])[0:16])

    landed_at(abuf.at[pl.ds(2, 14)], out_sem.at[0])
    landed_at(bbuf.at[pl.ds(1, 7), pl.ds(0, 2)], out_sem.at[0])
    landed_at(bbuf.at[pl.ds(1, 7), pl.ds(0, 2)], out_sem.at[1])
    for cat in range(2):
        landed_at(norm_bufs[cat].at[pl.ds(1, 7)], norm_sem.at[0, cat])
    for phase in range(ITERS):
        landed_at(row_recv.at[phase, pl.ds(1, 7)], row_sem.at[0, phase])
        landed_at(col_recv.at[phase, pl.ds(1, 15)], col_sem.at[0, phase])

    for r, k1, k2 in near_dims:
        add_half(r, k2, 0)
        add_half(r, k2, 1)
        send_half(r, k2, (r + 2) % 3, 2)
    for r in range(3):
        add_half(r, 0, 0)
        add_half(r, 0, 1)
    sums[pl.ds(0, 16), :] = row_result(ITERS)
    own_a = x % 2 + 2 * (y % 2) + 4 * (z % 2)
    near_rows = sums[pl.ds(pl.multiple_of((own_a // 4) * 8, 8), 8), :]
    mine = near_rows[0:2]
    for k in range(1, 4):
        mine = jnp.where(own_a % 4 == k, near_rows[2 * k : 2 * k + 2], mine)
    column = jnp.transpose(jnp.broadcast_to(1.0 / mine[:, None, :], (2, 128, 256)).reshape(256, 256))
    for r in range(3):
        half_landed(r, 0, 2)
        for i, (start, size) in enumerate(PIECES[r]):
            rows = pl.ds(start, size)
            inverse = column[start : start + size, i * 128 : i * 128 + 1]
            mapped_ref[i, rows, :] = ((numer[i, rows, :] + landed[2, i, rows, :].astype(f32)) * inverse).astype(bf16)
    landed_at(ship.at[pl.ds(2, 14)], out_sem.at[2])
    landed_at(row_recv.at[ITERS, pl.ds(1, 7)], row_sem.at[0, ITERS])


def transport(T, cid, own, partners, counts):
    vmem = pl.BlockSpec(memory_space=pltpu.VMEM)
    dma = pltpu.SemaphoreType.DMA
    return pl.pallas_call(
        functools.partial(kernel, T),
        out_shape=(
            jax.ShapeDtypeStruct((2, 256, 256), bf16),
            jax.ShapeDtypeStruct((4, 256), f32),
            jax.ShapeDtypeStruct((1, 1), f32),
            jax.ShapeDtypeStruct((1, 256), jnp.int32),
        ),
        in_specs=[pl.BlockSpec(memory_space=pltpu.HBM)] * 3,
        out_specs=(vmem, vmem, pl.BlockSpec(memory_space=pltpu.SMEM), vmem),
        scratch_shapes=[
            pltpu.VMEM((16, T), bf16),
            pltpu.VMEM((T, 16), bf16),
            pltpu.VMEM((32, T), bf16),
            pltpu.VMEM((T, 32), bf16),
            pltpu.VMEM((128, 32), bf16),
            pltpu.VMEM((32, 256), jnp.int32),
            pltpu.VMEM((1, 256), jnp.int32),
            pltpu.VMEM((40, 128), jnp.int32),
            pltpu.SMEM((40, 128), jnp.int32),
            pltpu.VMEM((256, 128), f32),
            pltpu.VMEM((8, 8, 256), f32),
            pltpu.VMEM((8, 8, 256), f32),
            dma((2, 2)),
            pltpu.VMEM((16, 256, 256), bf16),
            pltpu.VMEM((8, 4, 256, 256), bf16),
            pltpu.VMEM((T, 256, 256), bf16),
            pltpu.VMEM((16, 256, 1), f32),
            pltpu.VMEM((32, 8, 256), f32),
            pltpu.VMEM((T, 256), f32),
            pltpu.VMEM((256, T), f32),
            pltpu.VMEM((T, 256), f32),
            pltpu.VMEM((128, 256), f32),
            pltpu.VMEM((4, 16, 256), bf16),
            pltpu.VMEM((3, 32, 256), bf16),
            pltpu.VMEM((4, 8, 16, 256), bf16),
            pltpu.VMEM((3, 16, 32, 256), bf16),
            pltpu.VMEM((32, 256), f32),
            pltpu.VMEM((16, 256, 256), f32),
            pltpu.VMEM((16, 256, 256), bf16),
            pltpu.VMEM((3, 16, 256, 256), bf16),
            dma((3,)),
            dma((2,)),
            dma((2, 3, 8)),
            dma((8,)),
            dma((3,)),
            dma((2, 4)),
            dma((2, 3)),
            dma((3, 3, 8)),
            dma((1,)),
            pltpu.SemaphoreType.REGULAR((2,)),
        ],
        compiler_params=pltpu.CompilerParams(
            collective_id=cid, has_side_effects=True, vmem_limit_bytes=60 << 20
        ),
        name=f"transport_{T}",
    )(own, partners, counts)


def shards(embeds, partners, counts):
    args = embeds.reshape(4, 256, 256), partners.T, counts.reshape(1, 256)
    mapped, scale, most, limits = transport(64, 0, *args)
    mapped, scale = lax.cond(
        most.reshape(()) <= 64.0,
        lambda mapped, scale, *args: (mapped, scale),
        lambda mapped, scale, *args: transport(128, 1, *args)[:2],
        mapped,
        scale,
        *args[:2],
        limits,
    )
    return mapped.reshape(1, 1, 2, 256, 256), scale


def solution(mesh):
    in_specs = (P("side", ("grp", "dev"), None, None), P(), P())
    out_specs = (P(("grp", "dev"), "side", None, None, None), P(("grp", "dev"), None))
    return jax.shard_map(shards, mesh=mesh, in_specs=in_specs, out_specs=out_specs, check_vma=False)
```
